32 devices in a mesh: group: 2 (over x), row: 8 (over z, y), col: 2 (over core).
Axes of the slice: x: 2, y: 2, z: 4, core: 2. Of those that a mesh axis runs over, the one named last changes fastest.
Arguments:
- alignment: bfloat16 [128, 256, 256], P(('group', 'row'), 'col'), parts along dimension 0, may hold values from -6 to 6
- ln_gain: float32 [256], replicated, may hold values from 0.5 to 1.5
- ln_bias: float32 [256], replicated, may hold values from -3 to 3
- w_left: bfloat16 [256, 32], replicated, may hold values from -0.375 to 0.375
- b_left: float32 [32], replicated, may hold values from -3 to 3
- w_right: bfloat16 [256, 32], replicated, may hold values from -0.375 to 0.375
- b_right: float32 [32], replicated, may hold values from -3 to 3
- w_out: bfloat16 [1024, 128], replicated, may hold values from -1.5 to 1.5
- b_out: float32 [128], replicated, may hold values from -3 to 3
Outputs:
- pair_update: bfloat16 [512, 256, 128], P(('group', 'row'), 'col'), parts along dimension 0
The draws below stay inside these ranges and needn't reach their ends.
There are 2 independent parts, one for each index of `group`. The reference program is written for one: setup_inputs(seed, part) draws one part's arguments, and reference() takes and returns one part's arrays. A program takes and returns all parts, laid end to end along the dimension named above; an argument that names none is the same for every part. Nothing has to cross between parts.
All inputs are finite; a program needn't handle non-finite values.
Results may differ from the reference program's by a relative error of at most 0.0053.
Values may be sent and summed in bfloat16 or wider, within the bound.
No kernel may reach another device: no remote copies, remote signals or barrier semaphores. Data moves between devices by JAX's collectives and lax.ppermute only.
A program may use at most 128 MiB of HBM per device.

```python
import jax
import jax.numpy as jnp
from jax import lax

C_M = 256
C = 32
Z = 128
S = 64
ROWS_DEV = 32
RES = 256
N_ROW = 8


def block_levels(key, dims, cuts, low, top_value):
    loudness = 1.0
    for dim, blocks in cuts:
        draws = jax.random.uniform(jax.random.fold_in(jax.random.fold_in(key, 6), dim), (blocks,), jnp.float32, low / len(cuts), top_value / len(cuts))
        loudness = loudness * jnp.repeat(jnp.exp(draws), dims[dim] // blocks).reshape((-1,) + (1,) * (len(dims) - 1 - dim))
    return loudness


def normal_values(key, extent, deviation, bound, pieces=(), held_as=jnp.bfloat16):
    array = jax.random.normal(key, extent, jnp.float32) * deviation
    if len(pieces) > 0:
        array = block_levels(key, extent, pieces, -0.22, 0.18) * array
    return jnp.clip(array, min=-bound, max=bound).astype(held_as)


def setup_inputs(seed: int = 0, part: int = 0) -> dict:
    key_list = jax.random.split(jax.random.key(seed), 10)
    part_splits = jax.random.split(jax.random.fold_in(key_list[9], part), 10)
    alignment = normal_values(part_splits[0], (S, RES, C_M), 1.0, 6.0, ((0, 8), (1, 2)))
    ln_gain = jnp.clip(jax.random.uniform(key_list[1], (C_M,), jnp.float32, 0.5, 1.5), 0.5, 1.5)
    ln_bias = normal_values(key_list[2], (C_M,), 0.5, 3.0, (), jnp.float32)
    w_left = normal_values(key_list[3], (C_M, C), C_M ** -0.5, 0.375)
    b_left = normal_values(key_list[4], (C,), 0.5, 3.0, (), jnp.float32)
    w_right = normal_values(key_list[5], (C_M, C), C_M ** -0.5, 0.375)
    b_right = normal_values(key_list[6], (C,), 0.5, 3.0, (), jnp.float32)
    w_out = normal_values(key_list[7], (C * C, Z), 0.25, 1.5)
    b_out = normal_values(key_list[8], (Z,), 0.5, 3.0, (), jnp.float32)
    return dict(alignment=alignment, ln_gain=ln_gain, ln_bias=ln_bias, w_left=w_left, b_left=b_left, w_right=w_right, b_right=b_right, w_out=w_out, b_out=b_out)


def projected_sides(alignment, ln_gain, ln_bias, w_left, b_left, w_right, b_right):
    values = alignment.astype(jnp.float32)
    average = lax.optimization_barrier(jnp.mean(values, axis=-1, keepdims=True))
    centred = values - average
    variance = lax.optimization_barrier(jnp.mean(centred * centred, axis=-1, keepdims=True))
    normed = (centred * lax.rsqrt(variance + 1e-05) * ln_gain + ln_bias).astype(jnp.bfloat16)
    normed_wide = normed.astype(jnp.float32)
    left = (jnp.einsum('slm,mc->slc', normed_wide, w_left.astype(jnp.float32)) + b_left).astype(jnp.bfloat16)
    right = (jnp.einsum('slm,mc->slc', normed_wide, w_right.astype(jnp.float32)) + b_right).astype(jnp.bfloat16)
    return (left, right)

def reference(alignment, ln_gain, ln_bias, w_left, b_left, w_right, b_right, w_out, b_out):
    left, right = projected_sides(alignment, ln_gain, ln_bias, w_left, b_left, w_right, b_right)
    right_wide = right.astype(jnp.float32)

    def row_block(index):
        rows_left = lax.dynamic_slice_in_dim(left, (index * ROWS_DEV).astype(jnp.int32), ROWS_DEV, 1)
        outer = jnp.einsum('sic,sje->ijce', rows_left.astype(jnp.float32), right_wide) / S
        flat = outer.astype(jnp.bfloat16).reshape(ROWS_DEV * RES, C * C)
        update = jnp.dot(flat, w_out, preferred_element_type=jnp.float32) + b_out
        return update.astype(jnp.bfloat16).reshape(ROWS_DEV, RES, Z)
    blocks = lax.map(row_block, jnp.arange(N_ROW, dtype=jnp.int32))
    return blocks.reshape(RES, RES, Z)
```

```python
import functools

import jax
import jax.numpy as jnp
from jax import lax
from jax.experimental import pallas as pl
from jax.experimental.pallas import tpu as pltpu
from jax.sharding import PartitionSpec as P

LANES = 128


def features_kernel(scale, x_ref, gain_ref, bias_ref, wl_ref, bl_ref, wr_ref, br_ref,
                    left_ref, right_ref, normed_ref, left_f32, right_f32):
    seqs, width, channels = x_ref.shape
    c = wl_ref.shape[0]
    fold = LANES // c
    quarter = width // fold
    for s in range(seqs):
        values = x_ref[s].astype(jnp.float32)
        average = jnp.mean(values, axis=-1, keepdims=True)
        centred = values - average
        variance = jnp.mean(centred * centred, axis=-1, keepdims=True)
        normed = centred * lax.rsqrt(variance + 1e-05) * gain_ref[...] + bias_ref[...]
        for h in range(channels // LANES):
            normed_ref[h, s * width:(s + 1) * width] = normed[:, h * LANES:(h + 1) * LANES]
        right = lax.dot_general(wr_ref[...], normed.astype(jnp.bfloat16), (((1,), (1,)), ((), ())),
                                preferred_element_type=jnp.float32) + br_ref[...]
        for b in range(width // LANES):
            right_f32[pl.ds(b * c * seqs + s, c, stride=seqs), :] = right[:, b * LANES:(b + 1) * LANES]
    total = None
    for q in range(fold):
        part = jnp.concatenate(
            [normed_ref[h, pl.ds(q, seqs * quarter, stride=fold), :] for h in range(channels // LANES)], axis=1
        ).astype(jnp.bfloat16)
        zeros = [jnp.zeros((c, channels), jnp.bfloat16)]
        w = jnp.concatenate(zeros * q + [wl_ref[...]] + zeros * (fold - 1 - q), axis=0)
        term = lax.dot_general(part, w, (((1,), (1,)), ((), ())), preferred_element_type=jnp.float32)
        total = term if total is None else total + term
    total = (total + jnp.concatenate([bl_ref[...]] * fold, axis=1)) * scale
    for s in range(seqs):
        left_f32[pl.ds(s, quarter, stride=seqs), :] = total[s * quarter:(s + 1) * quarter]
    left_ref[...] = left_f32[...].astype(jnp.bfloat16)
    right_ref[...] = right_f32[...].astype(jnp.bfloat16)


def features(alignment, ln_gain, ln_bias, w_left, b_left, w_right, b_right, scale):
    seqs, width, channels = alignment.shape
    c = w_left.shape[1]
    left_rows = seqs * width * c // LANES
    right_rows = left_rows
    vmem = pl.BlockSpec(memory_space=pltpu.VMEM)
    return pl.pallas_call(
        functools.partial(features_kernel, scale),
        out_shape=(jax.ShapeDtypeStruct((left_rows, LANES), jnp.bfloat16),
                   jax.ShapeDtypeStruct((right_rows, LANES), jnp.bfloat16)),
        in_specs=[vmem] * 7,
        out_specs=(vmem, vmem),
        scratch_shapes=[pltpu.VMEM((channels // LANES, seqs * width, LANES), jnp.float32),
                        pltpu.VMEM((left_rows, LANES), jnp.float32),
                        pltpu.VMEM((right_rows, LANES), jnp.float32)],
        compiler_params=pltpu.CompilerParams(vmem_limit_bytes=32 * 1024 * 1024),
        name="features",
    )(alignment, ln_gain.reshape(1, -1), ln_bias.reshape(1, -1), w_left.T, b_left.reshape(1, -1),
      w_right.T, b_right.reshape(-1, 1))


def by_sequence(block, f32_ref, inner, seqs):
    sources = f32_ref.shape[0]
    for src in range(sources):
        f32_ref[src] = block(src)
    if seqs % 8 == 0:
        return lambda n: jnp.concatenate(
            [f32_ref[src, n * seqs:(n + 1) * seqs] for src in range(sources)], axis=0)
    flat = f32_ref.reshape(sources * inner * seqs, LANES)
    return lambda n: jnp.concatenate(
        [flat[pl.ds(n * seqs + s, sources, stride=inner * seqs), :] for s in range(seqs)], axis=0)


def pair_kernel(seqs, c, rows_step, recv_ref, w_ref, bias_ref, out_ref,
                left_f32, right_f32, left_t, right_b, w_f32, w_t, outer_ref):
    sources = recv_ref.shape[0]
    rows, width, z = out_ref.shape[0], out_ref.shape[1], out_ref.shape[2]
    left_rows = left_f32.shape[1]
    fold = LANES // c
    blocks = width // LANES
    step = pl.program_id(0)

    @pl.when(step == 0)
    def _():
        left_of = by_sequence(lambda src: recv_ref[src, :left_rows].astype(jnp.float32),
                              left_f32, left_rows // seqs, seqs)
        for k in range(left_rows // seqs):
            left_t[k * LANES:(k + 1) * LANES] = left_of(k).T.astype(jnp.bfloat16)
        for b in range(blocks):
            first = left_rows + b * c * seqs
            right_of = by_sequence(lambda src: recv_ref[src, first:first + c * seqs].astype(jnp.float32),
                                   right_f32, c, seqs)
            for e in range(c):
                at = (b * c + e) * LANES
                right_b[:, at:at + LANES] = right_of(e).astype(jnp.bfloat16)
        w_f32[...] = w_ref[...].astype(jnp.float32)
        for e in range(c):
            w_t[:, e * c:(e + 1) * c] = w_f32[pl.ds(e, c, stride=c), :].T.astype(jnp.bfloat16)

    here = left_t[pl.ds(pl.multiple_of(step * rows_step * c, rows_step * c), rows_step * c), :]
    for b in range(blocks):
        for e in range(0, c, 2):
            at = (b * c + e) * LANES
            outer = jnp.dot(here, right_b[:, at:at + 2 * LANES], preferred_element_type=jnp.float32)
            outer = outer.astype(jnp.bfloat16)
            for half in range(2):
                for i in range(rows_step):
                    outer_ref[i // 2, (e + half) * c:(e + half + 1) * c,
                              (i % 2) * LANES:(i % 2 + 1) * LANES] = (
                        outer[i * c:(i + 1) * c, half * LANES:(half + 1) * LANES])
        for p in range(rows_step // 2):
            update = jnp.dot(w_t[...], outer_ref[p], preferred_element_type=jnp.float32)
            for half in range(2):
                mine = update[:, half * LANES:(half + 1) * LANES].T + bias_ref[...]
                out_ref[2 * p + half, b * LANES:(b + 1) * LANES, :] = mine.astype(out_ref.dtype)


def pairs(received, w_out, b_out, seqs, c, rows, width):
    sources, all_rows, _ = received.shape
    z = w_out.shape[1]
    left_rows = rows * c * seqs // LANES
    rows_step = 8
    vmem = pl.BlockSpec(memory_space=pltpu.VMEM)
    total = sources * seqs
    return pl.pallas_call(
        functools.partial(pair_kernel, seqs, c, rows_step),
        grid=(rows // rows_step,),
        out_shape=jax.ShapeDtypeStruct((rows, width, z), jnp.bfloat16),
        in_specs=[vmem] * 3,
        out_specs=pl.BlockSpec((rows_step, width, z), lambda i: (i, 0, 0)),
        scratch_shapes=[pltpu.VMEM((sources, left_rows, LANES), jnp.float32),
                        pltpu.VMEM((sources, c * seqs, LANES), jnp.float32),
                        pltpu.VMEM((rows * c, total), jnp.bfloat16),
                        pltpu.VMEM((total, width * c), jnp.bfloat16),
                        pltpu.VMEM(w_out.shape, jnp.float32),
                        pltpu.VMEM((z, c * c), jnp.bfloat16),
                        pltpu.VMEM((rows_step // 2, c * c, 2 * LANES), jnp.bfloat16)],
        compiler_params=pltpu.CompilerParams(vmem_limit_bytes=48 * 1024 * 1024),
        name="pairs",
    )(received, w_out, b_out.reshape(1, -1))


def on_device(alignment, ln_gain, ln_bias, w_left, b_left, w_right, b_right, w_out, b_out):
    seqs, width, _ = alignment.shape
    c = w_left.shape[1]
    row_count = lax.axis_size("row")
    col_count = lax.axis_size("col")
    rows = width * col_count // row_count
    left, right = features(alignment, ln_gain, ln_bias, w_left, b_left, w_right, b_right,
                           1.0 / (seqs * row_count))
    left = left.reshape(width // rows, rows * c * seqs // LANES, LANES)
    left = lax.all_gather(left, "col", axis=0, tiled=True)
    send = jnp.concatenate(
        [left, jnp.broadcast_to(right[None], (row_count,) + right.shape)], axis=1)
    received = lax.all_to_all(send, "row", split_axis=0, concat_axis=0, tiled=True)
    return pairs(received, w_out, b_out, seqs, c, rows, width)


def solution(mesh):
    in_specs = (P(("group", "row"), "col", None), P(), P(), P(), P(), P(), P(), P(), P())
    out_specs = P(("group", "row"), "col", None)
    return jax.shard_map(
        on_device, mesh=mesh, in_specs=in_specs, out_specs=out_specs, check_vma=False
    )
```

```python
import functools

import jax
import jax.numpy as jnp
from jax import lax
from jax.experimental import pallas as pl
from jax.experimental.pallas import tpu as pltpu
from jax.sharding import PartitionSpec as P

LANES = 128


def features_kernel(scale, x_ref, gain_ref, bias_ref, wl_ref, bl_ref, wr_ref, br_ref,
                    left_ref, right_ref, normed_ref, left_f32, right_f32):
    seqs, width, channels = x_ref.shape
    c = wl_ref.shape[0]
    fold = LANES // c
    quarter = width // fold
    right_bias = jnp.broadcast_to(br_ref[...], (LANES, c)).T[:, :1]
    for s in range(seqs):
        values = x_ref[s].astype(jnp.float32)
        average = jnp.mean(values, axis=-1, keepdims=True)
        centred = values - average
        variance = jnp.mean(centred * centred, axis=-1, keepdims=True)
        normed = centred * lax.rsqrt(variance + 1e-05) * gain_ref[...] + bias_ref[...]
        for h in range(channels // LANES):
            normed_ref[h, s * width:(s + 1) * width] = normed[:, h * LANES:(h + 1) * LANES]
        right = lax.dot_general(wr_ref[...], normed.astype(jnp.bfloat16), (((1,), (1,)), ((), ())),
                                preferred_element_type=jnp.float32) + right_bias
        for b in range(width // LANES):
            right_f32[pl.ds(b * c * seqs + s, c, stride=seqs), :] = right[:, b * LANES:(b + 1) * LANES]
    total = None
    for q in range(fold):
        part = jnp.concatenate(
            [normed_ref[h, pl.ds(q, seqs * quarter, stride=fold), :] for h in range(channels // LANES)], axis=1
        ).astype(jnp.bfloat16)
        zeros = [jnp.zeros((c, channels), jnp.bfloat16)]
        w = jnp.concatenate(zeros * q + [wl_ref[...]] + zeros * (fold - 1 - q), axis=0)
        term = lax.dot_general(part, w, (((1,), (1,)), ((), ())), preferred_element_type=jnp.float32)
        total = term if total is None else total + term
    total = (total + jnp.concatenate([bl_ref[...]] * fold, axis=1)) * scale
    for s in range(seqs):
        left_f32[pl.ds(s, quarter, stride=seqs), :] = total[s * quarter:(s + 1) * quarter]
    left_ref[...] = left_f32[...].astype(jnp.bfloat16)
    right_ref[...] = right_f32[...].astype(jnp.bfloat16)


def features(alignment, ln_gain, ln_bias, w_left, b_left, w_right, b_right, scale):
    seqs, width, channels = alignment.shape
    c = w_left.shape[1]
    rows = seqs * width * c // LANES
    whole = [pl.BlockSpec(shape, lambda i, n=len(shape): (0,) * n)
             for shape in (alignment.shape, (1, channels), (1, channels), (c, channels), (1, c),
                           (c, channels), (1, c))]
    side = pl.BlockSpec((rows, LANES), lambda i: (0, 0))
    return pl.pallas_call(
        functools.partial(features_kernel, scale),
        grid=(1,),
        out_shape=(jax.ShapeDtypeStruct((rows, LANES), jnp.bfloat16),) * 2,
        in_specs=whole,
        out_specs=(side, side),
        scratch_shapes=[pltpu.VMEM((channels // LANES, seqs * width, LANES), jnp.float32),
                        pltpu.VMEM((rows, LANES), jnp.float32),
                        pltpu.VMEM((rows, LANES), jnp.float32)],
        compiler_params=pltpu.CompilerParams(vmem_limit_bytes=60 * 1024 * 1024),
        name="features",
    )(alignment, ln_gain.reshape(1, -1), ln_bias.reshape(1, -1), w_left.T, b_left.reshape(1, -1),
      w_right.T, b_right.reshape(1, -1))


def by_sequence(block, f32_ref, inner, seqs):
    sources = f32_ref.shape[0]
    for src in range(sources):
        f32_ref[src] = block(src)
    if seqs % 8 == 0:
        return lambda n: jnp.concatenate(
            [f32_ref[src, n * seqs:(n + 1) * seqs] for src in range(sources)], axis=0)
    flat = f32_ref.reshape(sources * inner * seqs, LANES)
    return lambda n: jnp.concatenate(
        [flat[pl.ds(n * seqs + s, sources, stride=inner * seqs), :] for s in range(seqs)], axis=0)


def pair_kernel(seqs, c, rows_step, order_ref, left_ref, w_ref, bias_ref, *refs):
    sources = left_ref.shape[0]
    right_refs = refs[:sources]
    out_ref, left_f32, right_f32, left_t, right_b, w_f32, w_t, outer_ref = refs[sources:]
    rows, width, z = out_ref.shape[0], out_ref.shape[1], out_ref.shape[2]
    left_rows = left_f32.shape[1]
    blocks = width // LANES
    step = pl.program_id(0)

    @pl.when(step == 0)
    def _():
        left_of = by_sequence(lambda src: left_ref[order_ref[src]].astype(jnp.float32),
                              left_f32, left_rows // seqs, seqs)
        for k in range(left_rows // seqs):
            left_t[k * LANES:(k + 1) * LANES] = left_of(k).T.astype(jnp.bfloat16)
        for b in range(blocks):
            right_of = by_sequence(
                lambda src: right_refs[src][b * c * seqs:(b + 1) * c * seqs].astype(jnp.float32),
                right_f32, c, seqs)
            for e in range(c):
                at = (b * c + e) * LANES
                right_b[:, at:at + LANES] = right_of(e).astype(jnp.bfloat16)
        w_f32[...] = w_ref[...].astype(jnp.float32)
        for e in range(c):
            w_t[:, e * c:(e + 1) * c] = w_f32[pl.ds(e, c, stride=c), :].T.astype(jnp.bfloat16)

    here = left_t[pl.ds(pl.multiple_of(step * rows_step * c, rows_step * c), rows_step * c), :]
    for b in range(blocks):
        for e in range(0, c, 2):
            at = (b * c + e) * LANES
            outer = jnp.dot(here, right_b[:, at:at + 2 * LANES], preferred_element_type=jnp.float32)
            outer = outer.astype(jnp.bfloat16)
            for half in range(2):
                for i in range(rows_step):
                    outer_ref[i // 2, (e + half) * c:(e + half + 1) * c,
                              (i % 2) * LANES:(i % 2 + 1) * LANES] = (
                        outer[i * c:(i + 1) * c, half * LANES:(half + 1) * LANES])
        for p in range(rows_step // 2):
            update = jnp.dot(w_t[...], outer_ref[p], preferred_element_type=jnp.float32)
            for half in range(2):
                mine = update[:, half * LANES:(half + 1) * LANES].T + bias_ref[...]
                out_ref[2 * p + half, b * LANES:(b + 1) * LANES, :] = mine.astype(out_ref.dtype)


def pairs(order, left, rights, w_out, b_out, seqs, c, width):
    sources, left_rows, _ = left.shape
    z = w_out.shape[1]
    rows = left_rows * LANES // (c * seqs)
    rows_step = 8
    total = sources * seqs
    operands = (left, w_out, b_out.reshape(1, -1), *rights)
    return pl.pallas_call(
        functools.partial(pair_kernel, seqs, c, rows_step),
        grid=(rows // rows_step,),
        out_shape=jax.ShapeDtypeStruct((rows, width, z), jnp.bfloat16),
        in_specs=[pl.BlockSpec(memory_space=pltpu.SMEM)]
        + [pl.BlockSpec(a.shape, lambda i, n=a.ndim: (0,) * n) for a in operands],
        out_specs=pl.BlockSpec((rows_step, width, z), lambda i: (i, 0, 0)),
        scratch_shapes=[pltpu.VMEM((sources, left_rows, LANES), jnp.float32),
                        pltpu.VMEM((sources, c * seqs, LANES), jnp.float32),
                        pltpu.VMEM((rows * c, total), jnp.bfloat16),
                        pltpu.VMEM((total, width * c), jnp.bfloat16),
                        pltpu.VMEM(w_out.shape, jnp.float32),
                        pltpu.VMEM((z, c * c), jnp.bfloat16),
                        pltpu.VMEM((rows_step // 2, c * c, 2 * LANES), jnp.bfloat16)],
        compiler_params=pltpu.CompilerParams(vmem_limit_bytes=48 * 1024 * 1024),
        name="pairs",
    )(order, *operands)


def ring_of(count):
    if count % 2 == 0 and count <= 8:
        return list(range(0, count, 2)) + list(range(count - 1, 0, -2))
    return list(range(count))


def on_device(alignment, ln_gain, ln_bias, w_left, b_left, w_right, b_right, w_out, b_out):
    seqs, width, _ = alignment.shape
    c = w_left.shape[1]
    row_count = lax.axis_size("row")
    col_count = lax.axis_size("col")
    rows = width * col_count // row_count
    ring = ring_of(row_count)
    left, right = features(alignment, ln_gain, ln_bias, w_left, b_left, w_right, b_right,
                           1.0 / (seqs * row_count))

    forth = [(ring[i], ring[(i + 1) % row_count]) for i in range(row_count)]
    back = [(b, a) for a, b in forth]
    rights = {0: right}
    for step in range(1, row_count // 2 + 1):
        rights[-step % row_count] = lax.ppermute(rights[(1 - step) % row_count], "row", forth)
        if 2 * step < row_count:
            rights[step] = lax.ppermute(rights[step - 1], "row", back)
    place = [0] * row_count
    for i, r in enumerate(ring):
        place[r] = i
    around = [[ring[(place[r] + t) % row_count] for t in range(row_count)] for r in range(row_count)]
    order = jnp.array(around, jnp.int32)[lax.axis_index("row")]

    left = left.reshape(width // rows, rows * c * seqs // LANES, LANES)
    left = lax.all_gather(left, "col", axis=0, tiled=True)
    left = lax.all_to_all(left, "row", split_axis=0, concat_axis=0, tiled=True)
    return pairs(order, left, [rights[t] for t in range(row_count)], w_out, b_out, seqs, c, width)


def solution(mesh):
    in_specs = (P(("group", "row"), "col", None), P(), P(), P(), P(), P(), P(), P(), P())
    out_specs = P(("group", "row"), "col", None)
    return jax.shard_map(
        on_device, mesh=mesh, in_specs=in_specs, out_specs=out_specs, check_vma=False
    )
```

```python
import functools

import jax
import jax.numpy as jnp
from jax import lax
from jax.experimental import pallas as pl
from jax.experimental.pallas import tpu as pltpu
from jax.sharding import PartitionSpec as P

LANES = 128


def features_kernel(scale, col_count, x_ref, gain_ref, bias_ref, wl_ref, bl_ref, wr_ref, br_ref,
                    right_ref, *refs):
    left_refs, (normed_ref, left_f32, right_f32) = refs[:-3], refs[-3:]
    seqs, width, channels = x_ref.shape
    c = wl_ref.shape[0]
    fold = LANES // c
    quarter = width // fold
    right_bias = jnp.broadcast_to(br_ref[...], (LANES, c)).T[:, :1]
    for s in range(seqs):
        values = x_ref[s].astype(jnp.float32)
        average = jnp.mean(values, axis=-1, keepdims=True)
        centred = values - average
        variance = jnp.mean(centred * centred, axis=-1, keepdims=True)
        normed = centred * lax.rsqrt(variance + 1e-05) * gain_ref[...] + bias_ref[...]
        for h in range(channels // LANES):
            normed_ref[h, s * width:(s + 1) * width] = normed[:, h * LANES:(h + 1) * LANES]
        right = lax.dot_general(wr_ref[...], normed.astype(jnp.bfloat16), (((1,), (1,)), ((), ())),
                                preferred_element_type=jnp.float32) + right_bias
        for b in range(width // LANES):
            right_f32[pl.ds(b * c * seqs + s, c, stride=seqs), :] = right[:, b * LANES:(b + 1) * LANES]
    total = None
    for q in range(fold):
        part = jnp.concatenate(
            [normed_ref[h, pl.ds(q, seqs * quarter, stride=fold), :] for h in range(channels // LANES)], axis=1
        ).astype(jnp.bfloat16)
        zeros = [jnp.zeros((c, channels), jnp.bfloat16)]
        w = jnp.concatenate(zeros * q + [wl_ref[...]] + zeros * (fold - 1 - q), axis=0)
        term = lax.dot_general(part, w, (((1,), (1,)), ((), ())), preferred_element_type=jnp.float32)
        total = term if total is None else total + term
    total = (total + jnp.concatenate([bl_ref[...]] * fold, axis=1)) * scale
    for s in range(seqs):
        left_f32[pl.ds(s, quarter, stride=seqs), :] = total[s * quarter:(s + 1) * quarter]
    here = lax.axis_index("row")
    for k, left_ref in enumerate(left_refs):
        rows = left_ref.shape[0]
        chip = lax.rem(here + k, len(left_refs)) // col_count
        left_ref[...] = left_f32[pl.ds(pl.multiple_of(chip * rows, rows), rows), :].astype(jnp.bfloat16)
    right_ref[...] = right_f32[...].astype(jnp.bfloat16)


def features(alignment, ln_gain, ln_bias, w_left, b_left, w_right, b_right, row_count, col_count):
    seqs, width, channels = alignment.shape
    c = w_left.shape[1]
    rows = seqs * width * c // LANES
    whole = [pl.BlockSpec(shape, lambda i, n=len(shape): (0,) * n)
             for shape in (alignment.shape, (1, channels), (1, channels), (c, channels), (1, c),
                           (c, channels), (1, c))]
    part = rows * col_count // row_count

    def side(n):
        return pl.BlockSpec((n, LANES), lambda i: (0, 0))

    return pl.pallas_call(
        functools.partial(features_kernel, 1.0 / (seqs * row_count), col_count),
        grid=(1,),
        out_shape=[jax.ShapeDtypeStruct((rows, LANES), jnp.bfloat16)]
        + [jax.ShapeDtypeStruct((part, LANES), jnp.bfloat16)] * row_count,
        in_specs=whole,
        out_specs=[side(rows)] + [side(part)] * row_count,
        scratch_shapes=[pltpu.VMEM((channels // LANES, seqs * width, LANES), jnp.float32),
                        pltpu.VMEM((rows, LANES), jnp.float32),
                        pltpu.VMEM((rows, LANES), jnp.float32)],
        compiler_params=pltpu.CompilerParams(vmem_limit_bytes=60 * 1024 * 1024),
        name="features",
    )(alignment, ln_gain.reshape(1, -1), ln_bias.reshape(1, -1), w_left.T, b_left.reshape(1, -1),
      w_right.T, b_right.reshape(1, -1))


def by_sequence(block, source_of, f32_ref, inner, seqs):
    sources = f32_ref.shape[0]
    for src in range(sources):
        f32_ref[source_of(src)] = block(src)
    if seqs % 8 == 0:
        return lambda n: jnp.concatenate(
            [f32_ref[src, n * seqs:(n + 1) * seqs] for src in range(sources)], axis=0)
    flat = f32_ref.reshape(sources * inner * seqs, LANES)
    return lambda n: jnp.concatenate(
        [flat[pl.ds(n * seqs + s, sources, stride=inner * seqs), :] for s in range(seqs)], axis=0)


def pair_kernel(seqs, c, rows_step, col_count, steps, w_ref, bias_ref, *refs):
    sources = len(steps)
    left_refs, right_refs, refs = refs[:sources], refs[sources:2 * sources], refs[2 * sources:]
    out_ref, left_f32, right_f32, left_t, right_b, w_f32, w_t, outer_ref = refs
    rows, width, z = out_ref.shape[0], out_ref.shape[1], out_ref.shape[2]
    left_rows = left_f32.shape[1]
    blocks = width // LANES
    step = pl.program_id(0)

    @pl.when(step == 0)
    def _():
        here, core = lax.axis_index("row"), lax.axis_index("col")
        place = lax.rem(here, sources // col_count) * col_count + core
        left_of = by_sequence(lambda k: left_refs[k][...].astype(jnp.float32),
                              lambda k: lax.rem(place - k + sources, sources),
                              left_f32, left_rows // seqs, seqs)
        for k in range(left_rows // seqs):
            left_t[k * LANES:(k + 1) * LANES] = left_of(k).T.astype(jnp.bfloat16)
        for b in range(blocks):
            right_of = by_sequence(
                lambda n: right_refs[n][b * c * seqs:(b + 1) * c * seqs].astype(jnp.float32),
                lambda n: source_at(here, steps[n], sources), right_f32, c, seqs)
            for e in range(c):
                at = (b * c + e) * LANES
                right_b[:, at:at + LANES] = right_of(e).astype(jnp.bfloat16)
        w_f32[...] = w_ref[...].astype(jnp.float32)
        for e in range(c):
            w_t[:, e * c:(e + 1) * c] = w_f32[pl.ds(e, c, stride=c), :].T.astype(jnp.bfloat16)

    here = left_t[pl.ds(pl.multiple_of(step * rows_step * c, rows_step * c), rows_step * c), :]
    for b in range(blocks):
        for e in range(0, c, 2):
            at = (b * c + e) * LANES
            outer = jnp.dot(here, right_b[:, at:at + 2 * LANES], preferred_element_type=jnp.float32)
            outer = outer.astype(jnp.bfloat16)
            for half in range(2):
                for i in range(rows_step):
                    outer_ref[i // 2, (e + half) * c:(e + half + 1) * c,
                              (i % 2) * LANES:(i % 2 + 1) * LANES] = (
                        outer[i * c:(i + 1) * c, half * LANES:(half + 1) * LANES])
        for p in range(rows_step // 2):
            update = jnp.dot(w_t[...], outer_ref[p], preferred_element_type=jnp.float32)
            for half in range(2):
                mine = update[:, half * LANES:(half + 1) * LANES].T + bias_ref[...]
                out_ref[2 * p + half, b * LANES:(b + 1) * LANES, :] = mine.astype(out_ref.dtype)


def pairs(lefts, rights, w_out, b_out, seqs, c, width, col_count):
    sources, left_rows = len(lefts), lefts[0].shape[0]
    z = w_out.shape[1]
    rows = left_rows * LANES // (c * seqs)
    rows_step = 8
    total = sources * seqs
    steps = list(rights)
    operands = (w_out, b_out.reshape(1, -1), *lefts, *rights.values())
    return pl.pallas_call(
        functools.partial(pair_kernel, seqs, c, rows_step, col_count, steps),
        grid=(rows // rows_step,),
        out_shape=jax.ShapeDtypeStruct((rows, width, z), jnp.bfloat16),
        in_specs=[pl.BlockSpec(a.shape, lambda i, n=a.ndim: (0,) * n) for a in operands],
        out_specs=pl.BlockSpec((rows_step, width, z), lambda i: (i, 0, 0)),
        scratch_shapes=[pltpu.VMEM((sources, left_rows, LANES), jnp.float32),
                        pltpu.VMEM((sources, c * seqs, LANES), jnp.float32),
                        pltpu.VMEM((rows * c, total), jnp.bfloat16),
                        pltpu.VMEM((total, width * c), jnp.bfloat16),
                        pltpu.VMEM(w_out.shape, jnp.float32),
                        pltpu.VMEM((z, c * c), jnp.bfloat16),
                        pltpu.VMEM((rows_step // 2, c * c, 2 * LANES), jnp.bfloat16)],
        compiler_params=pltpu.CompilerParams(vmem_limit_bytes=48 * 1024 * 1024),
        name="pairs",
    )(*operands)


def pair_width(count):
    return 2 if count % 2 == 0 else 1


def source_at(here, step, count):
    across = pair_width(count)
    along = count // across
    z, y = here // across, here % across
    z = (z ^ step[0]) if along & (along - 1) == 0 else (z + step[0]) % along
    return z * across + (y + step[1]) % across


def fetch(array, step, count):
    return lax.ppermute(array, "row", [(source_at(r, step, count), r) for r in range(count)])


def on_device(alignment, ln_gain, ln_bias, w_left, b_left, w_right, b_right, w_out, b_out):
    seqs, width, _ = alignment.shape
    c = w_left.shape[1]
    row_count = lax.axis_size("row")
    col_count = lax.axis_size("col")
    right, *lefts = features(alignment, ln_gain, ln_bias, w_left, b_left, w_right, b_right,
                             row_count, col_count)

    across = pair_width(row_count)
    along = row_count // across
    rights = {(0, 0): right}
    for a in reversed(range(1, along)):
        rights[a, 0] = fetch(right, (a, 0), row_count)
    if across == 2:
        for a in range(along):
            rights[a, 1] = fetch(rights[a, 0], (0, 1), row_count)

    chips = row_count // col_count
    received = []
    for k, left in enumerate(lefts):
        moves = []
        for r in range(row_count):
            for core in range(col_count):
                place = (r + k) % row_count
                to = (core * chips + place // col_count) * col_count + place % col_count
                moves.append((r * col_count + core, to))
        received.append(lax.ppermute(left, ("row", "col"), moves))
    return pairs(received, rights, w_out, b_out, seqs, c, width, col_count)


def solution(mesh):
    in_specs = (P(("group", "row"), "col", None), P(), P(), P(), P(), P(), P(), P(), P())
    out_specs = P(("group", "row"), "col", None)
    return jax.shard_map(
        on_device, mesh=mesh, in_specs=in_specs, out_specs=out_specs, check_vma=False
    )
```

```python
import functools

import jax
import jax.numpy as jnp
from jax import lax
from jax.experimental import pallas as pl
from jax.experimental.pallas import tpu as pltpu
from jax.sharding import PartitionSpec as P

LANES = 128


def features_kernel(scale, x_ref, gain_ref, bias_ref, wl_ref, bl_ref, wr_ref, br_ref,
                    left_ref, right_ref, normed_ref, left_f32, right_f32):
    seqs, width, channels = x_ref.shape
    c = wl_ref.shape[0]
    fold = LANES // c
    quarter = width // fold
    right_bias = jnp.broadcast_to(br_ref[...], (LANES, c)).T[:, :1]
    for s in range(seqs):
        values = x_ref[s].astype(jnp.float32)
        average = jnp.mean(values, axis=-1, keepdims=True)
        centred = values - average
        variance = jnp.mean(centred * centred, axis=-1, keepdims=True)
        normed = centred * lax.rsqrt(variance + 1e-05) * gain_ref[...] + bias_ref[...]
        for h in range(channels // LANES):
            normed_ref[h, s * width:(s + 1) * width] = normed[:, h * LANES:(h + 1) * LANES]
        right = lax.dot_general(wr_ref[...], normed.astype(jnp.bfloat16), (((1,), (1,)), ((), ())),
                                preferred_element_type=jnp.float32) + right_bias
        for b in range(width // LANES):
            right_f32[pl.ds(b * c * seqs + s, c, stride=seqs), :] = right[:, b * LANES:(b + 1) * LANES]
    total = None
    for q in range(fold):
        part = jnp.concatenate(
            [normed_ref[h, pl.ds(q, seqs * quarter, stride=fold), :] for h in range(channels // LANES)], axis=1
        ).astype(jnp.bfloat16)
        zeros = [jnp.zeros((c, channels), jnp.bfloat16)]
        w = jnp.concatenate(zeros * q + [wl_ref[...]] + zeros * (fold - 1 - q), axis=0)
        term = lax.dot_general(part, w, (((1,), (1,)), ((), ())), preferred_element_type=jnp.float32)
        total = term if total is None else total + term
    total = (total + jnp.concatenate([bl_ref[...]] * fold, axis=1)) * scale
    for s in range(seqs):
        left_f32[pl.ds(s, quarter, stride=seqs), :] = total[s * quarter:(s + 1) * quarter]
    left = left_f32[...].astype(jnp.bfloat16)
    for copy in range(left_ref.shape[0]):
        left_ref[copy] = left
    right_ref[...] = right_f32[...].astype(jnp.bfloat16)


def features(alignment, ln_gain, ln_bias, w_left, b_left, w_right, b_right, row_count, copies):
    seqs, width, channels = alignment.shape
    c = w_left.shape[1]
    rows = seqs * width * c // LANES
    whole = [pl.BlockSpec(shape, lambda i, n=len(shape): (0,) * n)
             for shape in (alignment.shape, (1, channels), (1, channels), (c, channels), (1, c),
                           (c, channels), (1, c))]
    return pl.pallas_call(
        functools.partial(features_kernel, 1.0 / (seqs * row_count)),
        grid=(1,),
        out_shape=(jax.ShapeDtypeStruct((copies, rows, LANES), jnp.bfloat16),
                   jax.ShapeDtypeStruct((rows, LANES), jnp.bfloat16)),
        in_specs=whole,
        out_specs=(pl.BlockSpec((copies, rows, LANES), lambda i: (0, 0, 0)),
                   pl.BlockSpec((rows, LANES), lambda i: (0, 0))),
        scratch_shapes=[pltpu.VMEM((channels // LANES, seqs * width, LANES), jnp.float32),
                        pltpu.VMEM((rows, LANES), jnp.float32),
                        pltpu.VMEM((rows, LANES), jnp.float32)],
        compiler_params=pltpu.CompilerParams(vmem_limit_bytes=60 * 1024 * 1024),
        name="features",
    )(alignment, ln_gain.reshape(1, -1), ln_bias.reshape(1, -1), w_left.T, b_left.reshape(1, -1),
      w_right.T, b_right.reshape(1, -1))


def by_sequence(block, source_of, f32_ref, inner, seqs):
    sources = f32_ref.shape[0]
    for src in range(sources):
        f32_ref[source_of(src)] = block(src)
    if seqs % 8 == 0:
        return lambda n: jnp.concatenate(
            [f32_ref[src, n * seqs:(n + 1) * seqs] for src in range(sources)], axis=0)
    flat = f32_ref.reshape(sources * inner * seqs, LANES)
    return lambda n: jnp.concatenate(
        [flat[pl.ds(n * seqs + s, sources, stride=inner * seqs), :] for s in range(seqs)], axis=0)


def pair_kernel(seqs, c, rows_step, col_count, steps, w_ref, bias_ref, mine_ref, other_ref, *refs):
    sources = len(steps)
    right_refs, refs = refs[:sources], refs[sources:]
    out_ref, left_f32, right_f32, left_t, right_b, w_f32, w_t, outer_ref = refs
    rows, width, z = out_ref.shape[0], out_ref.shape[1], out_ref.shape[2]
    left_rows = left_f32.shape[1]
    blocks = width // LANES
    step = pl.program_id(0)

    @pl.when(step == 0)
    def _():
        here, core = lax.axis_index("row"), lax.axis_index("col")
        mine = here // (sources // col_count) == core
        left_of = by_sequence(
            lambda n: jnp.where(mine, mine_ref[n].astype(jnp.float32), other_ref[n].astype(jnp.float32)),
            lambda n: n, left_f32, left_rows // seqs, seqs)
        for k in range(left_rows // seqs):
            left_t[k * LANES:(k + 1) * LANES] = left_of(k).T.astype(jnp.bfloat16)
        for b in range(blocks):
            right_of = by_sequence(
                lambda n: right_refs[n][b * c * seqs:(b + 1) * c * seqs].astype(jnp.float32),
                lambda n: source_at(here, steps[n], sources), right_f32, c, seqs)
            for e in range(c):
                at = (b * c + e) * LANES
                right_b[:, at:at + LANES] = right_of(e).astype(jnp.bfloat16)
        w_f32[...] = w_ref[...].astype(jnp.float32)
        for e in range(c):
            w_t[:, e * c:(e + 1) * c] = w_f32[pl.ds(e, c, stride=c), :].T.astype(jnp.bfloat16)

    here = left_t[pl.ds(pl.multiple_of(step * rows_step * c, rows_step * c), rows_step * c), :]
    for b in range(blocks):
        for e in range(0, c, 2):
            at = (b * c + e) * LANES
            outer = jnp.dot(here, right_b[:, at:at + 2 * LANES], preferred_element_type=jnp.float32)
            outer = outer.astype(jnp.bfloat16)
            for half in range(2):
                for i in range(rows_step):
                    outer_ref[i // 2, (e + half) * c:(e + half + 1) * c,
                              (i % 2) * LANES:(i % 2 + 1) * LANES] = (
                        outer[i * c:(i + 1) * c, half * LANES:(half + 1) * LANES])
        for p in range(rows_step // 2):
            update = jnp.dot(w_t[...], outer_ref[p], preferred_element_type=jnp.float32)
            for half in range(2):
                mine = update[:, half * LANES:(half + 1) * LANES].T + bias_ref[...]
                out_ref[2 * p + half, b * LANES:(b + 1) * LANES, :] = mine.astype(out_ref.dtype)


def pairs(lefts, rights, w_out, b_out, seqs, c, width, col_count):
    sources, left_rows, _ = lefts[0].shape
    z = w_out.shape[1]
    rows = left_rows * LANES // (c * seqs)
    rows_step = 8
    total = sources * seqs
    steps = list(rights)
    operands = (w_out, b_out.reshape(1, -1), *lefts, *rights.values())
    return pl.pallas_call(
        functools.partial(pair_kernel, seqs, c, rows_step, col_count, steps),
        grid=(rows // rows_step,),
        out_shape=jax.ShapeDtypeStruct((rows, width, z), jnp.bfloat16),
        in_specs=[pl.BlockSpec(a.shape, lambda i, n=a.ndim: (0,) * n) for a in operands],
        out_specs=pl.BlockSpec((rows_step, width, z), lambda i: (i, 0, 0)),
        scratch_shapes=[pltpu.VMEM((sources, left_rows, LANES), jnp.float32),
                        pltpu.VMEM((sources, c * seqs, LANES), jnp.float32),
                        pltpu.VMEM((rows * c, total), jnp.bfloat16),
                        pltpu.VMEM((total, width * c), jnp.bfloat16),
                        pltpu.VMEM(w_out.shape, jnp.float32),
                        pltpu.VMEM((z, c * c), jnp.bfloat16),
                        pltpu.VMEM((rows_step // 2, c * c, 2 * LANES), jnp.bfloat16)],
        compiler_params=pltpu.CompilerParams(vmem_limit_bytes=48 * 1024 * 1024),
        name="pairs",
    )(*operands)


def pair_width(count):
    return 2 if count % 2 == 0 else 1


def source_at(here, step, count):
    across = pair_width(count)
    along = count // across
    z, y = here // across, here % across
    z = (z ^ step[0]) if along & (along - 1) == 0 else (z + step[0]) % along
    return z * across + (y + step[1]) % across


def fetch(array, step, count):
    return lax.ppermute(array, "row", [(source_at(r, step, count), r) for r in range(count)])


def on_device(alignment, ln_gain, ln_bias, w_left, b_left, w_right, b_right, w_out, b_out):
    seqs, width, _ = alignment.shape
    c = w_left.shape[1]
    row_count = lax.axis_size("row")
    col_count = lax.axis_size("col")
    left, right = features(alignment, ln_gain, ln_bias, w_left, b_left, w_right, b_right,
                           row_count, col_count)

    across = pair_width(row_count)
    along = row_count // across
    rights = {(0, 0): right}
    for a in reversed(range(1, along)):
        rights[a, 0] = fetch(right, (a, 0), row_count)
    if across == 2:
        for a in range(along):
            rights[a, 1] = fetch(rights[a, 0], (0, 1), row_count)

    left = left.reshape(row_count, -1, LANES)
    mine = lax.all_to_all(left, "row", split_axis=0, concat_axis=0, tiled=True)
    other = lax.ppermute(mine, "col", [(i, (i + 1) % col_count) for i in range(col_count)])
    return pairs((mine, other), rights, w_out, b_out, seqs, c, width, col_count)


def solution(mesh):
    in_specs = (P(("group", "row"), "col", None), P(), P(), P(), P(), P(), P(), P(), P())
    out_specs = P(("group", "row"), "col", None)
    return jax.shard_map(
        on_device, mesh=mesh, in_specs=in_specs, out_specs=out_specs, check_vma=False
    )
```

```python
import functools

import jax
import jax.numpy as jnp
from jax import lax
from jax.experimental import pallas as pl
from jax.experimental.pallas import tpu as pltpu
from jax.sharding import PartitionSpec as P

LANES = 128
HALVES = 2
VMEM_LIMIT = 60 * 1024 * 1024


def whole(shape):
    return pl.BlockSpec(shape, lambda i: (0,) * len(shape))


def features_kernel(scale, x_ref, gain_ref, bias_ref, wl_ref, bl_ref, wr_ref, br_ref,
                    left_ref, right_ref, normed_ref, left_f32, right_f32):
    seqs, width, channels = x_ref.shape
    c = wl_ref.shape[0]
    part = c // HALVES
    blocks = width // LANES
    fold = LANES // c
    quarter = width // fold
    right_bias = jnp.broadcast_to(br_ref[...], (LANES, c)).T[:, :1]
    for s in range(seqs):
        values = x_ref[s].astype(jnp.float32)
        average = jnp.mean(values, axis=-1, keepdims=True)
        centred = values - average
        variance = jnp.mean(centred * centred, axis=-1, keepdims=True)
        normed = centred * lax.rsqrt(variance + 1e-05) * gain_ref[...] + bias_ref[...]
        for h in range(channels // LANES):
            normed_ref[h, s * width:(s + 1) * width] = normed[:, h * LANES:(h + 1) * LANES]
        right = lax.dot_general(wr_ref[...], normed.astype(jnp.bfloat16), (((1,), (1,)), ((), ())),
                                preferred_element_type=jnp.float32) + right_bias
        for h in range(HALVES):
            for b in range(blocks):
                right_f32[pl.ds((h * blocks + b) * part * seqs + s, part, stride=seqs), :] = (
                    right[h * part:(h + 1) * part, b * LANES:(b + 1) * LANES])
    total = None
    for q in range(fold):
        rows = jnp.concatenate(
            [normed_ref[h, pl.ds(q, seqs * quarter, stride=fold), :] for h in range(channels // LANES)], axis=1
        ).astype(jnp.bfloat16)
        zeros = [jnp.zeros((c, channels), jnp.bfloat16)]
        w = jnp.concatenate(zeros * q + [wl_ref[...]] + zeros * (fold - 1 - q), axis=0)
        term = lax.dot_general(rows, w, (((1,), (1,)), ((), ())), preferred_element_type=jnp.float32)
        total = term if total is None else total + term
    total = (total + jnp.concatenate([bl_ref[...]] * fold, axis=1)) * scale
    for s in range(seqs):
        left_f32[pl.ds(s, quarter, stride=seqs), :] = total[s * quarter:(s + 1) * quarter]
    left_ref[...] = left_f32[...].astype(jnp.bfloat16)
    right_ref[...] = right_f32[...].astype(jnp.bfloat16)


def features(alignment, ln_gain, ln_bias, w_left, b_left, w_right, b_right, scale):
    seqs, width, channels = alignment.shape
    c = w_left.shape[1]
    rows = seqs * width * c // LANES
    operands = (alignment, ln_gain.reshape(1, -1), ln_bias.reshape(1, -1), w_left.T, b_left.reshape(1, -1),
                w_right.T, b_right.reshape(1, -1))
    return pl.pallas_call(
        functools.partial(features_kernel, scale),
        grid=(1,),
        out_shape=(jax.ShapeDtypeStruct((rows, LANES), jnp.bfloat16),) * 2,
        in_specs=[whole(a.shape) for a in operands],
        out_specs=(whole((rows, LANES)),) * 2,
        scratch_shapes=[pltpu.VMEM((channels // LANES, seqs * width, LANES), jnp.float32),
                        pltpu.VMEM((rows, LANES), jnp.float32),
                        pltpu.VMEM((rows, LANES), jnp.float32)],
        compiler_params=pltpu.CompilerParams(vmem_limit_bytes=VMEM_LIMIT),
        name="features",
    )(*operands)


def repeat_kernel(left_ref, after_ref, out_ref):
    for copy in range(out_ref.shape[0]):
        out_ref[copy] = left_ref[...]


def repeat_after(left, after, copies):
    return pl.pallas_call(
        repeat_kernel,
        grid=(1,),
        out_shape=jax.ShapeDtypeStruct((copies,) + left.shape, left.dtype),
        in_specs=[whole(left.shape), pl.BlockSpec(memory_space=pl.ANY)],
        out_specs=whole((copies,) + left.shape),
        compiler_params=pltpu.CompilerParams(vmem_limit_bytes=VMEM_LIMIT),
        name="repeat",
    )(left, after)


def sequence_rows(block, f32_ref, inner, seqs):
    sources = f32_ref.shape[0]
    for n in range(sources):
        f32_ref[n] = block(n)
    if seqs % 8 == 0:
        return lambda m: jnp.concatenate(
            [f32_ref[n, m * seqs:(m + 1) * seqs] for n in range(sources)], axis=0)
    flat = f32_ref.reshape(sources * inner * seqs, LANES)
    return lambda m: jnp.concatenate(
        [flat[pl.ds(m * seqs + s, sources, stride=inner * seqs), :] for s in range(seqs)], axis=0)


def prepare_kernel(seqs, c, col_count, steps, mine_ref, other_ref, w_ref, left_ref, weights_ref,
                   left_f32, w_f32):
    sources, left_rows, _ = mine_ref.shape
    here, core = lax.axis_index("row"), lax.axis_index("col")
    mine = here // (sources // col_count) == core

    def block(n):
        source = source_at(here, steps[n], sources)
        return jnp.where(mine, mine_ref[source].astype(jnp.float32), other_ref[source].astype(jnp.float32))

    left_of = sequence_rows(block, left_f32, left_rows // seqs, seqs)
    for k in range(left_rows // seqs):
        left_ref[k * LANES:(k + 1) * LANES] = left_of(k).T.astype(jnp.bfloat16)
    w_f32[...] = w_ref[...].astype(jnp.float32)
    for e in range(c):
        weights_ref[:, e * c:(e + 1) * c] = w_f32[pl.ds(e, c, stride=c), :].T.astype(jnp.bfloat16)


def prepare(mine, other, w_out, steps, seqs, c, col_count):
    sources, left_rows, _ = mine.shape
    shapes = ((left_rows // seqs * LANES, sources * seqs), (w_out.shape[1], w_out.shape[0]))
    operands = (mine, other, w_out)
    return pl.pallas_call(
        functools.partial(prepare_kernel, seqs, c, col_count, steps),
        grid=(1,),
        out_shape=[jax.ShapeDtypeStruct(shape, jnp.bfloat16) for shape in shapes],
        in_specs=[whole(a.shape) for a in operands],
        out_specs=[whole(shape) for shape in shapes],
        scratch_shapes=[pltpu.VMEM(mine.shape, jnp.float32), pltpu.VMEM(w_out.shape, jnp.float32)],
        name="prepare",
    )(*operands)


def pair_kernel(seqs, c, first, last, left_ref, weights_ref, near_ref, far_ref, *refs):
    if not first:
        so_far_ref, refs = refs[0], refs[1:]
    if last:
        bias_ref, refs = refs[0], refs[1:]
    out_ref, right_f32, right_b, outer_ref = refs
    rows_step = out_ref.shape[0]
    along = near_ref.shape[0]
    part = right_f32.shape[1] // seqs
    blocks = right_b.shape[1] // LANES // part

    @pl.when(pl.program_id(0) == 0)
    def _():
        for b in range(blocks):
            at = b * part * seqs
            right_of = sequence_rows(
                lambda n: (near_ref if n < along else far_ref)[n % along, at:at + part * seqs].astype(jnp.float32),
                right_f32, part, seqs)
            for e in range(part):
                lanes = (b * part + e) * LANES
                right_b[:, lanes:lanes + LANES] = right_of(e).astype(jnp.bfloat16)

    for b in range(blocks):
        for e in range(0, part, 2):
            at = (b * part + e) * LANES
            outer = jnp.dot(left_ref[...], right_b[:, at:at + 2 * LANES], preferred_element_type=jnp.float32)
            outer = outer.astype(jnp.bfloat16)
            for half in range(2):
                for i in range(rows_step):
                    outer_ref[i // 2, (e + half) * c:(e + half + 1) * c,
                              (i % 2) * LANES:(i % 2 + 1) * LANES] = (
                        outer[i * c:(i + 1) * c, half * LANES:(half + 1) * LANES])
        for p in range(rows_step // 2):
            update = jnp.dot(weights_ref[...], outer_ref[p], preferred_element_type=jnp.float32)
            for half in range(2):
                mine = update[:, half * LANES:(half + 1) * LANES]
                i = 2 * p + half
                if not first:
                    mine = mine + so_far_ref[i, b]
                if last:
                    out_ref[i, b * LANES:(b + 1) * LANES, :] = (mine.T + bias_ref[...]).astype(out_ref.dtype)
                else:
                    out_ref[i, b] = mine


def pairs(half, left, weights, near, far, so_far, bias, seqs, c, width):
    along = near.shape[0]
    sources = 2 * along
    z = weights.shape[0]
    part = c // HALVES
    blocks = width // LANES
    rows = left.shape[0] // c
    rows_step = 8
    total = sources * seqs
    first, last = so_far is None, bias is not None
    sums = pl.BlockSpec((rows_step, blocks, z, LANES), lambda i: (i, 0, 0, 0))
    operands = [left, weights, near, far]
    in_specs = [pl.BlockSpec((rows_step * c, total), lambda i: (i, 0)),
                pl.BlockSpec((z, part * c), lambda i: (0, half)), whole(near.shape), whole(far.shape)]
    if not first:
        operands.append(so_far)
        in_specs.append(sums)
    if last:
        operands.append(bias.reshape(1, -1))
        in_specs.append(whole((1, z)))
    if last:
        out_shape = jax.ShapeDtypeStruct((rows, width, z), jnp.bfloat16)
        out_spec = pl.BlockSpec((rows_step, width, z), lambda i: (i, 0, 0))
    else:
        out_shape = jax.ShapeDtypeStruct((rows, blocks, z, LANES), jnp.float32)
        out_spec = sums
    return pl.pallas_call(
        functools.partial(pair_kernel, seqs, c, first, last),
        grid=(rows // rows_step,),
        out_shape=out_shape,
        in_specs=in_specs,
        out_specs=out_spec,
        scratch_shapes=[pltpu.VMEM((sources, part * seqs, LANES), jnp.float32),
                        pltpu.VMEM((total, width * part), jnp.bfloat16),
                        pltpu.VMEM((rows_step // 2, part * c, 2 * LANES), jnp.bfloat16)],
        compiler_params=pltpu.CompilerParams(vmem_limit_bytes=32 * 1024 * 1024),
        cost_estimate=pl.CostEstimate(flops=2 * rows * c * width * part * (total + z),
                                      bytes_accessed=4 * rows * width * z, transcendentals=0),
        name="pairs",
    )(*operands)


def source_at(here, step, count):
    along = count // 2
    n, across = here // 2, here % 2
    n = (n ^ step[0]) if along & (along - 1) == 0 else (n + step[0]) % along
    return n * 2 + (across + step[1]) % 2


def fetch(array, step, count):
    return lax.ppermute(array, "row", [(source_at(r, step, count), r) for r in range(count)])


def on_device(alignment, ln_gain, ln_bias, w_left, b_left, w_right, b_right, w_out, b_out):
    seqs, width, _ = alignment.shape
    c = w_left.shape[1]
    row_count = lax.axis_size("row")
    col_count = lax.axis_size("col")
    along = row_count // 2
    left, right = features(alignment, ln_gain, ln_bias, w_left, b_left, w_right, b_right,
                           1.0 / (seqs * row_count))

    blocks = [right] + [fetch(right, (a, 0), row_count) for a in range(1, along)]
    left = repeat_after(left, blocks[1], col_count).reshape(row_count, -1, LANES)
    mine = lax.all_to_all(left, "row", split_axis=0, concat_axis=0, tiled=True)
    other = lax.ppermute(mine, "col", [(i, (i + 1) % col_count) for i in range(col_count)])
    steps = [(a, b) for b in range(2) for a in range(along)]
    left, weights = prepare(mine, other, w_out, steps, seqs, c, col_count)

    rows = right.shape[0] // HALVES
    near = [jnp.stack([block[h * rows:(h + 1) * rows] for block in blocks]) for h in range(HALVES)]
    far = [fetch(part, (0, 1), row_count) for part in near]
    sums = None
    for h in range(HALVES):
        sums = pairs(h, left, weights, near[h], far[h], sums, b_out if h == HALVES - 1 else None, seqs, c, width)
    return sums


def solution(mesh):
    in_specs = (P(("group", "row"), "col", None), P(), P(), P(), P(), P(), P(), P(), P())
    out_specs = P(("group", "row"), "col", None)
    return jax.shard_map(
        on_device, mesh=mesh, in_specs=in_specs, out_specs=out_specs, check_vma=False
    )
```

```python
import functools

import jax
import jax.numpy as jnp
from jax import lax
from jax.experimental import pallas as pl
from jax.experimental.pallas import tpu as pltpu
from jax.sharding import PartitionSpec as P

LANES = 128
VMEM_LIMIT = 60 * 1024 * 1024


def whole(shape):
    return pl.BlockSpec(shape, lambda i: (0,) * len(shape))


def features_kernel(scale, x_ref, gain_ref, bias_ref, wl_ref, bl_ref, wr_ref, br_ref,
                    left_ref, right_ref, normed_ref, left_f32, right_f32):
    seqs, width, channels = x_ref.shape
    c = wl_ref.shape[0]
    blocks = width // LANES
    fold = LANES // c
    quarter = width // fold
    right_bias = jnp.broadcast_to(br_ref[...], (LANES, c)).T[:, :1]
    for s in range(seqs):
        values = x_ref[s].astype(jnp.float32)
        average = jnp.mean(values, axis=-1, keepdims=True)
        centred = values - average
        variance = jnp.mean(centred * centred, axis=-1, keepdims=True)
        normed = centred * lax.rsqrt(variance + 1e-05) * gain_ref[...] + bias_ref[...]
        for h in range(channels // LANES):
            normed_ref[h, s * width:(s + 1) * width] = normed[:, h * LANES:(h + 1) * LANES]
        right = lax.dot_general(wr_ref[...], normed.astype(jnp.bfloat16), (((1,), (1,)), ((), ())),
                                preferred_element_type=jnp.float32) + right_bias
        for b in range(blocks):
            right_f32[pl.ds(b * c * seqs + s, c, stride=seqs), :] = right[:, b * LANES:(b + 1) * LANES]
    total = None
    for q in range(fold):
        rows = jnp.concatenate(
            [normed_ref[h, pl.ds(q, seqs * quarter, stride=fold), :] for h in range(channels // LANES)], axis=1
        ).astype(jnp.bfloat16)
        zeros = [jnp.zeros((c, channels), jnp.bfloat16)]
        w = jnp.concatenate(zeros * q + [wl_ref[...]] + zeros * (fold - 1 - q), axis=0)
        term = lax.dot_general(rows, w, (((1,), (1,)), ((), ())), preferred_element_type=jnp.float32)
        total = term if total is None else total + term
    total = (total + jnp.concatenate([bl_ref[...]] * fold, axis=1)) * scale
    for s in range(seqs):
        left_f32[pl.ds(s, quarter, stride=seqs), :] = total[s * quarter:(s + 1) * quarter]
    along, _, rows, _ = left_ref.shape
    across = lax.rem(lax.axis_index("row"), 2)
    for n in range(along):
        for b in range(2):
            block = lax.rem(n * 2 + lax.rem(across + b, 2), left_f32.shape[0] // rows)
            left_ref[n, b] = left_f32[pl.ds(pl.multiple_of(block * rows, rows), rows), :].astype(jnp.bfloat16)
    right_ref[...] = right_f32[...].astype(jnp.bfloat16)


def features(alignment, ln_gain, ln_bias, w_left, b_left, w_right, b_right, row_count, col_count):
    seqs, width, channels = alignment.shape
    c = w_left.shape[1]
    rows = seqs * width * c // LANES
    shapes = ((row_count // 2, 2, rows * col_count // row_count, LANES), (rows, LANES))
    operands = (alignment, ln_gain.reshape(1, -1), ln_bias.reshape(1, -1), w_left.T, b_left.reshape(1, -1),
                w_right.T, b_right.reshape(1, -1))
    return pl.pallas_call(
        functools.partial(features_kernel, 1.0 / (seqs * row_count)),
        grid=(1,),
        out_shape=[jax.ShapeDtypeStruct(shape, jnp.bfloat16) for shape in shapes],
        in_specs=[whole(a.shape) for a in operands],
        out_specs=[whole(shape) for shape in shapes],
        scratch_shapes=[pltpu.VMEM((channels // LANES, seqs * width, LANES), jnp.float32),
                        pltpu.VMEM((rows, LANES), jnp.float32),
                        pltpu.VMEM((rows, LANES), jnp.float32)],
        compiler_params=pltpu.CompilerParams(vmem_limit_bytes=VMEM_LIMIT),
        name="features",
    )(*operands)


def sequence_rows(block, f32_ref, inner, seqs):
    sources = f32_ref.shape[0]
    for n in range(sources):
        f32_ref[n] = block(n)
    if seqs % 8 == 0:
        return lambda m: jnp.concatenate(
            [f32_ref[n, m * seqs:(m + 1) * seqs] for n in range(sources)], axis=0)
    flat = f32_ref.reshape(sources * inner * seqs, LANES)
    return lambda m: jnp.concatenate(
        [flat[pl.ds(m * seqs + s, sources, stride=inner * seqs), :] for s in range(seqs)], axis=0)


def prepare_kernel(seqs, c, col_count, steps, mine_ref, other_ref, w_ref, own_ref,
                   left_ref, weights_ref, right_ref, left_f32, w_f32):
    sources, left_rows, _ = mine_ref.shape
    along = sources // 2
    here, core = lax.axis_index("row"), lax.axis_index("col")
    mine = here // (sources // col_count) == core

    def block(n):
        source = steps[n][1] * along + source_at(here, steps[n], sources) // 2
        return jnp.where(mine, mine_ref[source].astype(jnp.float32), other_ref[source].astype(jnp.float32))

    left_of = sequence_rows(block, left_f32, left_rows // seqs, seqs)
    for k in range(left_rows // seqs):
        left_ref[k * LANES:(k + 1) * LANES] = left_of(k).T.astype(jnp.bfloat16)
    w_f32[...] = w_ref[...].astype(jnp.float32)
    for e in range(c):
        weights_ref[:, e * c:(e + 1) * c] = w_f32[pl.ds(e, c, stride=c), :].T.astype(jnp.bfloat16)
    right_ref[...] = own_ref[...]


def prepare(mine, other, w_out, right, steps, seqs, c, col_count):
    sources, left_rows, _ = mine.shape
    shapes = ((left_rows // seqs * LANES, sources * seqs), (w_out.shape[1], w_out.shape[0]), right.shape)
    operands = (mine, other, w_out, right)
    return pl.pallas_call(
        functools.partial(prepare_kernel, seqs, c, col_count, steps),
        grid=(1,),
        out_shape=[jax.ShapeDtypeStruct(shape, jnp.bfloat16) for shape in shapes],
        in_specs=[whole(a.shape) for a in operands],
        out_specs=[whole(shape) for shape in shapes],
        scratch_shapes=[pltpu.VMEM(mine.shape, jnp.float32), pltpu.VMEM(w_out.shape, jnp.float32)],
        compiler_params=pltpu.CompilerParams(vmem_limit_bytes=48 * 1024 * 1024),
        name="prepare",
    )(*operands)


def pair_kernel(seqs, c, sources, left_ref, weights_ref, bias_ref, *refs):
    right_refs, (out_ref, right_f32, right_b, outer_ref) = refs[:sources], refs[sources:]
    rows_step = out_ref.shape[0]
    blocks = out_ref.shape[1] // LANES

    @pl.when(pl.program_id(0) == 0)
    def _():
        for b in range(blocks):
            at = b * c * seqs
            right_of = sequence_rows(
                lambda n: right_refs[n][at:at + c * seqs].astype(jnp.float32), right_f32, c, seqs)
            for e in range(c):
                lanes = (b * c + e) * LANES
                right_b[:, lanes:lanes + LANES] = right_of(e).astype(jnp.bfloat16)

    for b in range(blocks):
        for e in range(0, c, 2):
            at = (b * c + e) * LANES
            outer = jnp.dot(left_ref[...], right_b[:, at:at + 2 * LANES], preferred_element_type=jnp.float32)
            outer = outer.astype(jnp.bfloat16)
            for half in range(2):
                for i in range(rows_step):
                    outer_ref[i // 2, (e + half) * c:(e + half + 1) * c,
                              (i % 2) * LANES:(i % 2 + 1) * LANES] = (
                        outer[i * c:(i + 1) * c, half * LANES:(half + 1) * LANES])
        for p in range(rows_step // 2):
            update = jnp.dot(weights_ref[...], outer_ref[p], preferred_element_type=jnp.float32)
            for half in range(2):
                mine = update[:, half * LANES:(half + 1) * LANES].T + bias_ref[...]
                out_ref[2 * p + half, b * LANES:(b + 1) * LANES, :] = mine.astype(out_ref.dtype)


def pairs(left, weights, bias, rights, seqs, c, width):
    sources = len(rights)
    z = weights.shape[0]
    rows = left.shape[0] // c
    rows_step = 8
    total = sources * seqs
    operands = (left, weights, bias.reshape(1, -1), *rights)
    return pl.pallas_call(
        functools.partial(pair_kernel, seqs, c, sources),
        grid=(rows // rows_step,),
        out_shape=jax.ShapeDtypeStruct((rows, width, z), jnp.bfloat16),
        in_specs=[pl.BlockSpec((rows_step * c, total), lambda i: (i, 0))] + [whole(a.shape) for a in operands[1:]],
        out_specs=pl.BlockSpec((rows_step, width, z), lambda i: (i, 0, 0)),
        scratch_shapes=[pltpu.VMEM((sources, c * seqs, LANES), jnp.float32),
                        pltpu.VMEM((total, width * c), jnp.bfloat16),
                        pltpu.VMEM((rows_step // 2, c * c, 2 * LANES), jnp.bfloat16)],
        compiler_params=pltpu.CompilerParams(vmem_limit_bytes=32 * 1024 * 1024),
        cost_estimate=pl.CostEstimate(flops=2 * rows * c * width * c * (total + z),
                                      bytes_accessed=2 * rows * width * z, transcendentals=0),
        name="pairs",
    )(*operands)


def source_at(here, step, count):
    along = count // 2
    n, across = here // 2, here % 2
    n = (n ^ step[0]) if along & (along - 1) == 0 else (n + step[0]) % along
    return n * 2 + (across + step[1]) % 2


def fetch(array, step, count):
    return lax.ppermute(array, "row", [(source_at(r, step, count), r) for r in range(count)])


def on_device(alignment, ln_gain, ln_bias, w_left, b_left, w_right, b_right, w_out, b_out):
    seqs, width, _ = alignment.shape
    c = w_left.shape[1]
    row_count = lax.axis_size("row")
    col_count = lax.axis_size("col")
    along = row_count // 2
    left, right = features(alignment, ln_gain, ln_bias, w_left, b_left, w_right, b_right, row_count, col_count)

    lines = [list(range(y, row_count, 2)) for y in range(2)]
    left = lax.all_to_all(left, "row", split_axis=0, concat_axis=0, axis_index_groups=lines, tiled=True)
    mine = jnp.concatenate([left[:, 0], fetch(left[:, 1], (0, 1), row_count)])
    other = lax.ppermute(mine, "col", [(i, (i + 1) % col_count) for i in range(col_count)])

    near = {0: right}
    for a in reversed(range(1, along)):
        near[a] = fetch(right, (a, 0), row_count)
    far = {a: fetch(near[a], (0, 1), row_count) for a in near}
    steps = [(a, b) for b in range(2) for a in near]
    left, weights, right = prepare(mine, other, w_out, right, steps, seqs, c, col_count)
    near[0] = right
    return pairs(left, weights, b_out, [*near.values(), *far.values()], seqs, c, width)


def solution(mesh):
    in_specs = (P(("group", "row"), "col", None), P(), P(), P(), P(), P(), P(), P(), P())
    out_specs = P(("group", "row"), "col", None)
    return jax.shard_map(
        on_device, mesh=mesh, in_specs=in_specs, out_specs=out_specs, check_vma=False
    )
```

```python
import functools

import jax
import jax.numpy as jnp
from jax import lax
from jax.experimental import pallas as pl
from jax.experimental.pallas import tpu as pltpu
from jax.sharding import PartitionSpec as P

LANES = 128
VMEM_LIMIT = 60 * 1024 * 1024


def whole(shape):
    return pl.BlockSpec(shape, lambda i: (0,) * len(shape))


def features_kernel(scale, x_ref, gain_ref, bias_ref, wl_ref, bl_ref, wr_ref, br_ref,
                    *refs):
    messages, (normed_ref, left_f32, right_f32) = refs[:-3], refs[-3:]
    seqs, width, channels = x_ref.shape
    c = wl_ref.shape[0]
    blocks = width // LANES
    fold = LANES // c
    quarter = width // fold
    right_bias = jnp.broadcast_to(br_ref[...], (LANES, c)).T[:, :1]
    for s in range(seqs):
        values = x_ref[s].astype(jnp.float32)
        average = jnp.mean(values, axis=-1, keepdims=True)
        centred = values - average
        variance = jnp.mean(centred * centred, axis=-1, keepdims=True)
        normed = centred * lax.rsqrt(variance + 1e-05) * gain_ref[...] + bias_ref[...]
        for h in range(channels // LANES):
            normed_ref[h, s * width:(s + 1) * width] = normed[:, h * LANES:(h + 1) * LANES]
        right = lax.dot_general(wr_ref[...], normed.astype(jnp.bfloat16), (((1,), (1,)), ((), ())),
                                preferred_element_type=jnp.float32) + right_bias
        for b in range(blocks):
            right_f32[pl.ds(b * c * seqs + s, c, stride=seqs), :] = right[:, b * LANES:(b + 1) * LANES]
    total = None
    for q in range(fold):
        rows = jnp.concatenate(
            [normed_ref[h, pl.ds(q, seqs * quarter, stride=fold), :] for h in range(channels // LANES)], axis=1
        ).astype(jnp.bfloat16)
        zeros = [jnp.zeros((c, channels), jnp.bfloat16)]
        w = jnp.concatenate(zeros * q + [wl_ref[...]] + zeros * (fold - 1 - q), axis=0)
        term = lax.dot_general(rows, w, (((1,), (1,)), ((), ())), preferred_element_type=jnp.float32)
        total = term if total is None else total + term
    total = (total + jnp.concatenate([bl_ref[...]] * fold, axis=1)) * scale
    for s in range(seqs):
        left_f32[pl.ds(s, quarter, stride=seqs), :] = total[s * quarter:(s + 1) * quarter]
    here = lax.axis_index("row")
    right = right_f32[...].astype(jnp.bfloat16)
    count = len(messages)
    for step, message in zip(steps_of(count), messages):
        with_right = carries_right(step)
        left_rows = message.shape[0] - right.shape[0] * with_right
        block = lax.rem(source_at(here, step, count), left_f32.shape[0] // left_rows)
        left = left_f32[pl.ds(pl.multiple_of(block * left_rows, left_rows), left_rows), :].astype(jnp.bfloat16)
        message[message.shape[0] - left_rows:] = left
        if with_right:
            message[:right.shape[0]] = right


def features(alignment, ln_gain, ln_bias, w_left, b_left, w_right, b_right, row_count, col_count):
    seqs, width, channels = alignment.shape
    c = w_left.shape[1]
    rows = seqs * width * c // LANES
    shapes = [(rows * carries_right(step) + rows * col_count // row_count, LANES) for step in steps_of(row_count)]
    operands = (alignment, ln_gain.reshape(1, -1), ln_bias.reshape(1, -1), w_left.T, b_left.reshape(1, -1),
                w_right.T, b_right.reshape(1, -1))
    return pl.pallas_call(
        functools.partial(features_kernel, 1.0 / (seqs * row_count)),
        grid=(1,),
        out_shape=[jax.ShapeDtypeStruct(shape, jnp.bfloat16) for shape in shapes],
        in_specs=[whole(a.shape) for a in operands],
        out_specs=[whole(shape) for shape in shapes],
        scratch_shapes=[pltpu.VMEM((channels // LANES, seqs * width, LANES), jnp.float32),
                        pltpu.VMEM((rows, LANES), jnp.float32),
                        pltpu.VMEM((rows, LANES), jnp.float32)],
        compiler_params=pltpu.CompilerParams(vmem_limit_bytes=VMEM_LIMIT),
        name="features",
    )(*operands)


def sequence_rows(block, f32_ref, inner, seqs):
    sources = f32_ref.shape[0]
    for n in range(sources):
        f32_ref[n] = block(n)
    if seqs % 8 == 0:
        return lambda m: jnp.concatenate(
            [f32_ref[n, m * seqs:(m + 1) * seqs] for n in range(sources)], axis=0)
    flat = f32_ref.reshape(sources * inner * seqs, LANES)
    return lambda m: jnp.concatenate(
        [flat[pl.ds(m * seqs + s, sources, stride=inner * seqs), :] for s in range(seqs)], axis=0)


def prepare_kernel(seqs, c, left_rows, w_ref, bias_ref, *refs):
    messages, refs = refs[:-6], refs[-6:]
    left_ref, weights_ref, right_ref, bias_out_ref, left_f32, w_f32 = refs
    left_of = sequence_rows(lambda n: messages[n][messages[n].shape[0] - left_rows:].astype(jnp.float32),
                            left_f32, left_rows // seqs, seqs)
    for k in range(left_rows // seqs):
        left_ref[k * LANES:(k + 1) * LANES] = left_of(k).T.astype(jnp.bfloat16)
    w_f32[...] = w_ref[...].astype(jnp.float32)
    for e in range(c):
        weights_ref[:, e * c:(e + 1) * c] = w_f32[pl.ds(e, c, stride=c), :].T.astype(jnp.bfloat16)
    right_ref[...] = messages[0][:right_ref.shape[0]]
    bias_out_ref[...] = bias_ref[...]


def prepare(messages, w_out, b_out, seqs, c, left_rows):
    sources = len(messages)
    z = w_out.shape[1]
    outs = [((left_rows // seqs * LANES, sources * seqs), jnp.bfloat16), ((z, w_out.shape[0]), jnp.bfloat16),
            ((messages[0].shape[0] - left_rows, LANES), jnp.bfloat16), ((1, z), jnp.float32)]
    operands = (w_out, b_out.reshape(1, -1), *messages)
    return pl.pallas_call(
        functools.partial(prepare_kernel, seqs, c, left_rows),
        grid=(1,),
        out_shape=[jax.ShapeDtypeStruct(*out) for out in outs],
        in_specs=[whole(a.shape) for a in operands],
        out_specs=[whole(out[0]) for out in outs],
        scratch_shapes=[pltpu.VMEM((sources, left_rows, LANES), jnp.float32), pltpu.VMEM(w_out.shape, jnp.float32)],
        compiler_params=pltpu.CompilerParams(vmem_limit_bytes=48 * 1024 * 1024),
        name="prepare",
    )(*operands)


def pair_kernel(seqs, c, sources, col_count, mine_ref, other_ref, weights_ref, bias_ref, *refs):
    right_refs, (out_ref, right_f32, right_b, outer_ref) = refs[:sources], refs[sources:]
    rows_step = out_ref.shape[0]
    blocks = out_ref.shape[1] // LANES

    @pl.when(pl.program_id(0) == 0)
    def _():
        for b in range(blocks):
            at = b * c * seqs
            right_of = sequence_rows(
                lambda n: right_refs[n][at:at + c * seqs].astype(jnp.float32), right_f32, c, seqs)
            for e in range(c):
                lanes = (b * c + e) * LANES
                right_b[:, lanes:lanes + LANES] = right_of(e).astype(jnp.bfloat16)

    half = lax.axis_index("row") // (sources // col_count)
    left = jnp.where(half == lax.axis_index("col"), mine_ref[...], other_ref[...])
    for b in range(blocks):
        for e in range(0, c, 2):
            at = (b * c + e) * LANES
            outer = jnp.dot(left, right_b[:, at:at + 2 * LANES], preferred_element_type=jnp.float32)
            outer = outer.astype(jnp.bfloat16)
            for half in range(2):
                for i in range(rows_step):
                    outer_ref[i // 2, (e + half) * c:(e + half + 1) * c,
                              (i % 2) * LANES:(i % 2 + 1) * LANES] = (
                        outer[i * c:(i + 1) * c, half * LANES:(half + 1) * LANES])
        for p in range(rows_step // 2):
            update = jnp.dot(weights_ref[...], outer_ref[p], preferred_element_type=jnp.float32)
            for half in range(2):
                mine = update[:, half * LANES:(half + 1) * LANES].T + bias_ref[...]
                out_ref[2 * p + half, b * LANES:(b + 1) * LANES, :] = mine.astype(out_ref.dtype)


def pairs(mine, other, weights, bias, rights, seqs, c, width, col_count):
    sources = len(rights)
    z = weights.shape[0]
    rows = mine.shape[0] // c
    rows_step = 8
    total = sources * seqs
    operands = (mine, other, weights, bias, *rights)
    return pl.pallas_call(
        functools.partial(pair_kernel, seqs, c, sources, col_count),
        grid=(rows // rows_step,),
        out_shape=jax.ShapeDtypeStruct((rows, width, z), jnp.bfloat16),
        in_specs=[pl.BlockSpec((rows_step * c, total), lambda i: (i, 0))] * 2 + [whole(a.shape) for a in operands[2:]],
        out_specs=pl.BlockSpec((rows_step, width, z), lambda i: (i, 0, 0)),
        scratch_shapes=[pltpu.VMEM((sources, c * seqs, LANES), jnp.float32),
                        pltpu.VMEM((total, width * c), jnp.bfloat16),
                        pltpu.VMEM((rows_step // 2, c * c, 2 * LANES), jnp.bfloat16)],
        compiler_params=pltpu.CompilerParams(vmem_limit_bytes=32 * 1024 * 1024),
        cost_estimate=pl.CostEstimate(flops=2 * rows * c * width * c * (total + z),
                                      bytes_accessed=2 * rows * width * z, transcendentals=0),
        name="pairs",
    )(*operands)


def source_at(here, step, count):
    along = count // 2
    n, across = here // 2, here % 2
    n = (n ^ step[0]) if along & (along - 1) == 0 else (n + step[0]) % along
    return n * 2 + (across + step[1]) % 2


def steps_of(count):
    return [(a, b) for b in range(2) for a in range(count // 2)]


def carries_right(step):
    return step[0] == 0 or step[1] == 0


def fetch(array, step, count):
    return lax.ppermute(array, "row", [(source_at(r, step, count), r) for r in range(count)])


def on_device(alignment, ln_gain, ln_bias, w_left, b_left, w_right, b_right, w_out, b_out):
    seqs, width, _ = alignment.shape
    c = w_left.shape[1]
    row_count = lax.axis_size("row")
    col_count = lax.axis_size("col")
    messages = features(alignment, ln_gain, ln_bias, w_left, b_left, w_right, b_right, row_count, col_count)
    steps = steps_of(row_count)
    left_rows = messages[-1].shape[0]
    right_rows = messages[0].shape[0] - left_rows

    here = {step: message if step == (0, 0) else fetch(message, step, row_count)
            for step, message in zip(steps, messages)}
    rights = {step: here[step] if carries_right(step) else fetch(here[step[0], 0][:right_rows], (0, 1), row_count)
              for step in steps}
    mine, weights, rights[0, 0], bias = prepare(list(here.values()), w_out, b_out, seqs, c, left_rows)
    other = lax.ppermute(mine, "col", [(i, (i + 1) % col_count) for i in range(col_count)])
    return pairs(mine, other, weights, bias, list(rights.values()), seqs, c, width, col_count)


def solution(mesh):
    in_specs = (P(("group", "row"), "col", None), P(), P(), P(), P(), P(), P(), P(), P())
    out_specs = P(("group", "row"), "col", None)
    return jax.shard_map(
        on_device, mesh=mesh, in_specs=in_specs, out_specs=out_specs, check_vma=False
    )
```

```python
import functools

import jax
import jax.numpy as jnp
from jax import lax
from jax.experimental import pallas as pl
from jax.experimental.pallas import tpu as pltpu
from jax.sharding import PartitionSpec as P

LANES = 128
VMEM_LIMIT = 60 * 1024 * 1024


def whole(shape):
    return pl.BlockSpec(shape, lambda i: (0,) * len(shape))


def features_kernel(scale, x_ref, gain_ref, bias_ref, wl_ref, bl_ref, wr_ref, br_ref,
                    *refs):
    outs, (normed_ref, left_f32, right_f32) = refs[:-3], refs[-3:]
    seqs, width, channels = x_ref.shape
    c = wl_ref.shape[0]
    blocks = width // LANES
    fold = LANES // c
    quarter = width // fold
    right_bias = jnp.broadcast_to(br_ref[...], (LANES, c)).T[:, :1]
    for s in range(seqs):
        values = x_ref[s].astype(jnp.float32)
        average = jnp.mean(values, axis=-1, keepdims=True)
        centred = values - average
        variance = jnp.mean(centred * centred, axis=-1, keepdims=True)
        normed = centred * lax.rsqrt(variance + 1e-05) * gain_ref[...] + bias_ref[...]
        for h in range(channels // LANES):
            normed_ref[h, s * width:(s + 1) * width] = normed[:, h * LANES:(h + 1) * LANES]
        right = lax.dot_general(wr_ref[...], normed.astype(jnp.bfloat16), (((1,), (1,)), ((), ())),
                                preferred_element_type=jnp.float32) + right_bias
        for b in range(blocks):
            right_f32[pl.ds(b * c * seqs + s, c, stride=seqs), :] = right[:, b * LANES:(b + 1) * LANES]
    total = None
    for q in range(fold):
        rows = jnp.concatenate(
            [normed_ref[h, pl.ds(q, seqs * quarter, stride=fold), :] for h in range(channels // LANES)], axis=1
        ).astype(jnp.bfloat16)
        zeros = [jnp.zeros((c, channels), jnp.bfloat16)]
        w = jnp.concatenate(zeros * q + [wl_ref[...]] + zeros * (fold - 1 - q), axis=0)
        term = lax.dot_general(rows, w, (((1,), (1,)), ((), ())), preferred_element_type=jnp.float32)
        total = term if total is None else total + term
    total = (total + jnp.concatenate([bl_ref[...]] * fold, axis=1)) * scale
    for s in range(seqs):
        left_f32[pl.ds(s, quarter, stride=seqs), :] = total[s * quarter:(s + 1) * quarter]
    right_ref, *left_refs = outs
    here = lax.axis_index("row")
    for step, left_ref in zip(half_steps(len(left_refs)), left_refs):
        rows = left_ref.shape[0]
        block = source_at(here, step) % len(left_refs)
        left_ref[...] = left_f32[pl.ds(pl.multiple_of(block * rows, rows), rows), :].astype(jnp.bfloat16)
    right_ref[...] = right_f32[...].astype(jnp.bfloat16)


def features(alignment, ln_gain, ln_bias, w_left, b_left, w_right, b_right, row_count, col_count):
    seqs, width, channels = alignment.shape
    c = w_left.shape[1]
    rows = seqs * width * c // LANES
    chips = row_count // col_count
    shapes = [(rows, LANES)] + [(rows // chips, LANES)] * chips
    operands = (alignment, ln_gain.reshape(1, -1), ln_bias.reshape(1, -1), w_left.T, b_left.reshape(1, -1),
                w_right.T, b_right.reshape(1, -1))
    return pl.pallas_call(
        functools.partial(features_kernel, 1.0 / (seqs * row_count)),
        grid=(1,),
        out_shape=[jax.ShapeDtypeStruct(shape, jnp.bfloat16) for shape in shapes],
        in_specs=[whole(a.shape) for a in operands],
        out_specs=[whole(shape) for shape in shapes],
        scratch_shapes=[pltpu.VMEM((channels // LANES, seqs * width, LANES), jnp.float32),
                        pltpu.VMEM((rows, LANES), jnp.float32),
                        pltpu.VMEM((rows, LANES), jnp.float32)],
        compiler_params=pltpu.CompilerParams(vmem_limit_bytes=VMEM_LIMIT),
        name="features",
    )(*operands)


def sequence_rows(block, f32_ref, inner, seqs):
    sources = f32_ref.shape[0]
    for n in range(sources):
        f32_ref[n] = block(n)
    if seqs % 8 == 0:
        return lambda m: jnp.concatenate(
            [f32_ref[n, m * seqs:(m + 1) * seqs] for n in range(sources)], axis=0)
    flat = f32_ref.reshape(sources * inner * seqs, LANES)
    return lambda m: jnp.concatenate(
        [flat[pl.ds(m * seqs + s, sources, stride=inner * seqs), :] for s in range(seqs)], axis=0)


def prepare_kernel(seqs, c, mine_ref, other_ref, w_ref, bias_ref, own_right_ref,
                   left_ref, weights_ref, right_ref, bias_out_ref, left_f32, w_f32):
    sources, left_rows, _ = left_f32.shape
    chips = sources // 2
    same_half = lax.axis_index("row") // chips == lax.axis_index("col")

    def block(n):
        first = n % chips * left_rows
        mine = mine_ref[first:first + left_rows].astype(jnp.float32)
        other = other_ref[first:first + left_rows].astype(jnp.float32)
        return jnp.where(same_half == (n < chips), mine, other)

    left_of = sequence_rows(block, left_f32, left_rows // seqs, seqs)
    for k in range(left_rows // seqs):
        left_ref[k * LANES:(k + 1) * LANES] = left_of(k).T.astype(jnp.bfloat16)
    w_f32[...] = w_ref[...].astype(jnp.float32)
    for e in range(c):
        weights_ref[:, e * c:(e + 1) * c] = w_f32[pl.ds(e, c, stride=c), :].T.astype(jnp.bfloat16)
    right_ref[...] = own_right_ref[...]
    bias_out_ref[...] = bias_ref[...]


def prepare(mine, other, w_out, b_out, right, sources, seqs, c):
    left_rows = mine.shape[0] * 2 // sources
    z = w_out.shape[1]
    outs = [((left_rows // seqs * LANES, sources * seqs), jnp.bfloat16), ((z, w_out.shape[0]), jnp.bfloat16),
            (right.shape, jnp.bfloat16), ((1, z), jnp.float32)]
    operands = (mine, other, w_out, b_out.reshape(1, -1), right)
    return pl.pallas_call(
        functools.partial(prepare_kernel, seqs, c),
        grid=(1,),
        out_shape=[jax.ShapeDtypeStruct(*out) for out in outs],
        in_specs=[whole(a.shape) for a in operands],
        out_specs=[whole(out[0]) for out in outs],
        scratch_shapes=[pltpu.VMEM((sources, left_rows, LANES), jnp.float32), pltpu.VMEM(w_out.shape, jnp.float32)],
        compiler_params=pltpu.CompilerParams(vmem_limit_bytes=48 * 1024 * 1024),
        name="prepare",
    )(*operands)


def pair_kernel(seqs, c, sources, left_ref, weights_ref, bias_ref, *refs):
    right_refs, (out_ref, right_f32, right_b, outer_ref) = refs[:sources], refs[sources:]
    rows_step = out_ref.shape[0]
    blocks = out_ref.shape[1] // LANES

    @pl.when(pl.program_id(0) == 0)
    def _():
        for b in range(blocks):
            at = b * c * seqs
            right_of = sequence_rows(
                lambda n: right_refs[n][at:at + c * seqs].astype(jnp.float32), right_f32, c, seqs)
            for e in range(c):
                lanes = (b * c + e) * LANES
                right_b[:, lanes:lanes + LANES] = right_of(e).astype(jnp.bfloat16)

    for b in range(blocks):
        for e in range(0, c, 2):
            at = (b * c + e) * LANES
            outer = jnp.dot(left_ref[...], right_b[:, at:at + 2 * LANES], preferred_element_type=jnp.float32)
            outer = outer.astype(jnp.bfloat16)
            for half in range(2):
                for i in range(rows_step):
                    outer_ref[i // 2, (e + half) * c:(e + half + 1) * c,
                              (i % 2) * LANES:(i % 2 + 1) * LANES] = (
                        outer[i * c:(i + 1) * c, half * LANES:(half + 1) * LANES])
        for p in range(rows_step // 2):
            update = jnp.dot(weights_ref[...], outer_ref[p], preferred_element_type=jnp.float32)
            for half in range(2):
                mine = update[:, half * LANES:(half + 1) * LANES].T + bias_ref[...]
                out_ref[2 * p + half, b * LANES:(b + 1) * LANES, :] = mine.astype(out_ref.dtype)


def pairs(left, weights, bias, rights, seqs, c, width):
    sources = len(rights)
    z = weights.shape[0]
    rows = left.shape[0] // c
    rows_step = 8
    total = sources * seqs
    operands = (left, weights, bias, *rights)
    return pl.pallas_call(
        functools.partial(pair_kernel, seqs, c, sources),
        grid=(rows // rows_step,),
        out_shape=jax.ShapeDtypeStruct((rows, width, z), jnp.bfloat16),
        in_specs=[pl.BlockSpec((rows_step * c, total), lambda i: (i, 0))] + [whole(a.shape) for a in operands[1:]],
        out_specs=pl.BlockSpec((rows_step, width, z), lambda i: (i, 0, 0)),
        scratch_shapes=[pltpu.VMEM((sources, c * seqs, LANES), jnp.float32),
                        pltpu.VMEM((total, width * c), jnp.bfloat16),
                        pltpu.VMEM((rows_step // 2, c * c, 2 * LANES), jnp.bfloat16)],
        compiler_params=pltpu.CompilerParams(vmem_limit_bytes=32 * 1024 * 1024),
        cost_estimate=pl.CostEstimate(flops=2 * rows * c * width * c * (total + z),
                                      bytes_accessed=2 * rows * width * z, transcendentals=0),
        name="pairs",
    )(*operands)


def source_at(here, step):
    return here ^ (2 * step[0] + step[1])


def half_steps(chips):
    return [(a, b) for b in range(2) for a in range(chips // 2)]


def fetch(array, step, count):
    return lax.ppermute(array, "row", [(source_at(r, step), r) for r in range(count)])


def fetch_left(array, step, count):
    chips = count // 2
    moves = []
    for r in range(count):
        for core in range(2):
            to = source_at(r % chips, step) + core * chips
            moves.append((2 * r + core, 2 * to + (core if r // chips == core else 1 - core)))
    return lax.ppermute(array, ("row", "col"), moves)


def on_device(alignment, ln_gain, ln_bias, w_left, b_left, w_right, b_right, w_out, b_out):
    seqs, width, _ = alignment.shape
    c = w_left.shape[1]
    row_count = lax.axis_size("row")
    col_count = lax.axis_size("col")
    right, *lefts = features(alignment, ln_gain, ln_bias, w_left, b_left, w_right, b_right, row_count, col_count)
    chips = row_count // 2
    along = chips

    near = [right] + [fetch(right, (a, 0), row_count) for a in range(1, along)]
    far = [fetch(block, (0, 1), row_count) for block in near]
    mine = jnp.concatenate([fetch_left(left, step, row_count) for step, left in zip(half_steps(chips), lefts)])
    other = lax.ppermute(mine, "col", [(0, 1), (1, 0)])
    left, weights, near[0], bias = prepare(mine, other, w_out, b_out, right, row_count, seqs, c)
    rights = [(near, far)[b][half * (along // 2) + a] for half in range(2) for a, b in half_steps(chips)]
    return pairs(left, weights, bias, rights, seqs, c, width)


def solution(mesh):
    in_specs = (P(("group", "row"), "col", None), P(), P(), P(), P(), P(), P(), P(), P())
    out_specs = P(("group", "row"), "col", None)
    return jax.shard_map(
        on_device, mesh=mesh, in_specs=in_specs, out_specs=out_specs, check_vma=False
    )
```

```python
import functools

import jax
import jax.numpy as jnp
from jax import lax
from jax.experimental import pallas as pl
from jax.experimental.pallas import tpu as pltpu
from jax.sharding import PartitionSpec as P

LANES = 128
VMEM_LIMIT = 60 * 1024 * 1024


def whole(shape):
    return pl.BlockSpec(shape, lambda i: (0,) * len(shape))


def features_kernel(scale, x_ref, gain_ref, bias_ref, wl_ref, bl_ref, wr_ref, br_ref,
                    left_ref, right_ref, normed_ref, left_f32, right_f32):
    seqs, width, channels = x_ref.shape
    c = wl_ref.shape[0]
    blocks = width // LANES
    fold = LANES // c
    quarter = width // fold
    right_bias = jnp.broadcast_to(br_ref[...], (LANES, c)).T[:, :1]
    for s in range(seqs):
        values = x_ref[s].astype(jnp.float32)
        average = jnp.mean(values, axis=-1, keepdims=True)
        centred = values - average
        variance = jnp.mean(centred * centred, axis=-1, keepdims=True)
        normed = centred * lax.rsqrt(variance + 1e-05) * gain_ref[...] + bias_ref[...]
        for h in range(channels // LANES):
            normed_ref[h, s * width:(s + 1) * width] = normed[:, h * LANES:(h + 1) * LANES]
        right = lax.dot_general(wr_ref[...], normed.astype(jnp.bfloat16), (((1,), (1,)), ((), ())),
                                preferred_element_type=jnp.float32) + right_bias
        for b in range(blocks):
            right_f32[pl.ds(b * c * seqs + s, c, stride=seqs), :] = right[:, b * LANES:(b + 1) * LANES]
    total = None
    for q in range(fold):
        rows = jnp.concatenate(
            [normed_ref[h, pl.ds(q, seqs * quarter, stride=fold), :] for h in range(channels // LANES)], axis=1
        ).astype(jnp.bfloat16)
        zeros = [jnp.zeros((c, channels), jnp.bfloat16)]
        w = jnp.concatenate(zeros * q + [wl_ref[...]] + zeros * (fold - 1 - q), axis=0)
        term = lax.dot_general(rows, w, (((1,), (1,)), ((), ())), preferred_element_type=jnp.float32)
        total = term if total is None else total + term
    total = (total + jnp.concatenate([bl_ref[...]] * fold, axis=1)) * scale
    for s in range(seqs):
        left_f32[pl.ds(s, quarter, stride=seqs), :] = total[s * quarter:(s + 1) * quarter]
    left = left_f32[...].astype(jnp.bfloat16)
    for copy in range(left_ref.shape[0]):
        left_ref[copy] = left
    right_ref[...] = right_f32[...].astype(jnp.bfloat16)


def features(alignment, ln_gain, ln_bias, w_left, b_left, w_right, b_right, row_count, col_count):
    seqs, width, channels = alignment.shape
    c = w_left.shape[1]
    rows = seqs * width * c // LANES
    shapes = ((col_count, rows, LANES), (rows, LANES))
    operands = (alignment, ln_gain.reshape(1, -1), ln_bias.reshape(1, -1), w_left.T, b_left.reshape(1, -1),
                w_right.T, b_right.reshape(1, -1))
    return pl.pallas_call(
        functools.partial(features_kernel, 1.0 / (seqs * row_count)),
        grid=(1,),
        out_shape=[jax.ShapeDtypeStruct(shape, jnp.bfloat16) for shape in shapes],
        in_specs=[whole(a.shape) for a in operands],
        out_specs=[whole(shape) for shape in shapes],
        scratch_shapes=[pltpu.VMEM((channels // LANES, seqs * width, LANES), jnp.float32),
                        pltpu.VMEM((rows, LANES), jnp.float32),
                        pltpu.VMEM((rows, LANES), jnp.float32)],
        compiler_params=pltpu.CompilerParams(vmem_limit_bytes=VMEM_LIMIT),
        name="features",
    )(*operands)


def sequence_rows(block, f32_ref, inner, seqs):
    sources = f32_ref.shape[0]
    for n in range(sources):
        f32_ref[n] = block(n)
    if seqs % 8 == 0:
        return lambda m: jnp.concatenate(
            [f32_ref[n, m * seqs:(m + 1) * seqs] for n in range(sources)], axis=0)
    flat = f32_ref.reshape(sources * inner * seqs, LANES)
    return lambda m: jnp.concatenate(
        [flat[pl.ds(m * seqs + s, sources, stride=inner * seqs), :] for s in range(seqs)], axis=0)


def prepare_kernel(seqs, c, steps, mine_ref, other_ref, w_ref, bias_ref, own_right_ref,
                   left_ref, weights_ref, right_ref, bias_out_ref, left_f32, w_f32):
    sources, left_rows, _ = left_f32.shape
    here = lax.axis_index("row")
    same_half = here // (sources // 2) == lax.axis_index("col")

    def block(n):
        source = source_at(here, steps[n])
        return jnp.where(same_half, mine_ref[source].astype(jnp.float32), other_ref[source].astype(jnp.float32))

    left_of = sequence_rows(block, left_f32, left_rows // seqs, seqs)
    for k in range(left_rows // seqs):
        left_ref[k * LANES:(k + 1) * LANES] = left_of(k).T.astype(jnp.bfloat16)
    w_f32[...] = w_ref[...].astype(jnp.float32)
    for e in range(c):
        weights_ref[:, e * c:(e + 1) * c] = w_f32[pl.ds(e, c, stride=c), :].T.astype(jnp.bfloat16)
    right_ref[...] = own_right_ref[...]
    bias_out_ref[...] = bias_ref[...]


def prepare(mine, other, w_out, b_out, right, steps, seqs, c):
    sources, left_rows, _ = mine.shape
    z = w_out.shape[1]
    outs = [((left_rows // seqs * LANES, sources * seqs), jnp.bfloat16), ((z, w_out.shape[0]), jnp.bfloat16),
            (right.shape, jnp.bfloat16), ((1, z), jnp.float32)]
    operands = (mine, other, w_out, b_out.reshape(1, -1), right)
    return pl.pallas_call(
        functools.partial(prepare_kernel, seqs, c, steps),
        grid=(1,),
        out_shape=[jax.ShapeDtypeStruct(*out) for out in outs],
        in_specs=[whole(a.shape) for a in operands],
        out_specs=[whole(out[0]) for out in outs],
        scratch_shapes=[pltpu.VMEM((sources, left_rows, LANES), jnp.float32), pltpu.VMEM(w_out.shape, jnp.float32)],
        compiler_params=pltpu.CompilerParams(vmem_limit_bytes=48 * 1024 * 1024),
        name="prepare",
    )(*operands)


def pair_kernel(seqs, c, right_at, left_ref, weights_ref, bias_ref, *refs):
    right_refs, (out_ref, right_f32, right_b, outer_ref) = refs[:-4], refs[-4:]
    rows_step = out_ref.shape[0]
    blocks = out_ref.shape[1] // LANES

    def block_of(n, at):
        array, first = right_at[n]
        return right_refs[array][first + at:first + at + c * seqs].astype(jnp.float32)

    @pl.when(pl.program_id(0) == 0)
    def _():
        for b in range(blocks):
            at = b * c * seqs
            right_of = sequence_rows(
                lambda n: block_of(n, at), right_f32, c, seqs)
            for e in range(c):
                lanes = (b * c + e) * LANES
                right_b[:, lanes:lanes + LANES] = right_of(e).astype(jnp.bfloat16)

    for b in range(blocks):
        for e in range(0, c, 2):
            at = (b * c + e) * LANES
            outer = jnp.dot(left_ref[...], right_b[:, at:at + 2 * LANES], preferred_element_type=jnp.float32)
            outer = outer.astype(jnp.bfloat16)
            for half in range(2):
                for i in range(rows_step):
                    outer_ref[i // 2, (e + half) * c:(e + half + 1) * c,
                              (i % 2) * LANES:(i % 2 + 1) * LANES] = (
                        outer[i * c:(i + 1) * c, half * LANES:(half + 1) * LANES])
        for p in range(rows_step // 2):
            update = jnp.dot(weights_ref[...], outer_ref[p], preferred_element_type=jnp.float32)
            for half in range(2):
                mine = update[:, half * LANES:(half + 1) * LANES].T + bias_ref[...]
                out_ref[2 * p + half, b * LANES:(b + 1) * LANES, :] = mine.astype(out_ref.dtype)


def pairs(left, weights, bias, rights, right_at, seqs, c, width):
    sources = len(right_at)
    z = weights.shape[0]
    rows = left.shape[0] // c
    rows_step = 8
    total = sources * seqs
    operands = (left, weights, bias, *rights)
    return pl.pallas_call(
        functools.partial(pair_kernel, seqs, c, right_at),
        grid=(rows // rows_step,),
        out_shape=jax.ShapeDtypeStruct((rows, width, z), jnp.bfloat16),
        in_specs=[pl.BlockSpec((rows_step * c, total), lambda i: (i, 0))] + [whole(a.shape) for a in operands[1:]],
        out_specs=pl.BlockSpec((rows_step, width, z), lambda i: (i, 0, 0)),
        scratch_shapes=[pltpu.VMEM((sources, c * seqs, LANES), jnp.float32),
                        pltpu.VMEM((total, width * c), jnp.bfloat16),
                        pltpu.VMEM((rows_step // 2, c * c, 2 * LANES), jnp.bfloat16)],
        compiler_params=pltpu.CompilerParams(vmem_limit_bytes=32 * 1024 * 1024),
        cost_estimate=pl.CostEstimate(flops=2 * rows * c * width * c * (total + z),
                                      bytes_accessed=2 * rows * width * z, transcendentals=0),
        name="pairs",
    )(*operands)


def source_at(here, step):
    return here ^ (2 * step[0] + step[1])


def fetch(array, step, count):
    return lax.ppermute(array, "row", [(source_at(r, step), r) for r in range(count)])


def on_device(alignment, ln_gain, ln_bias, w_left, b_left, w_right, b_right, w_out, b_out):
    seqs, width, _ = alignment.shape
    c = w_left.shape[1]
    row_count = lax.axis_size("row")
    col_count = lax.axis_size("col")
    left, right = features(alignment, ln_gain, ln_bias, w_left, b_left, w_right, b_right, row_count, col_count)
    along = row_count // 2
    rows = right.shape[0]

    across = fetch(right, (0, 1), row_count)
    line = [fetch(right, (a, 0), row_count) for a in reversed(range(1, along))][::-1]

    left, line[0] = lax.optimization_barrier((left, line[0]))
    mine = lax.all_to_all(left.reshape(row_count, -1, LANES), "row", split_axis=0, concat_axis=0, tiled=True)
    mine, across, *line = lax.optimization_barrier((mine, across, *line))
    far = fetch(jnp.concatenate(line), (0, 1), row_count)
    other = lax.ppermute(mine, "col", [(0, 1), (1, 0)])

    steps = [(a, b) for b in range(2) for a in range(along)]
    right_at = [(a, 0) for a in range(along)] + [(along, 0)] + [(along + 1, a * rows) for a in range(along - 1)]
    left, weights, right, bias = prepare(mine, other, w_out, b_out, right, steps, seqs, c)
    return pairs(left, weights, bias, [right, *line, across, far], right_at, seqs, c, width)


def solution(mesh):
    in_specs = (P(("group", "row"), "col", None), P(), P(), P(), P(), P(), P(), P(), P())
    out_specs = P(("group", "row"), "col", None)
    return jax.shard_map(
        on_device, mesh=mesh, in_specs=in_specs, out_specs=out_specs, check_vma=False
    )
```

```python
import functools

import jax
import jax.numpy as jnp
from jax import lax
from jax.experimental import pallas as pl
from jax.experimental.pallas import tpu as pltpu
from jax.sharding import PartitionSpec as P

LANES = 128
VMEM_LIMIT = 60 * 1024 * 1024


def whole(shape):
    return pl.BlockSpec(shape, lambda i: (0,) * len(shape))


def features_kernel(scale, x_ref, gain_ref, bias_ref, wl_ref, bl_ref, wr_ref, br_ref,
                    *refs):
    outs, (normed_ref, left_f32, right_f32) = refs[:-3], refs[-3:]
    seqs, width, channels = x_ref.shape
    c = wl_ref.shape[0]
    blocks = width // LANES
    fold = LANES // c
    quarter = width // fold
    right_bias = jnp.broadcast_to(br_ref[...], (LANES, c)).T[:, :1]
    for s in range(seqs):
        values = x_ref[s].astype(jnp.float32)
        average = jnp.mean(values, axis=-1, keepdims=True)
        centred = values - average
        variance = jnp.mean(centred * centred, axis=-1, keepdims=True)
        normed = centred * lax.rsqrt(variance + 1e-05) * gain_ref[...] + bias_ref[...]
        for h in range(channels // LANES):
            normed_ref[h, s * width:(s + 1) * width] = normed[:, h * LANES:(h + 1) * LANES]
        right = lax.dot_general(wr_ref[...], normed.astype(jnp.bfloat16), (((1,), (1,)), ((), ())),
                                preferred_element_type=jnp.float32) + right_bias
        for b in range(blocks):
            right_f32[pl.ds(b * c * seqs + s, c, stride=seqs), :] = right[:, b * LANES:(b + 1) * LANES]
    total = None
    for q in range(fold):
        rows = jnp.concatenate(
            [normed_ref[h, pl.ds(q, seqs * quarter, stride=fold), :] for h in range(channels // LANES)], axis=1
        ).astype(jnp.bfloat16)
        zeros = [jnp.zeros((c, channels), jnp.bfloat16)]
        w = jnp.concatenate(zeros * q + [wl_ref[...]] + zeros * (fold - 1 - q), axis=0)
        term = lax.dot_general(rows, w, (((1,), (1,)), ((), ())), preferred_element_type=jnp.float32)
        total = term if total is None else total + term
    total = (total + jnp.concatenate([bl_ref[...]] * fold, axis=1)) * scale
    for s in range(seqs):
        left_f32[pl.ds(s, quarter, stride=seqs), :] = total[s * quarter:(s + 1) * quarter]
    right_ref, *left_refs = outs
    here = lax.axis_index("row")
    for step, left_ref in zip(half_steps(len(left_refs)), left_refs):
        rows = left_ref.shape[0]
        block = source_at(here, step) % len(left_refs)
        left_ref[...] = left_f32[pl.ds(pl.multiple_of(block * rows, rows), rows), :].astype(jnp.bfloat16)
    right_ref[...] = right_f32[...].astype(jnp.bfloat16)


def features(alignment, ln_gain, ln_bias, w_left, b_left, w_right, b_right, row_count, col_count):
    seqs, width, channels = alignment.shape
    c = w_left.shape[1]
    rows = seqs * width * c // LANES
    chips = row_count // col_count
    shapes = [(rows, LANES)] + [(rows // chips, LANES)] * chips
    operands = (alignment, ln_gain.reshape(1, -1), ln_bias.reshape(1, -1), w_left.T, b_left.reshape(1, -1),
                w_right.T, b_right.reshape(1, -1))
    return pl.pallas_call(
        functools.partial(features_kernel, 1.0 / (seqs * row_count)),
        grid=(1,),
        out_shape=[jax.ShapeDtypeStruct(shape, jnp.bfloat16) for shape in shapes],
        in_specs=[whole(a.shape) for a in operands],
        out_specs=[whole(shape) for shape in shapes],
        scratch_shapes=[pltpu.VMEM((channels // LANES, seqs * width, LANES), jnp.float32),
                        pltpu.VMEM((rows, LANES), jnp.float32),
                        pltpu.VMEM((rows, LANES), jnp.float32)],
        compiler_params=pltpu.CompilerParams(vmem_limit_bytes=VMEM_LIMIT),
        name="features",
    )(*operands)


def sequence_rows(block, f32_ref, inner, seqs):
    sources = f32_ref.shape[0]
    for n in range(sources):
        f32_ref[n] = block(n)
    if seqs % 8 == 0:
        return lambda m: jnp.concatenate(
            [f32_ref[n, m * seqs:(m + 1) * seqs] for n in range(sources)], axis=0)
    flat = f32_ref.reshape(sources * inner * seqs, LANES)
    return lambda m: jnp.concatenate(
        [flat[pl.ds(m * seqs + s, sources, stride=inner * seqs), :] for s in range(seqs)], axis=0)


def prepare_kernel(seqs, c, mine_ref, other_ref, w_ref, bias_ref, own_right_ref,
                   left_ref, weights_ref, right_ref, bias_out_ref, left_f32, w_f32):
    sources, left_rows, _ = left_f32.shape
    chips = sources // 2
    same_half = lax.axis_index("row") // chips == lax.axis_index("col")

    def block(n):
        first = n % chips * left_rows
        mine = mine_ref[first:first + left_rows].astype(jnp.float32)
        other = other_ref[first:first + left_rows].astype(jnp.float32)
        return jnp.where(same_half == (n < chips), mine, other)

    left_of = sequence_rows(block, left_f32, left_rows // seqs, seqs)
    for k in range(left_rows // seqs):
        left_ref[k * LANES:(k + 1) * LANES] = left_of(k).T.astype(jnp.bfloat16)
    w_f32[...] = w_ref[...].astype(jnp.float32)
    for e in range(c):
        weights_ref[:, e * c:(e + 1) * c] = w_f32[pl.ds(e, c, stride=c), :].T.astype(jnp.bfloat16)
    right_ref[...] = own_right_ref[...]
    bias_out_ref[...] = bias_ref[...]


def prepare(mine, other, w_out, b_out, right, sources, seqs, c):
    left_rows = mine.shape[0] * 2 // sources
    z = w_out.shape[1]
    outs = [((left_rows // seqs * LANES, sources * seqs), jnp.bfloat16), ((z, w_out.shape[0]), jnp.bfloat16),
            (right.shape, jnp.bfloat16), ((1, z), jnp.float32)]
    operands = (mine, other, w_out, b_out.reshape(1, -1), right)
    return pl.pallas_call(
        functools.partial(prepare_kernel, seqs, c),
        grid=(1,),
        out_shape=[jax.ShapeDtypeStruct(*out) for out in outs],
        in_specs=[whole(a.shape) for a in operands],
        out_specs=[whole(out[0]) for out in outs],
        scratch_shapes=[pltpu.VMEM((sources, left_rows, LANES), jnp.float32), pltpu.VMEM(w_out.shape, jnp.float32)],
        compiler_params=pltpu.CompilerParams(vmem_limit_bytes=48 * 1024 * 1024),
        name="prepare",
    )(*operands)


def pair_kernel(seqs, c, right_at, left_ref, weights_ref, bias_ref, *refs):
    right_refs, (out_ref, right_f32, right_b, outer_ref) = refs[:-4], refs[-4:]
    rows_step = out_ref.shape[0]
    blocks = out_ref.shape[1] // LANES

    def block_of(n, at):
        array, first = right_at[n]
        return right_refs[array][first + at:first + at + c * seqs].astype(jnp.float32)

    @pl.when(pl.program_id(0) == 0)
    def _():
        for b in range(blocks):
            at = b * c * seqs
            right_of = sequence_rows(
                lambda n: block_of(n, at), right_f32, c, seqs)
            for e in range(c):
                lanes = (b * c + e) * LANES
                right_b[:, lanes:lanes + LANES] = right_of(e).astype(jnp.bfloat16)

    for b in range(blocks):
        for e in range(0, c, 2):
            at = (b * c + e) * LANES
            outer = jnp.dot(left_ref[...], right_b[:, at:at + 2 * LANES], preferred_element_type=jnp.float32)
            outer = outer.astype(jnp.bfloat16)
            for half in range(2):
                for i in range(rows_step):
                    outer_ref[i // 2, (e + half) * c:(e + half + 1) * c,
                              (i % 2) * LANES:(i % 2 + 1) * LANES] = (
                        outer[i * c:(i + 1) * c, half * LANES:(half + 1) * LANES])
        for p in range(rows_step // 2):
            update = jnp.dot(weights_ref[...], outer_ref[p], preferred_element_type=jnp.float32)
            for half in range(2):
                mine = update[:, half * LANES:(half + 1) * LANES].T + bias_ref[...]
                out_ref[2 * p + half, b * LANES:(b + 1) * LANES, :] = mine.astype(out_ref.dtype)


def pairs(left, weights, bias, rights, right_at, seqs, c, width):
    sources = len(right_at)
    z = weights.shape[0]
    rows = left.shape[0] // c
    rows_step = 8
    total = sources * seqs
    operands = (left, weights, bias, *rights)
    return pl.pallas_call(
        functools.partial(pair_kernel, seqs, c, right_at),
        grid=(rows // rows_step,),
        out_shape=jax.ShapeDtypeStruct((rows, width, z), jnp.bfloat16),
        in_specs=[pl.BlockSpec((rows_step * c, total), lambda i: (i, 0))] + [whole(a.shape) for a in operands[1:]],
        out_specs=pl.BlockSpec((rows_step, width, z), lambda i: (i, 0, 0)),
        scratch_shapes=[pltpu.VMEM((sources, c * seqs, LANES), jnp.float32),
                        pltpu.VMEM((total, width * c), jnp.bfloat16),
                        pltpu.VMEM((rows_step // 2, c * c, 2 * LANES), jnp.bfloat16)],
        compiler_params=pltpu.CompilerParams(vmem_limit_bytes=32 * 1024 * 1024),
        cost_estimate=pl.CostEstimate(flops=2 * rows * c * width * c * (total + z),
                                      bytes_accessed=2 * rows * width * z, transcendentals=0),
        name="pairs",
    )(*operands)


def source_at(here, step):
    return here ^ (2 * step[0] + step[1])


def half_steps(chips):
    return [(a, b) for b in range(2) for a in range(chips // 2)]


def fetch(array, step, count):
    return lax.ppermute(array, "row", [(source_at(r, step), r) for r in range(count)])


def fetch_left(array, step, count):
    chips = count // 2
    moves = []
    for r in range(count):
        for core in range(2):
            to = source_at(r % chips, step) + core * chips
            moves.append((2 * r + core, 2 * to + (core if r // chips == core else 1 - core)))
    return lax.ppermute(array, ("row", "col"), moves)


def on_device(alignment, ln_gain, ln_bias, w_left, b_left, w_right, b_right, w_out, b_out):
    seqs, width, _ = alignment.shape
    c = w_left.shape[1]
    row_count = lax.axis_size("row")
    col_count = lax.axis_size("col")
    right, *lefts = features(alignment, ln_gain, ln_bias, w_left, b_left, w_right, b_right, row_count, col_count)
    chips = along = row_count // 2
    rows = right.shape[0]

    line = [fetch(right, (a, 0), row_count) for a in range(1, along)]
    across = fetch(right, (0, 1), row_count)
    across, *held = lax.optimization_barrier((across, *line, *lefts[1:]))
    line, lefts[1:] = held[:along - 1], held[along - 1:]
    far = fetch(jnp.concatenate(line), (0, 1), row_count)

    mine = jnp.concatenate([fetch_left(left, step, row_count) for step, left in zip(half_steps(chips), lefts)])
    other = lax.ppermute(mine, "col", [(0, 1), (1, 0)])
    left, weights, right, bias = prepare(mine, other, w_out, b_out, right, row_count, seqs, c)
    places = [[(a, 0) for a in range(along)], [(along, 0)] + [(along + 1, a * rows) for a in range(along - 1)]]
    right_at = [places[b][half * (along // 2) + a] for half in range(2) for a, b in half_steps(chips)]
    return pairs(left, weights, bias, [right, *line, across, far], right_at, seqs, c, width)


def solution(mesh):
    in_specs = (P(("group", "row"), "col", None), P(), P(), P(), P(), P(), P(), P(), P())
    out_specs = P(("group", "row"), "col", None)
    return jax.shard_map(
        on_device, mesh=mesh, in_specs=in_specs, out_specs=out_specs, check_vma=False
    )
```

```python
import functools

import jax
import jax.numpy as jnp
from jax import lax
from jax.experimental import pallas as pl
from jax.experimental.pallas import tpu as pltpu
from jax.sharding import PartitionSpec as P

LANES = 128
VMEM_LIMIT = 60 * 1024 * 1024


def whole(shape):
    return pl.BlockSpec(shape, lambda i: (0,) * len(shape))


def features_kernel(scale, x_ref, gain_ref, bias_ref, wl_ref, bl_ref, wr_ref, br_ref,
                    *refs):
    outs, (normed_ref, left_f32, right_f32) = refs[:-3], refs[-3:]
    seqs, width, channels = x_ref.shape
    c = wl_ref.shape[0]
    blocks = width // LANES
    fold = LANES // c
    quarter = width // fold
    right_bias = jnp.broadcast_to(br_ref[...], (LANES, c)).T[:, :1]
    for s in range(seqs):
        values = x_ref[s].astype(jnp.float32)
        average = jnp.mean(values, axis=-1, keepdims=True)
        centred = values - average
        variance = jnp.mean(centred * centred, axis=-1, keepdims=True)
        normed = centred * lax.rsqrt(variance + 1e-05) * gain_ref[...] + bias_ref[...]
        for h in range(channels // LANES):
            normed_ref[h, s * width:(s + 1) * width] = normed[:, h * LANES:(h + 1) * LANES]
        right = lax.dot_general(wr_ref[...], normed.astype(jnp.bfloat16), (((1,), (1,)), ((), ())),
                                preferred_element_type=jnp.float32) + right_bias
        for b in range(blocks):
            right_f32[pl.ds(b * c * seqs + s, c, stride=seqs), :] = right[:, b * LANES:(b + 1) * LANES]
    total = None
    for q in range(fold):
        rows = jnp.concatenate(
            [normed_ref[h, pl.ds(q, seqs * quarter, stride=fold), :] for h in range(channels // LANES)], axis=1
        ).astype(jnp.bfloat16)
        zeros = [jnp.zeros((c, channels), jnp.bfloat16)]
        w = jnp.concatenate(zeros * q + [wl_ref[...]] + zeros * (fold - 1 - q), axis=0)
        term = lax.dot_general(rows, w, (((1,), (1,)), ((), ())), preferred_element_type=jnp.float32)
        total = term if total is None else total + term
    total = (total + jnp.concatenate([bl_ref[...]] * fold, axis=1)) * scale
    for s in range(seqs):
        left_f32[pl.ds(s, quarter, stride=seqs), :] = total[s * quarter:(s + 1) * quarter]
    own_ref, *message_refs = outs
    here = lax.axis_index("row")
    rows = own_ref.shape[0]
    chips = left_f32.shape[0] // rows

    def left_for(step):
        block = source_at(here, step) % chips
        return left_f32[pl.ds(pl.multiple_of(block * rows, rows), rows), :].astype(jnp.bfloat16)

    own_ref[...] = left_for((0, 0))
    right = right_f32[...].astype(jnp.bfloat16)
    for step, message_ref in zip(direct_steps(chips), message_refs):
        message_ref[:right.shape[0]] = right
        message_ref[right.shape[0]:] = left_for(step)
    same_half = here // chips == lax.axis_index("col")
    for (a, b), message_ref in zip(far_steps(chips), message_refs[chips:]):
        message_ref[...] = jnp.where(same_half, left_for((a + 1, b)), left_for((a, b)))


def features(alignment, ln_gain, ln_bias, w_left, b_left, w_right, b_right, row_count, col_count):
    seqs, width, channels = alignment.shape
    c = w_left.shape[1]
    rows = seqs * width * c // LANES
    chips = row_count // col_count
    part = rows // chips
    shapes = [(n, LANES) for n in [part] + [rows + part] * chips + [part] * (chips // 2)]
    operands = (alignment, ln_gain.reshape(1, -1), ln_bias.reshape(1, -1), w_left.T, b_left.reshape(1, -1),
                w_right.T, b_right.reshape(1, -1))
    return pl.pallas_call(
        functools.partial(features_kernel, 1.0 / (seqs * row_count)),
        grid=(1,),
        out_shape=[jax.ShapeDtypeStruct(shape, jnp.bfloat16) for shape in shapes],
        in_specs=[whole(a.shape) for a in operands],
        out_specs=[whole(shape) for shape in shapes],
        scratch_shapes=[pltpu.VMEM((channels // LANES, seqs * width, LANES), jnp.float32),
                        pltpu.VMEM((rows, LANES), jnp.float32),
                        pltpu.VMEM((rows, LANES), jnp.float32)],
        compiler_params=pltpu.CompilerParams(vmem_limit_bytes=VMEM_LIMIT),
        name="features",
    )(*operands)


def sequence_rows(block, f32_ref, inner, seqs):
    sources = f32_ref.shape[0]
    for n in range(sources):
        f32_ref[n] = block(n)
    if seqs % 8 == 0:
        return lambda m: jnp.concatenate(
            [f32_ref[n, m * seqs:(m + 1) * seqs] for n in range(sources)], axis=0)
    flat = f32_ref.reshape(sources * inner * seqs, LANES)
    return lambda m: jnp.concatenate(
        [flat[pl.ds(m * seqs + s, sources, stride=inner * seqs), :] for s in range(seqs)], axis=0)


def prepare_kernel(seqs, c, left_at, mine_ref, other_ref, w_ref, bias_ref, own_right_ref,
                   left_ref, weights_ref, right_ref, bias_out_ref, left_f32, w_f32):
    sources, left_rows, _ = left_f32.shape
    same_half = lax.axis_index("row") // (sources // 2) == lax.axis_index("col")

    def block(n):
        first, of_same_half = left_at[n][0] * left_rows, left_at[n][1]
        mine = mine_ref[first:first + left_rows].astype(jnp.float32)
        other = other_ref[first:first + left_rows].astype(jnp.float32)
        return jnp.where(same_half == of_same_half, mine, other)

    left_of = sequence_rows(block, left_f32, left_rows // seqs, seqs)
    for k in range(left_rows // seqs):
        left_ref[k * LANES:(k + 1) * LANES] = left_of(k).T.astype(jnp.bfloat16)
    w_f32[...] = w_ref[...].astype(jnp.float32)
    for e in range(c):
        weights_ref[:, e * c:(e + 1) * c] = w_f32[pl.ds(e, c, stride=c), :].T.astype(jnp.bfloat16)
    right_ref[...] = own_right_ref[:right_ref.shape[0]]
    bias_out_ref[...] = bias_ref[...]


def prepare(mine, other, left_at, left_rows, w_out, b_out, right, seqs, c):
    sources = len(left_at)
    z = w_out.shape[1]
    outs = [((left_rows // seqs * LANES, sources * seqs), jnp.bfloat16), ((z, w_out.shape[0]), jnp.bfloat16),
            ((right.shape[0] - left_rows, LANES), jnp.bfloat16), ((1, z), jnp.float32)]
    operands = (mine, other, w_out, b_out.reshape(1, -1), right)
    return pl.pallas_call(
        functools.partial(prepare_kernel, seqs, c, left_at),
        grid=(1,),
        out_shape=[jax.ShapeDtypeStruct(*out) for out in outs],
        in_specs=[whole(a.shape) for a in operands],
        out_specs=[whole(out[0]) for out in outs],
        scratch_shapes=[pltpu.VMEM((sources, left_rows, LANES), jnp.float32), pltpu.VMEM(w_out.shape, jnp.float32)],
        compiler_params=pltpu.CompilerParams(vmem_limit_bytes=48 * 1024 * 1024),
        name="prepare",
    )(*operands)


def pair_kernel(seqs, c, right_at, left_ref, weights_ref, bias_ref, *refs):
    right_refs, (out_ref, right_f32, right_b, outer_ref) = refs[:-4], refs[-4:]
    rows_step = out_ref.shape[0]
    blocks = out_ref.shape[1] // LANES

    def block_of(n, at):
        array, first = right_at[n]
        return right_refs[array][first + at:first + at + c * seqs].astype(jnp.float32)

    @pl.when(pl.program_id(0) == 0)
    def _():
        for b in range(blocks):
            at = b * c * seqs
            right_of = sequence_rows(
                lambda n: block_of(n, at), right_f32, c, seqs)
            for e in range(c):
                lanes = (b * c + e) * LANES
                right_b[:, lanes:lanes + LANES] = right_of(e).astype(jnp.bfloat16)

    for b in range(blocks):
        for e in range(0, c, 2):
            at = (b * c + e) * LANES
            outer = jnp.dot(left_ref[...], right_b[:, at:at + 2 * LANES], preferred_element_type=jnp.float32)
            outer = outer.astype(jnp.bfloat16)
            for half in range(2):
                for i in range(rows_step):
                    outer_ref[i // 2, (e + half) * c:(e + half + 1) * c,
                              (i % 2) * LANES:(i % 2 + 1) * LANES] = (
                        outer[i * c:(i + 1) * c, half * LANES:(half + 1) * LANES])
        for p in range(rows_step // 2):
            update = jnp.dot(weights_ref[...], outer_ref[p], preferred_element_type=jnp.float32)
            for half in range(2):
                mine = update[:, half * LANES:(half + 1) * LANES].T + bias_ref[...]
                out_ref[2 * p + half, b * LANES:(b + 1) * LANES, :] = mine.astype(out_ref.dtype)


def pairs(left, weights, bias, rights, right_at, seqs, c, width):
    sources = len(right_at)
    z = weights.shape[0]
    rows = left.shape[0] // c
    rows_step = 8
    total = sources * seqs
    operands = (left, weights, bias, *rights)
    return pl.pallas_call(
        functools.partial(pair_kernel, seqs, c, right_at),
        grid=(rows // rows_step,),
        out_shape=jax.ShapeDtypeStruct((rows, width, z), jnp.bfloat16),
        in_specs=[pl.BlockSpec((rows_step * c, total), lambda i: (i, 0))] + [whole(a.shape) for a in operands[1:]],
        out_specs=pl.BlockSpec((rows_step, width, z), lambda i: (i, 0, 0)),
        scratch_shapes=[pltpu.VMEM((sources, c * seqs, LANES), jnp.float32),
                        pltpu.VMEM((total, width * c), jnp.bfloat16),
                        pltpu.VMEM((rows_step // 2, c * c, 2 * LANES), jnp.bfloat16)],
        compiler_params=pltpu.CompilerParams(vmem_limit_bytes=32 * 1024 * 1024),
        cost_estimate=pl.CostEstimate(flops=2 * rows * c * width * c * (total + z),
                                      bytes_accessed=2 * rows * width * z, transcendentals=0),
        name="pairs",
    )(*operands)


def source_at(here, step):
    return here ^ (2 * step[0] + step[1])


def direct_steps(chips):
    return [(a, 0) for a in range(1, chips)] + [(0, 1)]


def far_steps(chips):
    return [(a, 1) for a in range(chips // 2)]


def fetch(array, step, count):
    return lax.ppermute(array, "row", [(source_at(r, step), r) for r in range(count)])


def fetch_far(array, step, count):
    chips = count // 2
    a, b = step
    moves = []
    for r in range(count):
        half = r // chips
        if a + 1 < chips // 2:
            moves.append((2 * source_at(r, (a + 1, b)) + half, 2 * r + half))
        moves.append((2 * source_at(r, (a + chips // 2, b)) + half, 2 * r + 1 - half))
    return lax.ppermute(array, ("row", "col"), moves)


def on_device(alignment, ln_gain, ln_bias, w_left, b_left, w_right, b_right, w_out, b_out):
    seqs, width, _ = alignment.shape
    c = w_left.shape[1]
    row_count = lax.axis_size("row")
    col_count = lax.axis_size("col")
    own, *messages = features(alignment, ln_gain, ln_bias, w_left, b_left, w_right, b_right, row_count, col_count)
    along = row_count // 2
    direct = messages[:along]
    left_rows = own.shape[0]
    rows = direct[0].shape[0] - left_rows

    *line, across = [fetch(message, step, row_count) for step, message in zip(direct_steps(along), direct)]
    beyond = [fetch_far(message, step, row_count) for step, message in zip(far_steps(along), messages[along:])]
    across, *line = lax.optimization_barrier((across, *line))
    far = fetch(jnp.concatenate([block[:rows] for block in line]), (0, 1), row_count)

    mine = jnp.concatenate([own] + [block[rows:] for block in (*line, across)] + beyond)
    other = lax.ppermute(mine, "col", [(0, 1), (1, 0)])
    left_at = [(a, True) for a in range(along + 1)]
    left_at += [(along + a, True) if a < along // 2 else (a + 1 + along // 2, False) for a in range(1, along)]
    left, weights, right, bias = prepare(mine, other, left_at, left_rows, w_out, b_out, direct[0], seqs, c)
    right_at = [(a, 0) for a in range(along + 1)] + [(along + 1, a * rows) for a in range(along - 1)]
    return pairs(left, weights, bias, [right, *line, across, far], right_at, seqs, c, width)


def solution(mesh):
    in_specs = (P(("group", "row"), "col", None), P(), P(), P(), P(), P(), P(), P(), P())
    out_specs = P(("group", "row"), "col", None)
    return jax.shard_map(
        on_device, mesh=mesh, in_specs=in_specs, out_specs=out_specs, check_vma=False
    )
```

```python
import functools

import jax
import jax.numpy as jnp
from jax import lax
from jax.experimental import pallas as pl
from jax.experimental.pallas import tpu as pltpu
from jax.sharding import PartitionSpec as P

LANES = 128
VMEM_LIMIT = 60 * 1024 * 1024


def whole(shape):
    return pl.BlockSpec(shape, lambda i: (0,) * len(shape))


def features_kernel(scale, x_ref, gain_ref, bias_ref, wl_ref, bl_ref, wr_ref, br_ref,
                    *refs):
    outs, (normed_ref, left_f32, right_f32) = refs[:-3], refs[-3:]
    seqs, width, channels = x_ref.shape
    c = wl_ref.shape[0]
    blocks = width // LANES
    fold = LANES // c
    quarter = width // fold
    right_bias = jnp.broadcast_to(br_ref[...], (LANES, c)).T[:, :1]
    for s in range(seqs):
        values = x_ref[s].astype(jnp.float32)
        average = jnp.mean(values, axis=-1, keepdims=True)
        centred = values - average
        variance = jnp.mean(centred * centred, axis=-1, keepdims=True)
        normed = centred * lax.rsqrt(variance + 1e-05) * gain_ref[...] + bias_ref[...]
        for h in range(channels // LANES):
            normed_ref[h, s * width:(s + 1) * width] = normed[:, h * LANES:(h + 1) * LANES]
        right = lax.dot_general(wr_ref[...], normed.astype(jnp.bfloat16), (((1,), (1,)), ((), ())),
                                preferred_element_type=jnp.float32) + right_bias
        for b in range(blocks):
            right_f32[pl.ds(b * c * seqs + s, c, stride=seqs), :] = right[:, b * LANES:(b + 1) * LANES]
    total = None
    for q in range(fold):
        rows = jnp.concatenate(
            [normed_ref[h, pl.ds(q, seqs * quarter, stride=fold), :] for h in range(channels // LANES)], axis=1
        ).astype(jnp.bfloat16)
        zeros = [jnp.zeros((c, channels), jnp.bfloat16)]
        w = jnp.concatenate(zeros * q + [wl_ref[...]] + zeros * (fold - 1 - q), axis=0)
        term = lax.dot_general(rows, w, (((1,), (1,)), ((), ())), preferred_element_type=jnp.float32)
        total = term if total is None else total + term
    total = (total + jnp.concatenate([bl_ref[...]] * fold, axis=1)) * scale
    for s in range(seqs):
        left_f32[pl.ds(s, quarter, stride=seqs), :] = total[s * quarter:(s + 1) * quarter]
    own_ref, *message_refs = outs
    here = lax.axis_index("row")
    rows = own_ref.shape[0]
    chips = left_f32.shape[0] // rows

    def left_for(step):
        block = source_at(here, step) % chips
        return left_f32[pl.ds(pl.multiple_of(block * rows, rows), rows), :].astype(jnp.bfloat16)

    own_ref[...] = left_for((0, 0))
    right = right_f32[...].astype(jnp.bfloat16)
    for step, message_ref in zip(direct_steps(chips), message_refs):
        message_ref[:right.shape[0]] = right
        message_ref[right.shape[0]:] = left_for(step)
    same_half = here // chips == lax.axis_index("col")
    for (a, b), message_ref in zip(far_steps(chips), message_refs[chips:]):
        message_ref[...] = jnp.where(same_half, left_for((a + 1, b)), left_for((a, b)))


def features(alignment, ln_gain, ln_bias, w_left, b_left, w_right, b_right, row_count, col_count):
    seqs, width, channels = alignment.shape
    c = w_left.shape[1]
    rows = seqs * width * c // LANES
    chips = row_count // col_count
    part = rows // chips
    shapes = [(n, LANES) for n in [part] + [rows + part] * chips + [part] * (chips // 2)]
    operands = (alignment, ln_gain.reshape(1, -1), ln_bias.reshape(1, -1), w_left.T, b_left.reshape(1, -1),
                w_right.T, b_right.reshape(1, -1))
    return pl.pallas_call(
        functools.partial(features_kernel, 1.0 / (seqs * row_count)),
        grid=(1,),
        out_shape=[jax.ShapeDtypeStruct(shape, jnp.bfloat16) for shape in shapes],
        in_specs=[whole(a.shape) for a in operands],
        out_specs=[whole(shape) for shape in shapes],
        scratch_shapes=[pltpu.VMEM((channels // LANES, seqs * width, LANES), jnp.float32),
                        pltpu.VMEM((rows, LANES), jnp.float32),
                        pltpu.VMEM((rows, LANES), jnp.float32)],
        compiler_params=pltpu.CompilerParams(vmem_limit_bytes=VMEM_LIMIT),
        name="features",
    )(*operands)


def sequence_rows(block, f32_ref, inner, seqs):
    sources = f32_ref.shape[0]
    for n in range(sources):
        f32_ref[n] = block(n)
    if seqs % 8 == 0:
        return lambda m: jnp.concatenate(
            [f32_ref[n, m * seqs:(m + 1) * seqs] for n in range(sources)], axis=0)
    flat = f32_ref.reshape(sources * inner * seqs, LANES)
    return lambda m: jnp.concatenate(
        [flat[pl.ds(m * seqs + s, sources, stride=inner * seqs), :] for s in range(seqs)], axis=0)


def prepare_kernel(seqs, c, left_at, mine_ref, other_ref, w_ref, bias_ref, own_right_ref,
                   left_ref, weights_ref, right_ref, bias_out_ref, left_f32, w_f32):
    sources, left_rows, _ = left_f32.shape
    same_half = lax.axis_index("row") // (sources // 2) == lax.axis_index("col")

    def block(n):
        first, of_same_half = left_at[n][0] * left_rows, left_at[n][1]
        mine = mine_ref[first:first + left_rows].astype(jnp.float32)
        other = other_ref[first:first + left_rows].astype(jnp.float32)
        return jnp.where(same_half == of_same_half, mine, other)

    left_of = sequence_rows(block, left_f32, left_rows // seqs, seqs)
    for k in range(left_rows // seqs):
        left_ref[k * LANES:(k + 1) * LANES] = left_of(k).T.astype(jnp.bfloat16)
    w_f32[...] = w_ref[...].astype(jnp.float32)
    for e in range(c):
        weights_ref[:, e * c:(e + 1) * c] = w_f32[pl.ds(e, c, stride=c), :].T.astype(jnp.bfloat16)
    right_ref[...] = own_right_ref[:right_ref.shape[0]]
    bias_out_ref[...] = bias_ref[...]


def prepare(mine, other, left_at, left_rows, w_out, b_out, right, seqs, c):
    sources = len(left_at)
    z = w_out.shape[1]
    outs = [((left_rows // seqs * LANES, sources * seqs), jnp.bfloat16), ((z, w_out.shape[0]), jnp.bfloat16),
            ((right.shape[0] - left_rows, LANES), jnp.bfloat16), ((1, z), jnp.float32)]
    operands = (mine, other, w_out, b_out.reshape(1, -1), right)
    return pl.pallas_call(
        functools.partial(prepare_kernel, seqs, c, left_at),
        grid=(1,),
        out_shape=[jax.ShapeDtypeStruct(*out) for out in outs],
        in_specs=[whole(a.shape) for a in operands],
        out_specs=[whole(out[0]) for out in outs],
        scratch_shapes=[pltpu.VMEM((sources, left_rows, LANES), jnp.float32), pltpu.VMEM(w_out.shape, jnp.float32)],
        compiler_params=pltpu.CompilerParams(vmem_limit_bytes=48 * 1024 * 1024),
        name="prepare",
    )(*operands)


def pair_kernel(seqs, c, right_at, left_ref, weights_ref, bias_ref, *refs):
    right_refs, (out_ref, right_f32, right_b, outer_ref) = refs[:-4], refs[-4:]
    rows_step = out_ref.shape[0]
    blocks = out_ref.shape[1] // LANES

    def block_of(n, at):
        array, first = right_at[n]
        return right_refs[array][first + at:first + at + c * seqs].astype(jnp.float32)

    @pl.when(pl.program_id(0) == 0)
    def _():
        for b in range(blocks):
            at = b * c * seqs
            right_of = sequence_rows(
                lambda n: block_of(n, at), right_f32, c, seqs)
            for e in range(c):
                lanes = (b * c + e) * LANES
                right_b[:, lanes:lanes + LANES] = right_of(e).astype(jnp.bfloat16)

    for b in range(blocks):
        for e in range(0, c, 2):
            at = (b * c + e) * LANES
            outer = jnp.dot(left_ref[...], right_b[:, at:at + 2 * LANES], preferred_element_type=jnp.float32)
            outer = outer.astype(jnp.bfloat16)
            for half in range(2):
                for i in range(rows_step):
                    outer_ref[i // 2, (e + half) * c:(e + half + 1) * c,
                              (i % 2) * LANES:(i % 2 + 1) * LANES] = (
                        outer[i * c:(i + 1) * c, half * LANES:(half + 1) * LANES])
        for p in range(rows_step // 2):
            update = jnp.dot(weights_ref[...], outer_ref[p], preferred_element_type=jnp.float32)
            for half in range(2):
                mine = update[:, half * LANES:(half + 1) * LANES].T + bias_ref[...]
                out_ref[2 * p + half, b * LANES:(b + 1) * LANES, :] = mine.astype(out_ref.dtype)


def pairs(left, weights, bias, rights, right_at, seqs, c, width):
    sources = len(right_at)
    z = weights.shape[0]
    rows = left.shape[0] // c
    rows_step = 8
    total = sources * seqs
    operands = (left, weights, bias, *rights)
    return pl.pallas_call(
        functools.partial(pair_kernel, seqs, c, right_at),
        grid=(rows // rows_step,),
        out_shape=jax.ShapeDtypeStruct((rows, width, z), jnp.bfloat16),
        in_specs=[pl.BlockSpec((rows_step * c, total), lambda i: (i, 0))] + [whole(a.shape) for a in operands[1:]],
        out_specs=pl.BlockSpec((rows_step, width, z), lambda i: (i, 0, 0)),
        scratch_shapes=[pltpu.VMEM((sources, c * seqs, LANES), jnp.float32),
                        pltpu.VMEM((total, width * c), jnp.bfloat16),
                        pltpu.VMEM((rows_step // 2, c * c, 2 * LANES), jnp.bfloat16)],
        compiler_params=pltpu.CompilerParams(vmem_limit_bytes=32 * 1024 * 1024),
        cost_estimate=pl.CostEstimate(flops=2 * rows * c * width * c * (total + z),
                                      bytes_accessed=2 * rows * width * z, transcendentals=0),
        name="pairs",
    )(*operands)


def source_at(here, step):
    return here ^ (2 * step[0] + step[1])


def direct_steps(chips):
    return [(a, 0) for a in range(1, chips)] + [(0, 1)]


def far_steps(chips):
    return [(a, 1) for a in range(chips // 2)]


def fetch(array, step, count):
    return lax.ppermute(array, "row", [(source_at(r, step), r) for r in range(count)])


def fetch_far(array, step, count):
    chips = count // 2
    a, b = step
    moves = []
    for r in range(count):
        half = r // chips
        if a + 1 < chips // 2:
            moves.append((2 * source_at(r, (a + 1, b)) + half, 2 * r + half))
        moves.append((2 * source_at(r, (a + chips // 2, b)) + half, 2 * r + 1 - half))
    return lax.ppermute(array, ("row", "col"), moves)


def on_device(alignment, ln_gain, ln_bias, w_left, b_left, w_right, b_right, w_out, b_out):
    seqs, width, _ = alignment.shape
    c = w_left.shape[1]
    row_count = lax.axis_size("row")
    col_count = lax.axis_size("col")
    own, *messages = features(alignment, ln_gain, ln_bias, w_left, b_left, w_right, b_right, row_count, col_count)
    along = row_count // 2
    direct = messages[:along]
    left_rows = own.shape[0]
    rows = direct[0].shape[0] - left_rows

    line = [fetch(message, step, row_count) for step, message in reversed([*zip(direct_steps(along), direct[:-1])])][::-1]
    beyond = [fetch_far(message, step, row_count) for step, message in zip(far_steps(along), messages[along:])]
    beyond[0], beside = lax.optimization_barrier((beyond[0], direct[-1]))
    across = fetch(beside, (0, 1), row_count)
    far = [fetch(block[:rows], (0, 1), row_count) for block in reversed(line)][::-1]
    *far[:-1], held = lax.optimization_barrier((*far[:-1], tuple(line)))

    mine = jnp.concatenate([own] + [block[rows:] for block in (*held, across)] + beyond)
    other = lax.ppermute(mine, "col", [(0, 1), (1, 0)])
    left_at = [(a, True) for a in range(along + 1)]
    left_at += [(along + a, True) if a < along // 2 else (a + 1 + along // 2, False) for a in range(1, along)]
    left, weights, right, bias = prepare(mine, other, left_at, left_rows, w_out, b_out, direct[0], seqs, c)
    right_at = [(n, 0) for n in range(row_count)]
    return pairs(left, weights, bias, [right, *line, across, *far], right_at, seqs, c, width)


def solution(mesh):
    in_specs = (P(("group", "row"), "col", None), P(), P(), P(), P(), P(), P(), P(), P())
    out_specs = P(("group", "row"), "col", None)
    return jax.shard_map(
        on_device, mesh=mesh, in_specs=in_specs, out_specs=out_specs, check_vma=False
    )
```

```python
import functools

import jax
import jax.numpy as jnp
from jax import lax
from jax.experimental import pallas as pl
from jax.experimental.pallas import tpu as pltpu
from jax.sharding import PartitionSpec as P

LANES = 128
VMEM_LIMIT = 60 * 1024 * 1024


def whole(shape):
    return pl.BlockSpec(shape, lambda i: (0,) * len(shape))


def features_kernel(scale, x_ref, gain_ref, bias_ref, wl_ref, bl_ref, wr_ref, br_ref,
                    *refs):
    outs, (normed_ref, left_f32, right_f32) = refs[:-3], refs[-3:]
    seqs, width, channels = x_ref.shape
    c = wl_ref.shape[0]
    blocks = width // LANES
    fold = LANES // c
    quarter = width // fold
    right_bias = jnp.broadcast_to(br_ref[...], (LANES, c)).T[:, :1]
    for s in range(seqs):
        values = x_ref[s].astype(jnp.float32)
        average = jnp.mean(values, axis=-1, keepdims=True)
        centred = values - average
        variance = jnp.mean(centred * centred, axis=-1, keepdims=True)
        normed = centred * lax.rsqrt(variance + 1e-05) * gain_ref[...] + bias_ref[...]
        for h in range(channels // LANES):
            normed_ref[h, s * width:(s + 1) * width] = normed[:, h * LANES:(h + 1) * LANES]
        right = lax.dot_general(wr_ref[...], normed.astype(jnp.bfloat16), (((1,), (1,)), ((), ())),
                                preferred_element_type=jnp.float32) + right_bias
        for b in range(blocks):
            right_f32[pl.ds(b * c * seqs + s, c, stride=seqs), :] = right[:, b * LANES:(b + 1) * LANES]
    total = None
    for q in range(fold):
        rows = jnp.concatenate(
            [normed_ref[h, pl.ds(q, seqs * quarter, stride=fold), :] for h in range(channels // LANES)], axis=1
        ).astype(jnp.bfloat16)
        zeros = [jnp.zeros((c, channels), jnp.bfloat16)]
        w = jnp.concatenate(zeros * q + [wl_ref[...]] + zeros * (fold - 1 - q), axis=0)
        term = lax.dot_general(rows, w, (((1,), (1,)), ((), ())), preferred_element_type=jnp.float32)
        total = term if total is None else total + term
    total = (total + jnp.concatenate([bl_ref[...]] * fold, axis=1)) * scale
    for s in range(seqs):
        left_f32[pl.ds(s, quarter, stride=seqs), :] = total[s * quarter:(s + 1) * quarter]
    own_ref, *message_refs = outs
    here = lax.axis_index("row")
    rows = own_ref.shape[0]
    chips = left_f32.shape[0] // rows

    def left_for(step):
        block = source_at(here, step) % chips
        return left_f32[pl.ds(pl.multiple_of(block * rows, rows), rows), :].astype(jnp.bfloat16)

    own_ref[...] = left_for((0, 0))
    right = right_f32[...].astype(jnp.bfloat16)
    for step, message_ref in zip(direct_steps(chips), message_refs):
        message_ref[:right.shape[0]] = right
        message_ref[right.shape[0]:] = left_for(step)
    same_half = here // chips == lax.axis_index("col")
    for (a, b), message_ref in zip(far_steps(chips), message_refs[chips:]):
        message_ref[...] = jnp.where(same_half, left_for((a + 1, b)), left_for((a, b)))


def features(alignment, ln_gain, ln_bias, w_left, b_left, w_right, b_right, row_count, col_count):
    seqs, width, channels = alignment.shape
    c = w_left.shape[1]
    rows = seqs * width * c // LANES
    chips = row_count // col_count
    part = rows // chips
    shapes = [(n, LANES) for n in [part] + [rows + part] * chips + [part] * (chips // 2)]
    operands = (alignment, ln_gain.reshape(1, -1), ln_bias.reshape(1, -1), w_left.T, b_left.reshape(1, -1),
                w_right.T, b_right.reshape(1, -1))
    return pl.pallas_call(
        functools.partial(features_kernel, 1.0 / (seqs * row_count)),
        grid=(1,),
        out_shape=[jax.ShapeDtypeStruct(shape, jnp.bfloat16) for shape in shapes],
        in_specs=[whole(a.shape) for a in operands],
        out_specs=[whole(shape) for shape in shapes],
        scratch_shapes=[pltpu.VMEM((channels // LANES, seqs * width, LANES), jnp.float32),
                        pltpu.VMEM((rows, LANES), jnp.float32),
                        pltpu.VMEM((rows, LANES), jnp.float32)],
        compiler_params=pltpu.CompilerParams(vmem_limit_bytes=VMEM_LIMIT),
        name="features",
    )(*operands)


def sequence_rows(block, f32_ref, inner, seqs):
    sources = f32_ref.shape[0]
    for n in range(sources):
        f32_ref[n] = block(n)
    if seqs % 8 == 0:
        return lambda m: jnp.concatenate(
            [f32_ref[n, m * seqs:(m + 1) * seqs] for n in range(sources)], axis=0)
    flat = f32_ref.reshape(sources * inner * seqs, LANES)
    return lambda m: jnp.concatenate(
        [flat[pl.ds(m * seqs + s, sources, stride=inner * seqs), :] for s in range(seqs)], axis=0)


def prepare_kernel(seqs, left_at, mine_ref, other_ref, left_ref, left_f32):
    sources, left_rows, _ = left_f32.shape
    same_half = lax.axis_index("row") // (sources // 2) == lax.axis_index("col")

    def block(n):
        first, of_same_half = left_at[n][0] * left_rows, left_at[n][1]
        mine = mine_ref[first:first + left_rows].astype(jnp.float32)
        other = other_ref[first:first + left_rows].astype(jnp.float32)
        return jnp.where(same_half == of_same_half, mine, other)

    left_of = sequence_rows(block, left_f32, left_rows // seqs, seqs)
    for k in range(left_rows // seqs):
        left_ref[k * LANES:(k + 1) * LANES] = left_of(k).T.astype(jnp.bfloat16)


def prepare(mine, other, left_at, left_rows, seqs):
    sources = len(left_at)
    shape = (left_rows // seqs * LANES, sources * seqs)
    return pl.pallas_call(
        functools.partial(prepare_kernel, seqs, left_at),
        grid=(1,),
        out_shape=jax.ShapeDtypeStruct(shape, jnp.bfloat16),
        in_specs=[whole(mine.shape), whole(other.shape)],
        out_specs=whole(shape),
        scratch_shapes=[pltpu.VMEM((sources, left_rows, LANES), jnp.float32)],
        compiler_params=pltpu.CompilerParams(vmem_limit_bytes=48 * 1024 * 1024),
        name="prepare",
    )(mine, other)


def constants_kernel(c, rows, w_ref, bias_ref, message_ref, weights_ref, bias_out_ref, right_ref, w_f32):
    w_f32[...] = w_ref[...].astype(jnp.float32)
    for e in range(c):
        weights_ref[:, e * c:(e + 1) * c] = w_f32[pl.ds(e, c, stride=c), :].T.astype(jnp.bfloat16)
    bias_out_ref[...] = bias_ref[...]
    right_ref[...] = message_ref[:rows]


def constants(w_out, b_out, message, rows, c):
    z = w_out.shape[1]
    operands = (w_out, b_out.reshape(1, -1), message)
    outs = [((z, w_out.shape[0]), jnp.bfloat16), ((1, z), jnp.float32), ((rows, LANES), jnp.bfloat16)]
    return pl.pallas_call(
        functools.partial(constants_kernel, c, rows),
        grid=(1,),
        out_shape=[jax.ShapeDtypeStruct(*out) for out in outs],
        in_specs=[whole(a.shape) for a in operands],
        out_specs=[whole(out[0]) for out in outs],
        scratch_shapes=[pltpu.VMEM(w_out.shape, jnp.float32)],
        compiler_params=pltpu.CompilerParams(vmem_limit_bytes=48 * 1024 * 1024),
        name="constants",
    )(*operands)


def pair_kernel(seqs, c, right_at, left_ref, weights_ref, bias_ref, *refs):
    right_refs, (out_ref, right_f32, right_b, outer_ref) = refs[:-4], refs[-4:]
    rows_step = out_ref.shape[0]
    blocks = out_ref.shape[1] // LANES

    def block_of(n, at):
        array, first = right_at[n]
        return right_refs[array][first + at:first + at + c * seqs].astype(jnp.float32)

    @pl.when(pl.program_id(0) == 0)
    def _():
        for b in range(blocks):
            at = b * c * seqs
            right_of = sequence_rows(
                lambda n: block_of(n, at), right_f32, c, seqs)
            for e in range(c):
                lanes = (b * c + e) * LANES
                right_b[:, lanes:lanes + LANES] = right_of(e).astype(jnp.bfloat16)

    for b in range(blocks):
        for e in range(0, c, 2):
            at = (b * c + e) * LANES
            outer = jnp.dot(left_ref[...], right_b[:, at:at + 2 * LANES], preferred_element_type=jnp.float32)
            outer = outer.astype(jnp.bfloat16)
            for half in range(2):
                for i in range(rows_step):
                    outer_ref[i // 2, (e + half) * c:(e + half + 1) * c,
                              (i % 2) * LANES:(i % 2 + 1) * LANES] = (
                        outer[i * c:(i + 1) * c, half * LANES:(half + 1) * LANES])
        for p in range(rows_step // 2):
            update = jnp.dot(weights_ref[...], outer_ref[p], preferred_element_type=jnp.float32)
            for half in range(2):
                mine = update[:, half * LANES:(half + 1) * LANES].T + bias_ref[...]
                out_ref[2 * p + half, b * LANES:(b + 1) * LANES, :] = mine.astype(out_ref.dtype)


def pairs(left, weights, bias, rights, right_at, seqs, c, width):
    sources = len(right_at)
    z = weights.shape[0]
    rows = left.shape[0] // c
    rows_step = 8
    total = sources * seqs
    operands = (left, weights, bias, *rights)
    return pl.pallas_call(
        functools.partial(pair_kernel, seqs, c, right_at),
        grid=(rows // rows_step,),
        out_shape=jax.ShapeDtypeStruct((rows, width, z), jnp.bfloat16),
        in_specs=[pl.BlockSpec((rows_step * c, total), lambda i: (i, 0))] + [whole(a.shape) for a in operands[1:]],
        out_specs=pl.BlockSpec((rows_step, width, z), lambda i: (i, 0, 0)),
        scratch_shapes=[pltpu.VMEM((sources, c * seqs, LANES), jnp.float32),
                        pltpu.VMEM((total, width * c), jnp.bfloat16),
                        pltpu.VMEM((rows_step // 2, c * c, 2 * LANES), jnp.bfloat16)],
        compiler_params=pltpu.CompilerParams(vmem_limit_bytes=32 * 1024 * 1024),
        cost_estimate=pl.CostEstimate(flops=2 * rows * c * width * c * (total + z),
                                      bytes_accessed=2 * rows * width * z, transcendentals=0),
        name="pairs",
    )(*operands)


def source_at(here, step):
    return here ^ (2 * step[0] + step[1])


def direct_steps(chips):
    return [(a, 0) for a in range(1, chips)] + [(0, 1)]


def far_steps(chips):
    return [(a, 1) for a in range(chips // 2)]


def fetch(array, step, count):
    return lax.ppermute(array, "row", [(source_at(r, step), r) for r in range(count)])


def fetch_far(array, step, count):
    chips = count // 2
    a, b = step
    moves = []
    for r in range(count):
        half = r // chips
        if a + 1 < chips // 2:
            moves.append((2 * source_at(r, (a + 1, b)) + half, 2 * r + half))
        moves.append((2 * source_at(r, (a + chips // 2, b)) + half, 2 * r + 1 - half))
    return lax.ppermute(array, ("row", "col"), moves)


def on_device(alignment, ln_gain, ln_bias, w_left, b_left, w_right, b_right, w_out, b_out):
    seqs, width, _ = alignment.shape
    c = w_left.shape[1]
    row_count = lax.axis_size("row")
    col_count = lax.axis_size("col")
    own, *messages = features(alignment, ln_gain, ln_bias, w_left, b_left, w_right, b_right, row_count, col_count)
    along = row_count // 2
    direct = messages[:along]
    left_rows = own.shape[0]
    rows = direct[0].shape[0] - left_rows

    line = [fetch(message, step, row_count) for step, message in reversed([*zip(direct_steps(along), direct[:-1])])][::-1]
    across = fetch(direct[-1], (0, 1), row_count)
    far = []
    for block in reversed(line):
        block, across = lax.optimization_barrier((block, across))
        far.insert(0, fetch(block[:rows], (0, 1), row_count))
    first, *later = messages[along:]
    later, _ = lax.optimization_barrier((tuple(later), tuple(line)))
    beyond = [fetch_far(message, step, row_count) for step, message in zip(far_steps(along), (first, *later))]

    message, _ = lax.optimization_barrier((direct[0], line[0]))
    weights, bias, right = constants(w_out, b_out, message, rows, c)
    weights, bias, right, held, *far[1:] = lax.optimization_barrier((weights, bias, right, tuple(line), *far[1:]))

    mine = jnp.concatenate([own] + [block[rows:] for block in (*held, across)] + beyond)
    other = lax.ppermute(mine, "col", [(0, 1), (1, 0)])
    other, far[0] = lax.optimization_barrier((other, far[0]))
    left_at = [(a, True) for a in range(along + 1)]
    left_at += [(along + a, True) if a < along // 2 else (a + 1 + along // 2, False) for a in range(1, along)]
    left = prepare(mine, other, left_at, left_rows, seqs)
    right_at = [(n, 0) for n in range(row_count)]
    return pairs(left, weights, bias, [right, *line, across, *far], right_at, seqs, c, width)


def solution(mesh):
    in_specs = (P(("group", "row"), "col", None), P(), P(), P(), P(), P(), P(), P(), P())
    out_specs = P(("group", "row"), "col", None)
    return jax.shard_map(
        on_device, mesh=mesh, in_specs=in_specs, out_specs=out_specs, check_vma=False
    )
```

```python
import functools

import jax
import jax.numpy as jnp
from jax import lax
from jax.experimental import pallas as pl
from jax.experimental.pallas import tpu as pltpu
from jax.sharding import PartitionSpec as P

LANES = 128
VMEM_LIMIT = 60 * 1024 * 1024


def whole(shape):
    return pl.BlockSpec(shape, lambda i: (0,) * len(shape))


def features_kernel(scale, x_ref, gain_ref, bias_ref, wl_ref, bl_ref, wr_ref, br_ref,
                    *refs):
    outs, (normed_ref, left_f32, right_f32) = refs[:-3], refs[-3:]
    seqs, width, channels = x_ref.shape
    c = wl_ref.shape[0]
    blocks = width // LANES
    fold = LANES // c
    quarter = width // fold
    right_bias = jnp.broadcast_to(br_ref[...], (LANES, c)).T[:, :1]
    for s in range(seqs):
        values = x_ref[s].astype(jnp.float32)
        average = jnp.mean(values, axis=-1, keepdims=True)
        centred = values - average
        variance = jnp.mean(centred * centred, axis=-1, keepdims=True)
        normed = centred * lax.rsqrt(variance + 1e-05) * gain_ref[...] + bias_ref[...]
        for h in range(channels // LANES):
            normed_ref[h, s * width:(s + 1) * width] = normed[:, h * LANES:(h + 1) * LANES]
        right = lax.dot_general(wr_ref[...], normed.astype(jnp.bfloat16), (((1,), (1,)), ((), ())),
                                preferred_element_type=jnp.float32) + right_bias
        for b in range(blocks):
            right_f32[pl.ds(b * c * seqs + s, c, stride=seqs), :] = right[:, b * LANES:(b + 1) * LANES]
    total = None
    for q in range(fold):
        rows = jnp.concatenate(
            [normed_ref[h, pl.ds(q, seqs * quarter, stride=fold), :] for h in range(channels // LANES)], axis=1
        ).astype(jnp.bfloat16)
        zeros = [jnp.zeros((c, channels), jnp.bfloat16)]
        w = jnp.concatenate(zeros * q + [wl_ref[...]] + zeros * (fold - 1 - q), axis=0)
        term = lax.dot_general(rows, w, (((1,), (1,)), ((), ())), preferred_element_type=jnp.float32)
        total = term if total is None else total + term
    total = (total + jnp.concatenate([bl_ref[...]] * fold, axis=1)) * scale
    for s in range(seqs):
        left_f32[pl.ds(s, quarter, stride=seqs), :] = total[s * quarter:(s + 1) * quarter]
    own_ref, *message_refs = outs
    here = lax.axis_index("row")
    rows = own_ref.shape[0]
    chips = left_f32.shape[0] // rows

    def left_for(step):
        block = source_at(here, step) % chips
        return left_f32[pl.ds(pl.multiple_of(block * rows, rows), rows), :].astype(jnp.bfloat16)

    own_ref[...] = left_for((0, 0))
    right = right_f32[...].astype(jnp.bfloat16)
    for step, message_ref in zip(direct_steps(chips), message_refs):
        first = rows if carries_far(step, chips) else 0
        message_ref[first:first + right.shape[0]] = right
        if first:
            message_ref[:rows] = left_for(step)
            message_ref[first + right.shape[0]:] = left_for((step[0], 1))
        else:
            message_ref[right.shape[0]:] = left_for(step)
    same_half = here // chips == lax.axis_index("col")
    for (a, b), message_ref in zip(far_steps(chips), message_refs[chips:]):
        message_ref[...] = jnp.where(same_half, left_for((a + 1, b)), left_for((a, b)))


def features(alignment, ln_gain, ln_bias, w_left, b_left, w_right, b_right, row_count, col_count):
    seqs, width, channels = alignment.shape
    c = w_left.shape[1]
    rows = seqs * width * c // LANES
    chips = row_count // col_count
    part = rows // chips
    shapes = [(part, LANES)]
    shapes += [(rows + part * (2 if carries_far(step, chips) else 1), LANES) for step in direct_steps(chips)]
    shapes += [(part, LANES)] * len(far_steps(chips))
    operands = (alignment, ln_gain.reshape(1, -1), ln_bias.reshape(1, -1), w_left.T, b_left.reshape(1, -1),
                w_right.T, b_right.reshape(1, -1))
    return pl.pallas_call(
        functools.partial(features_kernel, 1.0 / (seqs * row_count)),
        grid=(1,),
        out_shape=[jax.ShapeDtypeStruct(shape, jnp.bfloat16) for shape in shapes],
        in_specs=[whole(a.shape) for a in operands],
        out_specs=[whole(shape) for shape in shapes],
        scratch_shapes=[pltpu.VMEM((channels // LANES, seqs * width, LANES), jnp.float32),
                        pltpu.VMEM((rows, LANES), jnp.float32),
                        pltpu.VMEM((rows, LANES), jnp.float32)],
        compiler_params=pltpu.CompilerParams(vmem_limit_bytes=VMEM_LIMIT),
        name="features",
    )(*operands)


def sequence_rows(block, f32_ref, inner, seqs):
    sources = f32_ref.shape[0]
    for n in range(sources):
        f32_ref[n] = block(n)
    if seqs % 8 == 0:
        return lambda m: jnp.concatenate(
            [f32_ref[n, m * seqs:(m + 1) * seqs] for n in range(sources)], axis=0)
    flat = f32_ref.reshape(sources * inner * seqs, LANES)
    return lambda m: jnp.concatenate(
        [flat[pl.ds(m * seqs + s, sources, stride=inner * seqs), :] for s in range(seqs)], axis=0)


def prepare_kernel(seqs, left_at, mine_ref, other_ref, left_ref, left_f32):
    sources, left_rows, _ = left_f32.shape
    same_half = lax.axis_index("row") // (sources // 2) == lax.axis_index("col")

    def block(n):
        first, of_same_half = left_at[n][0] * left_rows, left_at[n][1]
        mine = mine_ref[first:first + left_rows].astype(jnp.float32)
        other = other_ref[first:first + left_rows].astype(jnp.float32)
        return jnp.where(same_half == of_same_half, mine, other)

    left_of = sequence_rows(block, left_f32, left_rows // seqs, seqs)
    for k in range(left_rows // seqs):
        left_ref[k * LANES:(k + 1) * LANES] = left_of(k).T.astype(jnp.bfloat16)


def prepare(mine, other, left_at, left_rows, seqs):
    sources = len(left_at)
    shape = (left_rows // seqs * LANES, sources * seqs)
    return pl.pallas_call(
        functools.partial(prepare_kernel, seqs, left_at),
        grid=(1,),
        out_shape=jax.ShapeDtypeStruct(shape, jnp.bfloat16),
        in_specs=[whole(mine.shape), whole(other.shape)],
        out_specs=whole(shape),
        scratch_shapes=[pltpu.VMEM((sources, left_rows, LANES), jnp.float32)],
        compiler_params=pltpu.CompilerParams(vmem_limit_bytes=48 * 1024 * 1024),
        name="prepare",
    )(mine, other)


def constants_kernel(c, rows, w_ref, bias_ref, message_ref, weights_ref, bias_out_ref, right_ref, w_f32):
    w_f32[...] = w_ref[...].astype(jnp.float32)
    for e in range(c):
        weights_ref[:, e * c:(e + 1) * c] = w_f32[pl.ds(e, c, stride=c), :].T.astype(jnp.bfloat16)
    bias_out_ref[...] = bias_ref[...]
    right_ref[...] = message_ref[:rows]


def constants(w_out, b_out, message, rows, c):
    z = w_out.shape[1]
    operands = (w_out, b_out.reshape(1, -1), message)
    outs = [((z, w_out.shape[0]), jnp.bfloat16), ((1, z), jnp.float32), ((rows, LANES), jnp.bfloat16)]
    return pl.pallas_call(
        functools.partial(constants_kernel, c, rows),
        grid=(1,),
        out_shape=[jax.ShapeDtypeStruct(*out) for out in outs],
        in_specs=[whole(a.shape) for a in operands],
        out_specs=[whole(out[0]) for out in outs],
        scratch_shapes=[pltpu.VMEM(w_out.shape, jnp.float32)],
        compiler_params=pltpu.CompilerParams(vmem_limit_bytes=48 * 1024 * 1024),
        name="constants",
    )(*operands)


def pair_kernel(seqs, c, right_at, left_ref, weights_ref, bias_ref, *refs):
    right_refs, (out_ref, right_f32, right_b, outer_ref) = refs[:-4], refs[-4:]
    rows_step = out_ref.shape[0]
    blocks = out_ref.shape[1] // LANES

    def block_of(n, at):
        array, first = right_at[n]
        return right_refs[array][first + at:first + at + c * seqs].astype(jnp.float32)

    @pl.when(pl.program_id(0) == 0)
    def _():
        for b in range(blocks):
            at = b * c * seqs
            right_of = sequence_rows(
                lambda n: block_of(n, at), right_f32, c, seqs)
            for e in range(c):
                lanes = (b * c + e) * LANES
                right_b[:, lanes:lanes + LANES] = right_of(e).astype(jnp.bfloat16)

    for b in range(blocks):
        for e in range(0, c, 2):
            at = (b * c + e) * LANES
            outer = jnp.dot(left_ref[...], right_b[:, at:at + 2 * LANES], preferred_element_type=jnp.float32)
            outer = outer.astype(jnp.bfloat16)
            for half in range(2):
                for i in range(rows_step):
                    outer_ref[i // 2, (e + half) * c:(e + half + 1) * c,
                              (i % 2) * LANES:(i % 2 + 1) * LANES] = (
                        outer[i * c:(i + 1) * c, half * LANES:(half + 1) * LANES])
        for p in range(rows_step // 2):
            update = jnp.dot(weights_ref[...], outer_ref[p], preferred_element_type=jnp.float32)
            for half in range(2):
                mine = update[:, half * LANES:(half + 1) * LANES].T + bias_ref[...]
                out_ref[2 * p + half, b * LANES:(b + 1) * LANES, :] = mine.astype(out_ref.dtype)


def pairs(left, weights, bias, rights, right_at, seqs, c, width):
    sources = len(right_at)
    z = weights.shape[0]
    rows = left.shape[0] // c
    rows_step = 8
    total = sources * seqs
    operands = (left, weights, bias, *rights)
    return pl.pallas_call(
        functools.partial(pair_kernel, seqs, c, right_at),
        grid=(rows // rows_step,),
        out_shape=jax.ShapeDtypeStruct((rows, width, z), jnp.bfloat16),
        in_specs=[pl.BlockSpec((rows_step * c, total), lambda i: (i, 0))] + [whole(a.shape) for a in operands[1:]],
        out_specs=pl.BlockSpec((rows_step, width, z), lambda i: (i, 0, 0)),
        scratch_shapes=[pltpu.VMEM((sources, c * seqs, LANES), jnp.float32),
                        pltpu.VMEM((total, width * c), jnp.bfloat16),
                        pltpu.VMEM((rows_step // 2, c * c, 2 * LANES), jnp.bfloat16)],
        compiler_params=pltpu.CompilerParams(vmem_limit_bytes=32 * 1024 * 1024),
        cost_estimate=pl.CostEstimate(flops=2 * rows * c * width * c * (total + z),
                                      bytes_accessed=2 * rows * width * z, transcendentals=0),
        name="pairs",
    )(*operands)


def source_at(here, step):
    return here ^ (2 * step[0] + step[1])


def direct_steps(chips):
    return [(a, 0) for a in range(1, chips)] + [(0, 1)]


def far_steps(chips):
    return [(a, 1) for a in range(chips // 2 - 1)]


def carries_far(step, chips):
    return step == (chips - 1, 0)


def fetch(array, step, count):
    return lax.ppermute(array, "row", [(source_at(r, step), r) for r in range(count)])


def fetch_far(array, step, count):
    chips = count // 2
    a, b = step
    moves = []
    for r in range(count):
        half = r // chips
        moves.append((2 * source_at(r, (a + 1, b)) + half, 2 * r + half))
        moves.append((2 * source_at(r, (a + chips // 2, b)) + half, 2 * r + 1 - half))
    return lax.ppermute(array, ("row", "col"), moves)


def on_device(alignment, ln_gain, ln_bias, w_left, b_left, w_right, b_right, w_out, b_out):
    seqs, width, _ = alignment.shape
    c = w_left.shape[1]
    row_count = lax.axis_size("row")
    col_count = lax.axis_size("col")
    own, *messages = features(alignment, ln_gain, ln_bias, w_left, b_left, w_right, b_right, row_count, col_count)
    along = row_count // 2
    direct = messages[:along]
    left_rows = own.shape[0]
    rows = direct[0].shape[0] - left_rows

    line = [fetch(message, step, row_count) for step, message in reversed([*zip(direct_steps(along), direct[:-1])])][::-1]
    across = fetch(direct[-1], (0, 1), row_count)
    beyond = [fetch_far(message, step, row_count) for step, message in zip(far_steps(along), messages[along:])]
    far = []
    for step, block in reversed([*zip(direct_steps(along), line)]):
        block, across = lax.optimization_barrier((block, across))
        block = block[left_rows:] if carries_far(step, along) else block[:rows]
        far.insert(0, fetch(block, (0, 1), row_count))

    message, _ = lax.optimization_barrier((direct[0], line[0]))
    weights, bias, right = constants(w_out, b_out, message, rows, c)
    weights, bias, right, held, far = lax.optimization_barrier((weights, bias, right, tuple(line), tuple(far)))
    mine = jnp.concatenate([own] + [block[rows:] for block in held[:-1]] + [held[-1][:left_rows], across[rows:]]
                           + beyond + [far[-1][rows:]])
    other = lax.ppermute(mine, "col", [(0, 1), (1, 0)])
    half = along // 2
    left_at = [(a, True) for a in range(along + 1)]
    left_at += [(along + a, True) if a < half else (along + 1 + a - half, False) for a in range(1, along - 1)]
    left_at += [(along + half, True)]
    left = prepare(mine, other, left_at, left_rows, seqs)
    right_at = [(n, left_rows if n == along - 1 else 0) for n in range(row_count)]
    return pairs(left, weights, bias, [right, *line, across, *far], right_at, seqs, c, width)


def solution(mesh):
    in_specs = (P(("group", "row"), "col", None), P(), P(), P(), P(), P(), P(), P(), P())
    out_specs = P(("group", "row"), "col", None)
    return jax.shard_map(
        on_device, mesh=mesh, in_specs=in_specs, out_specs=out_specs, check_vma=False
    )
```

```python
import functools

import jax
import jax.numpy as jnp
from jax import lax
from jax.experimental import pallas as pl
from jax.experimental.pallas import tpu as pltpu
from jax.sharding import PartitionSpec as P

LANES = 128
VMEM_LIMIT = 60 * 1024 * 1024


def whole(shape):
    return pl.BlockSpec(shape, lambda i: (0,) * len(shape))


def features_kernel(scale, x_ref, gain_ref, bias_ref, wl_ref, bl_ref, wr_ref, br_ref,
                    *refs):
    outs, (normed_ref, left_f32, right_f32) = refs[:-3], refs[-3:]
    seqs, width, channels = x_ref.shape
    c = wl_ref.shape[0]
    blocks = width // LANES
    fold = LANES // c
    quarter = width // fold
    right_bias = jnp.broadcast_to(br_ref[...], (LANES, c)).T[:, :1]
    for s in range(seqs):
        values = x_ref[s].astype(jnp.float32)
        average = jnp.mean(values, axis=-1, keepdims=True)
        centred = values - average
        variance = jnp.mean(centred * centred, axis=-1, keepdims=True)
        normed = centred * lax.rsqrt(variance + 1e-05) * gain_ref[...] + bias_ref[...]
        for h in range(channels // LANES):
            normed_ref[h, s * width:(s + 1) * width] = normed[:, h * LANES:(h + 1) * LANES]
        right = lax.dot_general(wr_ref[...], normed.astype(jnp.bfloat16), (((1,), (1,)), ((), ())),
                                preferred_element_type=jnp.float32) + right_bias
        for b in range(blocks):
            right_f32[pl.ds(b * c * seqs + s, c, stride=seqs), :] = right[:, b * LANES:(b + 1) * LANES]
    total = None
    for q in range(fold):
        rows = jnp.concatenate(
            [normed_ref[h, pl.ds(q, seqs * quarter, stride=fold), :] for h in range(channels // LANES)], axis=1
        ).astype(jnp.bfloat16)
        zeros = [jnp.zeros((c, channels), jnp.bfloat16)]
        w = jnp.concatenate(zeros * q + [wl_ref[...]] + zeros * (fold - 1 - q), axis=0)
        term = lax.dot_general(rows, w, (((1,), (1,)), ((), ())), preferred_element_type=jnp.float32)
        total = term if total is None else total + term
    total = (total + jnp.concatenate([bl_ref[...]] * fold, axis=1)) * scale
    for s in range(seqs):
        left_f32[pl.ds(s, quarter, stride=seqs), :] = total[s * quarter:(s + 1) * quarter]
    own_ref, *message_refs = outs
    here = lax.axis_index("row")
    rows = own_ref.shape[0]
    chips = left_f32.shape[0] // rows

    def left_for(step):
        block = source_at(here, step) % chips
        return left_f32[pl.ds(pl.multiple_of(block * rows, rows), rows), :].astype(jnp.bfloat16)

    own_ref[...] = left_for((0, 0))
    right = right_f32[...].astype(jnp.bfloat16)
    for step, message_ref in zip(direct_steps(chips), message_refs):
        first = rows if carries_far(step, chips) else 0
        message_ref[first:first + right.shape[0]] = right
        if first:
            message_ref[:rows] = left_for(step)
            message_ref[first + right.shape[0]:] = left_for((step[0], 1))
        else:
            message_ref[right.shape[0]:] = left_for(step)
    same_half = here // chips == lax.axis_index("col")
    for (a, b), message_ref in zip(far_steps(chips), message_refs[chips:]):
        message_ref[...] = jnp.where(same_half, left_for((a + 1, b)), left_for((a, b)))


def features(alignment, ln_gain, ln_bias, w_left, b_left, w_right, b_right, row_count, col_count):
    seqs, width, channels = alignment.shape
    c = w_left.shape[1]
    rows = seqs * width * c // LANES
    chips = row_count // col_count
    part = rows // chips
    shapes = [(part, LANES)]
    shapes += [(rows + part * (2 if carries_far(step, chips) else 1), LANES) for step in direct_steps(chips)]
    shapes += [(part, LANES)] * len(far_steps(chips))
    operands = (alignment, ln_gain.reshape(1, -1), ln_bias.reshape(1, -1), w_left.T, b_left.reshape(1, -1),
                w_right.T, b_right.reshape(1, -1))
    return pl.pallas_call(
        functools.partial(features_kernel, 1.0 / (seqs * row_count)),
        grid=(1,),
        out_shape=[jax.ShapeDtypeStruct(shape, jnp.bfloat16) for shape in shapes],
        in_specs=[whole(a.shape) for a in operands],
        out_specs=[whole(shape) for shape in shapes],
        scratch_shapes=[pltpu.VMEM((channels // LANES, seqs * width, LANES), jnp.float32),
                        pltpu.VMEM((rows, LANES), jnp.float32),
                        pltpu.VMEM((rows, LANES), jnp.float32)],
        compiler_params=pltpu.CompilerParams(vmem_limit_bytes=VMEM_LIMIT),
        name="features",
    )(*operands)


def sequence_rows(block, f32_ref, inner, seqs):
    sources = f32_ref.shape[0]
    for n in range(sources):
        f32_ref[n] = block(n)
    if seqs % 8 == 0:
        return lambda m: jnp.concatenate(
            [f32_ref[n, m * seqs:(m + 1) * seqs] for n in range(sources)], axis=0)
    flat = f32_ref.reshape(sources * inner * seqs, LANES)
    return lambda m: jnp.concatenate(
        [flat[pl.ds(m * seqs + s, sources, stride=inner * seqs), :] for s in range(seqs)], axis=0)


def prepare_kernel(seqs, left_at, mine_ref, other_ref, left_ref, left_f32):
    sources, left_rows, _ = left_f32.shape
    same_half = lax.axis_index("row") // (sources // 2) == lax.axis_index("col")

    def block(n):
        first, of_same_half = left_at[n][0] * left_rows, left_at[n][1]
        mine = mine_ref[first:first + left_rows].astype(jnp.float32)
        other = other_ref[first:first + left_rows].astype(jnp.float32)
        return jnp.where(same_half == of_same_half, mine, other)

    left_of = sequence_rows(block, left_f32, left_rows // seqs, seqs)
    for k in range(left_rows // seqs):
        left_ref[k * LANES:(k + 1) * LANES] = left_of(k).T.astype(jnp.bfloat16)


def prepare(mine, other, left_at, left_rows, seqs):
    sources = len(left_at)
    shape = (left_rows // seqs * LANES, sources * seqs)
    return pl.pallas_call(
        functools.partial(prepare_kernel, seqs, left_at),
        grid=(1,),
        out_shape=jax.ShapeDtypeStruct(shape, jnp.bfloat16),
        in_specs=[whole(mine.shape), whole(other.shape)],
        out_specs=whole(shape),
        scratch_shapes=[pltpu.VMEM((sources, left_rows, LANES), jnp.float32)],
        compiler_params=pltpu.CompilerParams(vmem_limit_bytes=48 * 1024 * 1024),
        name="prepare",
    )(mine, other)


def constants_kernel(c, rows, w_ref, bias_ref, message_ref, weights_ref, bias_out_ref, right_ref, w_f32):
    w_f32[...] = w_ref[...].astype(jnp.float32)
    for e in range(c):
        weights_ref[:, e * c:(e + 1) * c] = w_f32[pl.ds(e, c, stride=c), :].T.astype(jnp.bfloat16)
    bias_out_ref[...] = bias_ref[...]
    right_ref[...] = message_ref[:rows]


def constants(w_out, b_out, message, rows, c):
    z = w_out.shape[1]
    operands = (w_out, b_out.reshape(1, -1), message)
    outs = [((z, w_out.shape[0]), jnp.bfloat16), ((1, z), jnp.float32), ((rows, LANES), jnp.bfloat16)]
    return pl.pallas_call(
        functools.partial(constants_kernel, c, rows),
        grid=(1,),
        out_shape=[jax.ShapeDtypeStruct(*out) for out in outs],
        in_specs=[whole(a.shape) for a in operands],
        out_specs=[whole(out[0]) for out in outs],
        scratch_shapes=[pltpu.VMEM(w_out.shape, jnp.float32)],
        compiler_params=pltpu.CompilerParams(vmem_limit_bytes=48 * 1024 * 1024),
        name="constants",
    )(*operands)


def pair_kernel(seqs, c, right_at, left_ref, weights_ref, bias_ref, *refs):
    right_refs, (out_ref, right_f32, right_b, outer_ref) = refs[:-4], refs[-4:]
    rows_step = out_ref.shape[0]
    blocks = out_ref.shape[1] // LANES

    def block_of(n, at):
        array, first = right_at[n]
        return right_refs[array][first + at:first + at + c * seqs].astype(jnp.float32)

    @pl.when(pl.program_id(0) == 0)
    def _():
        for b in range(blocks):
            at = b * c * seqs
            right_of = sequence_rows(
                lambda n: block_of(n, at), right_f32, c, seqs)
            for e in range(c):
                lanes = (b * c + e) * LANES
                right_b[:, lanes:lanes + LANES] = right_of(e).astype(jnp.bfloat16)

    for b in range(blocks):
        for e in range(0, c, 2):
            at = (b * c + e) * LANES
            outer = jnp.dot(left_ref[...], right_b[:, at:at + 2 * LANES], preferred_element_type=jnp.float32)
            outer = outer.astype(jnp.bfloat16)
            for half in range(2):
                for i in range(rows_step):
                    outer_ref[i // 2, (e + half) * c:(e + half + 1) * c,
                              (i % 2) * LANES:(i % 2 + 1) * LANES] = (
                        outer[i * c:(i + 1) * c, half * LANES:(half + 1) * LANES])
        for p in range(rows_step // 2):
            update = jnp.dot(weights_ref[...], outer_ref[p], preferred_element_type=jnp.float32)
            for half in range(2):
                mine = update[:, half * LANES:(half + 1) * LANES].T + bias_ref[...]
                out_ref[2 * p + half, b * LANES:(b + 1) * LANES, :] = mine.astype(out_ref.dtype)


def pairs(left, weights, bias, rights, right_at, seqs, c, width):
    sources = len(right_at)
    z = weights.shape[0]
    rows = left.shape[0] // c
    rows_step = 8
    total = sources * seqs
    operands = (left, weights, bias, *rights)
    return pl.pallas_call(
        functools.partial(pair_kernel, seqs, c, right_at),
        grid=(rows // rows_step,),
        out_shape=jax.ShapeDtypeStruct((rows, width, z), jnp.bfloat16),
        in_specs=[pl.BlockSpec((rows_step * c, total), lambda i: (i, 0))] + [whole(a.shape) for a in operands[1:]],
        out_specs=pl.BlockSpec((rows_step, width, z), lambda i: (i, 0, 0)),
        scratch_shapes=[pltpu.VMEM((sources, c * seqs, LANES), jnp.float32),
                        pltpu.VMEM((total, width * c), jnp.bfloat16),
                        pltpu.VMEM((rows_step // 2, c * c, 2 * LANES), jnp.bfloat16)],
        compiler_params=pltpu.CompilerParams(vmem_limit_bytes=32 * 1024 * 1024),
        cost_estimate=pl.CostEstimate(flops=2 * rows * c * width * c * (total + z),
                                      bytes_accessed=2 * rows * width * z, transcendentals=0),
        name="pairs",
    )(*operands)


def source_at(here, step):
    return here ^ (2 * step[0] + step[1])


def direct_steps(chips):
    return [(a, 0) for a in range(1, chips)] + [(0, 1)]


def far_steps(chips):
    return [(a, 1) for a in range(chips // 2 - 1)]


def carries_far(step, chips):
    return step == (chips - 1, 0)


def fetch(array, step, count):
    return lax.ppermute(array, "row", [(source_at(r, step), r) for r in range(count)])


def fetch_far(array, step, count):
    chips = count // 2
    a, b = step
    moves = []
    for r in range(count):
        half = r // chips
        moves.append((2 * source_at(r, (a + 1, b)) + half, 2 * r + half))
        moves.append((2 * source_at(r, (a + chips // 2, b)) + half, 2 * r + 1 - half))
    return lax.ppermute(array, ("row", "col"), moves)


def on_device(alignment, ln_gain, ln_bias, w_left, b_left, w_right, b_right, w_out, b_out):
    seqs, width, _ = alignment.shape
    c = w_left.shape[1]
    row_count = lax.axis_size("row")
    col_count = lax.axis_size("col")
    own, *messages = features(alignment, ln_gain, ln_bias, w_left, b_left, w_right, b_right, row_count, col_count)
    along = row_count // 2
    direct = messages[:along]
    left_rows = own.shape[0]
    rows = direct[0].shape[0] - left_rows

    line = [fetch(message, step, row_count) for step, message in reversed([*zip(direct_steps(along), direct[:-1])])][::-1]
    across = fetch(direct[-1], (0, 1), row_count)
    beyond = [fetch_far(message, step, row_count) for step, message in zip(far_steps(along), messages[along:])]
    *near, last = line
    last, across = lax.optimization_barrier((last, across))
    last_far = fetch(last[left_rows:], (0, 1), row_count)
    *near, last_far = lax.optimization_barrier((*near, last_far))
    far = [fetch(block[:rows], (0, 1), row_count) for block in reversed(near)][::-1] + [last_far]

    message, _ = lax.optimization_barrier((direct[0], line[0]))
    weights, bias, right = constants(w_out, b_out, message, rows, c)
    held = [*near, last]
    line = held
    mine = jnp.concatenate([own] + [block[rows:] for block in held[:-1]] + [held[-1][:left_rows], across[rows:]]
                           + beyond + [far[-1][rows:]])
    other = lax.ppermute(mine, "col", [(0, 1), (1, 0)])
    half = along // 2
    left_at = [(a, True) for a in range(along + 1)]
    left_at += [(along + a, True) if a < half else (along + 1 + a - half, False) for a in range(1, along - 1)]
    left_at += [(along + half, True)]
    left = prepare(mine, other, left_at, left_rows, seqs)
    right_at = [(n, left_rows if n == along - 1 else 0) for n in range(row_count)]
    return pairs(left, weights, bias, [right, *line, across, *far], right_at, seqs, c, width)


def solution(mesh):
    in_specs = (P(("group", "row"), "col", None), P(), P(), P(), P(), P(), P(), P(), P())
    out_specs = P(("group", "row"), "col", None)
    return jax.shard_map(
        on_device, mesh=mesh, in_specs=in_specs, out_specs=out_specs, check_vma=False
    )
```

```python
import functools

import jax
import jax.numpy as jnp
from jax import lax
from jax.experimental import pallas as pl
from jax.experimental.pallas import tpu as pltpu
from jax.sharding import PartitionSpec as P

LANES = 128
VMEM_LIMIT = 60 * 1024 * 1024


def whole(shape):
    return pl.BlockSpec(shape, lambda i: (0,) * len(shape))


def features_kernel(scale, x_ref, gain_ref, bias_ref, wl_ref, bl_ref, wr_ref, br_ref,
                    *refs):
    outs, (normed_ref, left_f32, right_f32) = refs[:-3], refs[-3:]
    seqs, width, channels = x_ref.shape
    c = wl_ref.shape[0]
    blocks = width // LANES
    fold = LANES // c
    quarter = width // fold
    right_bias = jnp.broadcast_to(br_ref[...], (LANES, c)).T[:, :1]
    for s in range(seqs):
        values = x_ref[s].astype(jnp.float32)
        average = jnp.mean(values, axis=-1, keepdims=True)
        centred = values - average
        variance = jnp.mean(centred * centred, axis=-1, keepdims=True)
        normed = centred * lax.rsqrt(variance + 1e-05) * gain_ref[...] + bias_ref[...]
        for h in range(channels // LANES):
            normed_ref[h, s * width:(s + 1) * width] = normed[:, h * LANES:(h + 1) * LANES]
        right = lax.dot_general(wr_ref[...], normed.astype(jnp.bfloat16), (((1,), (1,)), ((), ())),
                                preferred_element_type=jnp.float32) + right_bias
        for b in range(blocks):
            right_f32[pl.ds(b * c * seqs + s, c, stride=seqs), :] = right[:, b * LANES:(b + 1) * LANES]
    total = None
    for q in range(fold):
        rows = jnp.concatenate(
            [normed_ref[h, pl.ds(q, seqs * quarter, stride=fold), :] for h in range(channels // LANES)], axis=1
        ).astype(jnp.bfloat16)
        zeros = [jnp.zeros((c, channels), jnp.bfloat16)]
        w = jnp.concatenate(zeros * q + [wl_ref[...]] + zeros * (fold - 1 - q), axis=0)
        term = lax.dot_general(rows, w, (((1,), (1,)), ((), ())), preferred_element_type=jnp.float32)
        total = term if total is None else total + term
    total = (total + jnp.concatenate([bl_ref[...]] * fold, axis=1)) * scale
    for s in range(seqs):
        left_f32[pl.ds(s, quarter, stride=seqs), :] = total[s * quarter:(s + 1) * quarter]
    own_ref, *message_refs = outs
    here = lax.axis_index("row")
    rows = own_ref.shape[0]
    chips = left_f32.shape[0] // rows

    def left_for(step):
        block = source_at(here, step) % chips
        return left_f32[pl.ds(pl.multiple_of(block * rows, rows), rows), :].astype(jnp.bfloat16)

    own_ref[...] = left_for((0, 0))
    right = right_f32[...].astype(jnp.bfloat16)
    core = lax.axis_index("col")
    for n, message_ref in enumerate(message_refs[:chips]):
        a, b = by_core(core, *(direct_steps(chips)[m] for m in sent_by(n)))
        first = message_ref.shape[0] - right.shape[0] - rows
        if first:
            message_ref[:rows] = left_for((a, b))
        message_ref[first:first + right.shape[0]] = right
        message_ref[first + right.shape[0]:] = left_for((a, 1) if first else (a, b))
    same_half = here // chips == lax.axis_index("col")
    for (a, b), message_ref in zip(far_steps(chips), message_refs[chips:]):
        message_ref[...] = jnp.where(same_half, left_for((a + 1, b)), left_for((a, b)))


def features(alignment, ln_gain, ln_bias, w_left, b_left, w_right, b_right, row_count, col_count):
    seqs, width, channels = alignment.shape
    c = w_left.shape[1]
    rows = seqs * width * c // LANES
    chips = row_count // col_count
    part = rows // chips
    shapes = [(part, LANES)]
    shapes += [(rows + part * (2 if n < 2 else 1), LANES) for n in range(chips)]
    shapes += [(part, LANES)] * len(far_steps(chips))
    operands = (alignment, ln_gain.reshape(1, -1), ln_bias.reshape(1, -1), w_left.T, b_left.reshape(1, -1),
                w_right.T, b_right.reshape(1, -1))
    return pl.pallas_call(
        functools.partial(features_kernel, 1.0 / (seqs * row_count)),
        grid=(1,),
        out_shape=[jax.ShapeDtypeStruct(shape, jnp.bfloat16) for shape in shapes],
        in_specs=[whole(a.shape) for a in operands],
        out_specs=[whole(shape) for shape in shapes],
        scratch_shapes=[pltpu.VMEM((channels // LANES, seqs * width, LANES), jnp.float32),
                        pltpu.VMEM((rows, LANES), jnp.float32),
                        pltpu.VMEM((rows, LANES), jnp.float32)],
        compiler_params=pltpu.CompilerParams(vmem_limit_bytes=VMEM_LIMIT),
        name="features",
    )(*operands)


def sequence_rows(block, f32_ref, inner, seqs):
    sources = f32_ref.shape[0]
    for n in range(sources):
        f32_ref[n] = block(n)
    if seqs % 8 == 0:
        return lambda m: jnp.concatenate(
            [f32_ref[n, m * seqs:(m + 1) * seqs] for n in range(sources)], axis=0)
    flat = f32_ref.reshape(sources * inner * seqs, LANES)
    return lambda m: jnp.concatenate(
        [flat[pl.ds(m * seqs + s, sources, stride=inner * seqs), :] for s in range(seqs)], axis=0)


def prepare_kernel(seqs, left_at, mine_ref, other_ref, left_ref, left_f32):
    sources, left_rows, _ = left_f32.shape
    same_half = lax.axis_index("row") // (sources // 2) == lax.axis_index("col")

    def block(n):
        first, of_same_half = left_at[n][0] * left_rows, left_at[n][1]
        mine = mine_ref[first:first + left_rows].astype(jnp.float32)
        other = other_ref[first:first + left_rows].astype(jnp.float32)
        return jnp.where(same_half == of_same_half, mine, other)

    left_of = sequence_rows(block, left_f32, left_rows // seqs, seqs)
    for k in range(left_rows // seqs):
        left_ref[k * LANES:(k + 1) * LANES] = left_of(k).T.astype(jnp.bfloat16)


def prepare(mine, other, left_at, left_rows, seqs):
    sources = len(left_at)
    shape = (left_rows // seqs * LANES, sources * seqs)
    return pl.pallas_call(
        functools.partial(prepare_kernel, seqs, left_at),
        grid=(1,),
        out_shape=jax.ShapeDtypeStruct(shape, jnp.bfloat16),
        in_specs=[whole(mine.shape), whole(other.shape)],
        out_specs=whole(shape),
        scratch_shapes=[pltpu.VMEM((sources, left_rows, LANES), jnp.float32)],
        compiler_params=pltpu.CompilerParams(vmem_limit_bytes=48 * 1024 * 1024),
        name="prepare",
    )(mine, other)


def constants_kernel(c, rows, w_ref, bias_ref, message_ref, weights_ref, bias_out_ref, right_ref, w_f32):
    w_f32[...] = w_ref[...].astype(jnp.float32)
    for e in range(c):
        weights_ref[:, e * c:(e + 1) * c] = w_f32[pl.ds(e, c, stride=c), :].T.astype(jnp.bfloat16)
    bias_out_ref[...] = bias_ref[...]
    right_ref[...] = message_ref[:rows]


def constants(w_out, b_out, message, rows, c):
    z = w_out.shape[1]
    operands = (w_out, b_out.reshape(1, -1), message)
    outs = [((z, w_out.shape[0]), jnp.bfloat16), ((1, z), jnp.float32), ((rows, LANES), jnp.bfloat16)]
    return pl.pallas_call(
        functools.partial(constants_kernel, c, rows),
        grid=(1,),
        out_shape=[jax.ShapeDtypeStruct(*out) for out in outs],
        in_specs=[whole(a.shape) for a in operands],
        out_specs=[whole(out[0]) for out in outs],
        scratch_shapes=[pltpu.VMEM(w_out.shape, jnp.float32)],
        compiler_params=pltpu.CompilerParams(vmem_limit_bytes=48 * 1024 * 1024),
        name="constants",
    )(*operands)


def pair_kernel(seqs, c, right_at, left_ref, weights_ref, bias_ref, *refs):
    right_refs, (out_ref, right_f32, right_b, outer_ref) = refs[:-4], refs[-4:]
    rows_step = out_ref.shape[0]
    blocks = out_ref.shape[1] // LANES

    def block_of(n, at):
        array, first = right_at[n]
        return right_refs[array][first + at:first + at + c * seqs].astype(jnp.float32)

    @pl.when(pl.program_id(0) == 0)
    def _():
        for b in range(blocks):
            at = b * c * seqs
            right_of = sequence_rows(
                lambda n: block_of(n, at), right_f32, c, seqs)
            for e in range(c):
                lanes = (b * c + e) * LANES
                right_b[:, lanes:lanes + LANES] = right_of(e).astype(jnp.bfloat16)

    for b in range(blocks):
        for e in range(0, c, 2):
            at = (b * c + e) * LANES
            outer = jnp.dot(left_ref[...], right_b[:, at:at + 2 * LANES], preferred_element_type=jnp.float32)
            outer = outer.astype(jnp.bfloat16)
            for half in range(2):
                for i in range(rows_step):
                    outer_ref[i // 2, (e + half) * c:(e + half + 1) * c,
                              (i % 2) * LANES:(i % 2 + 1) * LANES] = (
                        outer[i * c:(i + 1) * c, half * LANES:(half + 1) * LANES])
        for p in range(rows_step // 2):
            update = jnp.dot(weights_ref[...], outer_ref[p], preferred_element_type=jnp.float32)
            for half in range(2):
                mine = update[:, half * LANES:(half + 1) * LANES].T + bias_ref[...]
                out_ref[2 * p + half, b * LANES:(b + 1) * LANES, :] = mine.astype(out_ref.dtype)


def pairs(left, weights, bias, rights, right_at, seqs, c, width):
    sources = len(right_at)
    z = weights.shape[0]
    rows = left.shape[0] // c
    rows_step = 8
    total = sources * seqs
    operands = (left, weights, bias, *rights)
    return pl.pallas_call(
        functools.partial(pair_kernel, seqs, c, right_at),
        grid=(rows // rows_step,),
        out_shape=jax.ShapeDtypeStruct((rows, width, z), jnp.bfloat16),
        in_specs=[pl.BlockSpec((rows_step * c, total), lambda i: (i, 0))] + [whole(a.shape) for a in operands[1:]],
        out_specs=pl.BlockSpec((rows_step, width, z), lambda i: (i, 0, 0)),
        scratch_shapes=[pltpu.VMEM((sources, c * seqs, LANES), jnp.float32),
                        pltpu.VMEM((total, width * c), jnp.bfloat16),
                        pltpu.VMEM((rows_step // 2, c * c, 2 * LANES), jnp.bfloat16)],
        compiler_params=pltpu.CompilerParams(vmem_limit_bytes=32 * 1024 * 1024),
        cost_estimate=pl.CostEstimate(flops=2 * rows * c * width * c * (total + z),
                                      bytes_accessed=2 * rows * width * z, transcendentals=0),
        name="pairs",
    )(*operands)


def source_at(here, step):
    return here ^ (2 * step[0] + step[1])


def direct_steps(chips):
    return [(chips - 1, 0), (0, 1)] + [(a, 0) for a in reversed(range(1, chips - 1))]


def sent_by(n):
    return n, n ^ 1


def by_core(core, of_0, of_1):
    return jax.tree.map(lambda x, y: jnp.where(core == 0, x, y), of_0, of_1)


def far_steps(chips):
    return [(a, 1) for a in range(chips // 2 - 1)]


def fetch(array, step, count):
    return lax.ppermute(array, "row", [(source_at(r, step), r) for r in range(count)])


def fetch_direct(array, n, count):
    steps = direct_steps(count // 2)
    moves = [(2 * source_at(r, steps[m]) + core, 2 * r + core) for r in range(count) for core, m in enumerate(sent_by(n))]
    return lax.ppermute(array, ("row", "col"), moves)


def fetch_far(array, step, count):
    chips = count // 2
    a, b = step
    moves = []
    for r in range(count):
        half = r // chips
        moves.append((2 * source_at(r, (a + 1, b)) + half, 2 * r + half))
        moves.append((2 * source_at(r, (a + chips // 2, b)) + half, 2 * r + 1 - half))
    return lax.ppermute(array, ("row", "col"), moves)


def on_device(alignment, ln_gain, ln_bias, w_left, b_left, w_right, b_right, w_out, b_out):
    seqs, width, _ = alignment.shape
    c = w_left.shape[1]
    row_count = lax.axis_size("row")
    col_count = lax.axis_size("col")
    own, *messages = features(alignment, ln_gain, ln_bias, w_left, b_left, w_right, b_right, row_count, col_count)
    along = row_count // 2
    left_rows = own.shape[0]
    rows = messages[0].shape[0] - 2 * left_rows

    core = lax.axis_index("col")
    direct = [fetch_direct(message, n, row_count) for n, message in reversed([*enumerate(messages[:along])])][::-1]
    beyond = [fetch_far(message, step, row_count) for step, message in zip(far_steps(along), messages[along:])]
    last, across = by_core(core, (direct[0], direct[1]), (direct[1], direct[0]))
    last_far = fetch(last[left_rows:], (0, 1), row_count)
    *rest, last_far = lax.optimization_barrier((*direct[2:], last_far))
    rest = [by_core(core, *(rest[m] for m in sent_by(n))) for n in range(along - 2)]
    far = fetch(jnp.concatenate([block[:rows] for block in rest]), (0, 1), row_count)

    message, _ = lax.optimization_barrier((messages[along - 1], across))
    weights, bias, right = constants(w_out, b_out, message, rows, c)
    near = rest[::-1]
    mine = jnp.concatenate([own] + [block[rows:] for block in near] + [last[:left_rows], across[:left_rows]]
                           + beyond + [last_far[rows:]])
    other = lax.ppermute(mine, "col", [(0, 1), (1, 0)])
    half = along // 2
    left_at = [(a, True) for a in range(along + 1)]
    left_at += [(along + a, True) if a < half else (along + 1 + a - half, False) for a in range(1, along - 1)]
    left_at += [(along + half, True)]
    left = prepare(mine, other, left_at, left_rows, seqs)
    right_at = [(a, 0) for a in range(along - 1)] + [(along - 1, left_rows), (along, left_rows)]
    right_at += [(along + 1, (along - 2 - a) * rows) for a in range(1, along - 1)] + [(along + 2, 0)]
    return pairs(left, weights, bias, [right, *near, last, across, far, last_far], right_at, seqs, c, width)


def solution(mesh):
    in_specs = (P(("group", "row"), "col", None), P(), P(), P(), P(), P(), P(), P(), P())
    out_specs = P(("group", "row"), "col", None)
    return jax.shard_map(
        on_device, mesh=mesh, in_specs=in_specs, out_specs=out_specs, check_vma=False
    )
```

```python
import functools

import jax
import jax.numpy as jnp
from jax import lax
from jax.experimental import pallas as pl
from jax.experimental.pallas import tpu as pltpu
from jax.sharding import PartitionSpec as P

LANES = 128
VMEM_LIMIT = 60 * 1024 * 1024


def whole(shape):
    return pl.BlockSpec(shape, lambda i: (0,) * len(shape))


def features_kernel(scale, x_ref, gain_ref, bias_ref, wl_ref, bl_ref, wr_ref, br_ref,
                    *refs):
    outs, (normed_ref, left_f32, right_f32) = refs[:-3], refs[-3:]
    seqs, width, channels = x_ref.shape
    c = wl_ref.shape[0]
    blocks = width // LANES
    fold = LANES // c
    quarter = width // fold
    right_bias = jnp.broadcast_to(br_ref[...], (LANES, c)).T[:, :1]
    for s in range(seqs):
        values = x_ref[s].astype(jnp.float32)
        average = jnp.mean(values, axis=-1, keepdims=True)
        centred = values - average
        variance = jnp.mean(centred * centred, axis=-1, keepdims=True)
        normed = centred * lax.rsqrt(variance + 1e-05) * gain_ref[...] + bias_ref[...]
        for h in range(channels // LANES):
            normed_ref[h, s * width:(s + 1) * width] = normed[:, h * LANES:(h + 1) * LANES]
        right = lax.dot_general(wr_ref[...], normed.astype(jnp.bfloat16), (((1,), (1,)), ((), ())),
                                preferred_element_type=jnp.float32) + right_bias
        for b in range(blocks):
            right_f32[pl.ds(b * c * seqs + s, c, stride=seqs), :] = right[:, b * LANES:(b + 1) * LANES]
    total = None
    for q in range(fold):
        rows = jnp.concatenate(
            [normed_ref[h, pl.ds(q, seqs * quarter, stride=fold), :] for h in range(channels // LANES)], axis=1
        ).astype(jnp.bfloat16)
        zeros = [jnp.zeros((c, channels), jnp.bfloat16)]
        w = jnp.concatenate(zeros * q + [wl_ref[...]] + zeros * (fold - 1 - q), axis=0)
        term = lax.dot_general(rows, w, (((1,), (1,)), ((), ())), preferred_element_type=jnp.float32)
        total = term if total is None else total + term
    total = (total + jnp.concatenate([bl_ref[...]] * fold, axis=1)) * scale
    for s in range(seqs):
        left_f32[pl.ds(s, quarter, stride=seqs), :] = total[s * quarter:(s + 1) * quarter]
    own_ref, *message_refs = outs
    here = lax.axis_index("row")
    rows = own_ref.shape[0]
    chips = left_f32.shape[0] // rows

    def left_for(step):
        block = source_at(here, step) % chips
        return left_f32[pl.ds(pl.multiple_of(block * rows, rows), rows), :].astype(jnp.bfloat16)

    own_ref[...] = left_for((0, 0))
    right = right_f32[...].astype(jnp.bfloat16)
    core = lax.axis_index("col")
    for n, message_ref in enumerate(message_refs[:chips]):
        a, b = by_core(core, *(direct_steps(chips)[m] for m in sent_by(n)))
        first = message_ref.shape[0] - right.shape[0] - rows
        if first:
            message_ref[:rows] = left_for((a, b))
        message_ref[first:first + right.shape[0]] = right
        message_ref[first + right.shape[0]:] = left_for((a, 1) if first else (a, b))
    same_half = here // chips == lax.axis_index("col")
    for (a, b), message_ref in zip(far_steps(chips), message_refs[chips:]):
        message_ref[...] = jnp.where(same_half, left_for((a + 1, b)), left_for((a, b)))


def features(alignment, ln_gain, ln_bias, w_left, b_left, w_right, b_right, row_count, col_count):
    seqs, width, channels = alignment.shape
    c = w_left.shape[1]
    rows = seqs * width * c // LANES
    chips = row_count // col_count
    part = rows // chips
    shapes = [(part, LANES)]
    shapes += [(rows + part * (2 if n < 2 else 1), LANES) for n in range(chips)]
    shapes += [(part, LANES)] * len(far_steps(chips))
    operands = (alignment, ln_gain.reshape(1, -1), ln_bias.reshape(1, -1), w_left.T, b_left.reshape(1, -1),
                w_right.T, b_right.reshape(1, -1))
    return pl.pallas_call(
        functools.partial(features_kernel, 1.0 / (seqs * row_count)),
        grid=(1,),
        out_shape=[jax.ShapeDtypeStruct(shape, jnp.bfloat16) for shape in shapes],
        in_specs=[whole(a.shape) for a in operands],
        out_specs=[whole(shape) for shape in shapes],
        scratch_shapes=[pltpu.VMEM((channels // LANES, seqs * width, LANES), jnp.float32),
                        pltpu.VMEM((rows, LANES), jnp.float32),
                        pltpu.VMEM((rows, LANES), jnp.float32)],
        compiler_params=pltpu.CompilerParams(vmem_limit_bytes=VMEM_LIMIT),
        name="features",
    )(*operands)


def sequence_rows(block, f32_ref, inner, seqs):
    sources = f32_ref.shape[0]
    for n in range(sources):
        f32_ref[n] = block(n)
    if seqs % 8 == 0:
        return lambda m: jnp.concatenate(
            [f32_ref[n, m * seqs:(m + 1) * seqs] for n in range(sources)], axis=0)
    flat = f32_ref.reshape(sources * inner * seqs, LANES)
    return lambda m: jnp.concatenate(
        [flat[pl.ds(m * seqs + s, sources, stride=inner * seqs), :] for s in range(seqs)], axis=0)


def prepare_kernel(seqs, left_at, mine_ref, other_ref, left_ref, left_f32):
    sources, left_rows, _ = left_f32.shape
    same_half = lax.axis_index("row") // (sources // 2) == lax.axis_index("col")

    def block(n):
        first, of_same_half = left_at[n][0] * left_rows, left_at[n][1]
        mine = mine_ref[first:first + left_rows].astype(jnp.float32)
        other = other_ref[first:first + left_rows].astype(jnp.float32)
        return jnp.where(same_half == of_same_half, mine, other)

    left_of = sequence_rows(block, left_f32, left_rows // seqs, seqs)
    for k in range(left_rows // seqs):
        left_ref[k * LANES:(k + 1) * LANES] = left_of(k).T.astype(jnp.bfloat16)


def prepare(mine, other, left_at, left_rows, seqs):
    sources = len(left_at)
    shape = (left_rows // seqs * LANES, sources * seqs)
    return pl.pallas_call(
        functools.partial(prepare_kernel, seqs, left_at),
        grid=(1,),
        out_shape=jax.ShapeDtypeStruct(shape, jnp.bfloat16),
        in_specs=[whole(mine.shape), whole(other.shape)],
        out_specs=whole(shape),
        scratch_shapes=[pltpu.VMEM((sources, left_rows, LANES), jnp.float32)],
        compiler_params=pltpu.CompilerParams(vmem_limit_bytes=48 * 1024 * 1024),
        name="prepare",
    )(mine, other)


def constants_kernel(c, rows, w_ref, bias_ref, message_ref, weights_ref, bias_out_ref, right_ref, w_f32):
    w_f32[...] = w_ref[...].astype(jnp.float32)
    for e in range(c):
        weights_ref[:, e * c:(e + 1) * c] = w_f32[pl.ds(e, c, stride=c), :].T.astype(jnp.bfloat16)
    bias_out_ref[...] = bias_ref[...]
    right_ref[...] = message_ref[:rows]


def constants(w_out, b_out, message, rows, c):
    z = w_out.shape[1]
    operands = (w_out, b_out.reshape(1, -1), message)
    outs = [((z, w_out.shape[0]), jnp.bfloat16), ((1, z), jnp.float32), ((rows, LANES), jnp.bfloat16)]
    return pl.pallas_call(
        functools.partial(constants_kernel, c, rows),
        grid=(1,),
        out_shape=[jax.ShapeDtypeStruct(*out) for out in outs],
        in_specs=[whole(a.shape) for a in operands],
        out_specs=[whole(out[0]) for out in outs],
        scratch_shapes=[pltpu.VMEM(w_out.shape, jnp.float32)],
        compiler_params=pltpu.CompilerParams(vmem_limit_bytes=48 * 1024 * 1024),
        name="constants",
    )(*operands)


def pair_kernel(seqs, c, right_at, left_ref, weights_ref, bias_ref, *refs):
    right_refs, (out_ref, right_f32, right_b, outer_ref) = refs[:-4], refs[-4:]
    rows_step = out_ref.shape[0]
    blocks = out_ref.shape[1] // LANES

    def block_of(n, at):
        array, first = right_at[n]
        return right_refs[array][first + at:first + at + c * seqs].astype(jnp.float32)

    @pl.when(pl.program_id(0) == 0)
    def _():
        for b in range(blocks):
            at = b * c * seqs
            right_of = sequence_rows(
                lambda n: block_of(n, at), right_f32, c, seqs)
            for e in range(c):
                lanes = (b * c + e) * LANES
                right_b[:, lanes:lanes + LANES] = right_of(e).astype(jnp.bfloat16)

    for b in range(blocks):
        for e in range(0, c, 2):
            at = (b * c + e) * LANES
            outer = jnp.dot(left_ref[...], right_b[:, at:at + 2 * LANES], preferred_element_type=jnp.float32)
            outer = outer.astype(jnp.bfloat16)
            for half in range(2):
                for i in range(rows_step):
                    outer_ref[i // 2, (e + half) * c:(e + half + 1) * c,
                              (i % 2) * LANES:(i % 2 + 1) * LANES] = (
                        outer[i * c:(i + 1) * c, half * LANES:(half + 1) * LANES])
        for p in range(rows_step // 2):
            update = jnp.dot(weights_ref[...], outer_ref[p], preferred_element_type=jnp.float32)
            for half in range(2):
                mine = update[:, half * LANES:(half + 1) * LANES].T + bias_ref[...]
                out_ref[2 * p + half, b * LANES:(b + 1) * LANES, :] = mine.astype(out_ref.dtype)


def pairs(left, weights, bias, rights, right_at, seqs, c, width):
    sources = len(right_at)
    z = weights.shape[0]
    rows = left.shape[0] // c
    rows_step = 8
    total = sources * seqs
    operands = (left, weights, bias, *rights)
    return pl.pallas_call(
        functools.partial(pair_kernel, seqs, c, right_at),
        grid=(rows // rows_step,),
        out_shape=jax.ShapeDtypeStruct((rows, width, z), jnp.bfloat16),
        in_specs=[pl.BlockSpec((rows_step * c, total), lambda i: (i, 0))] + [whole(a.shape) for a in operands[1:]],
        out_specs=pl.BlockSpec((rows_step, width, z), lambda i: (i, 0, 0)),
        scratch_shapes=[pltpu.VMEM((sources, c * seqs, LANES), jnp.float32),
                        pltpu.VMEM((total, width * c), jnp.bfloat16),
                        pltpu.VMEM((rows_step // 2, c * c, 2 * LANES), jnp.bfloat16)],
        compiler_params=pltpu.CompilerParams(vmem_limit_bytes=32 * 1024 * 1024),
        cost_estimate=pl.CostEstimate(flops=2 * rows * c * width * c * (total + z),
                                      bytes_accessed=2 * rows * width * z, transcendentals=0),
        name="pairs",
    )(*operands)


def source_at(here, step):
    return here ^ (2 * step[0] + step[1])


def direct_steps(chips):
    return [(chips - 1, 0), (0, 1)] + [(a, 0) for a in reversed(range(1, chips - 1))]


def sent_by(n):
    return n, n ^ 1


def by_core(core, of_0, of_1):
    return jax.tree.map(lambda x, y: jnp.where(core == 0, x, y), of_0, of_1)


def far_steps(chips):
    return [(a, 1) for a in range(chips // 2 - 1)]


def fetch(array, step, count):
    return lax.ppermute(array, "row", [(source_at(r, step), r) for r in range(count)])


def fetch_direct(array, n, count):
    steps = direct_steps(count // 2)
    moves = [(2 * source_at(r, steps[m]) + core, 2 * r + core) for r in range(count) for core, m in enumerate(sent_by(n))]
    return lax.ppermute(array, ("row", "col"), moves)


def fetch_far(array, step, count):
    chips = count // 2
    a, b = step
    moves = []
    for r in range(count):
        half = r // chips
        moves.append((2 * source_at(r, (a + 1, b)) + half, 2 * r + half))
        moves.append((2 * source_at(r, (a + chips // 2, b)) + half, 2 * r + 1 - half))
    return lax.ppermute(array, ("row", "col"), moves)


def on_device(alignment, ln_gain, ln_bias, w_left, b_left, w_right, b_right, w_out, b_out):
    seqs, width, _ = alignment.shape
    c = w_left.shape[1]
    row_count = lax.axis_size("row")
    col_count = lax.axis_size("col")
    own, *messages = features(alignment, ln_gain, ln_bias, w_left, b_left, w_right, b_right, row_count, col_count)
    along = row_count // 2
    left_rows = own.shape[0]
    rows = messages[0].shape[0] - 2 * left_rows

    core = lax.axis_index("col")
    direct = [fetch_direct(message, n, row_count) for n, message in reversed([*enumerate(messages[:along])])][::-1]
    messages[along:], direct[:2] = lax.optimization_barrier((messages[along:], direct[:2]))
    beyond = [fetch_far(message, step, row_count) for step, message in zip(far_steps(along), messages[along:])]
    last, across = by_core(core, (direct[0], direct[1]), (direct[1], direct[0]))
    last_far = fetch(last[left_rows:], (0, 1), row_count)
    *rest, last_far = lax.optimization_barrier((*direct[2:], last_far))
    rest = [by_core(core, *(rest[m] for m in sent_by(n))) for n in range(along - 2)]
    far = fetch(jnp.concatenate([block[:rows] for block in rest]), (0, 1), row_count)

    message, _ = lax.optimization_barrier((messages[along - 1], across))
    weights, bias, right = constants(w_out, b_out, message, rows, c)
    near = rest[::-1]
    mine = jnp.concatenate([own] + [block[rows:] for block in near] + [last[:left_rows], across[:left_rows]]
                           + beyond + [last_far[rows:]])
    other = lax.ppermute(mine, "col", [(0, 1), (1, 0)])
    half = along // 2
    left_at = [(a, True) for a in range(along + 1)]
    left_at += [(along + a, True) if a < half else (along + 1 + a - half, False) for a in range(1, along - 1)]
    left_at += [(along + half, True)]
    left = prepare(mine, other, left_at, left_rows, seqs)
    right_at = [(a, 0) for a in range(along - 1)] + [(along - 1, left_rows), (along, left_rows)]
    right_at += [(along + 1, (along - 2 - a) * rows) for a in range(1, along - 1)] + [(along + 2, 0)]
    return pairs(left, weights, bias, [right, *near, last, across, far, last_far], right_at, seqs, c, width)


def solution(mesh):
    in_specs = (P(("group", "row"), "col", None), P(), P(), P(), P(), P(), P(), P(), P())
    out_specs = P(("group", "row"), "col", None)
    return jax.shard_map(
        on_device, mesh=mesh, in_specs=in_specs, out_specs=out_specs, check_vma=False
    )
```

```python
import functools

import jax
import jax.numpy as jnp
from jax import lax
from jax.experimental import pallas as pl
from jax.experimental.pallas import tpu as pltpu
from jax.sharding import PartitionSpec as P

LANES = 128
VMEM_LIMIT = 60 * 1024 * 1024


def whole(shape):
    return pl.BlockSpec(shape, lambda i: (0,) * len(shape))


def features_kernel(scale, x_ref, gain_ref, bias_ref, wl_ref, bl_ref, wr_ref, br_ref,
                    *refs):
    outs, (normed_ref, left_f32, right_f32) = refs[:-3], refs[-3:]
    seqs, width, channels = x_ref.shape
    c = wl_ref.shape[0]
    blocks = width // LANES
    fold = LANES // c
    quarter = width // fold
    right_bias = jnp.broadcast_to(br_ref[...], (LANES, c)).T[:, :1]
    for s in range(seqs):
        values = x_ref[s].astype(jnp.float32)
        average = jnp.mean(values, axis=-1, keepdims=True)
        centred = values - average
        variance = jnp.mean(centred * centred, axis=-1, keepdims=True)
        normed = centred * lax.rsqrt(variance + 1e-05) * gain_ref[...] + bias_ref[...]
        for h in range(channels // LANES):
            normed_ref[h, s * width:(s + 1) * width] = normed[:, h * LANES:(h + 1) * LANES]
        right = lax.dot_general(wr_ref[...], normed.astype(jnp.bfloat16), (((1,), (1,)), ((), ())),
                                preferred_element_type=jnp.float32) + right_bias
        for b in range(blocks):
            right_f32[pl.ds(b * c * seqs + s, c, stride=seqs), :] = right[:, b * LANES:(b + 1) * LANES]
    total = None
    for q in range(fold):
        rows = jnp.concatenate(
            [normed_ref[h, pl.ds(q, seqs * quarter, stride=fold), :] for h in range(channels // LANES)], axis=1
        ).astype(jnp.bfloat16)
        zeros = [jnp.zeros((c, channels), jnp.bfloat16)]
        w = jnp.concatenate(zeros * q + [wl_ref[...]] + zeros * (fold - 1 - q), axis=0)
        term = lax.dot_general(rows, w, (((1,), (1,)), ((), ())), preferred_element_type=jnp.float32)
        total = term if total is None else total + term
    total = (total + jnp.concatenate([bl_ref[...]] * fold, axis=1)) * scale
    for s in range(seqs):
        left_f32[pl.ds(s, quarter, stride=seqs), :] = total[s * quarter:(s + 1) * quarter]
    own_ref, *message_refs = outs
    here = lax.axis_index("row")
    rows = own_ref.shape[0]
    chips = left_f32.shape[0] // rows

    def left_for(step):
        block = source_at(here, step) % chips
        return left_f32[pl.ds(pl.multiple_of(block * rows, rows), rows), :].astype(jnp.bfloat16)

    own_ref[...] = left_for((0, 0))
    right = right_f32[...].astype(jnp.bfloat16)
    core = lax.axis_index("col")
    for n, message_ref in enumerate(message_refs):
        a, b = by_core(core, *(direct_steps(chips)[m] for m in sent_by(n)))
        message_ref[:rows] = left_for((a, b))
        message_ref[rows:rows + right.shape[0]] = right
        message_ref[rows + right.shape[0]:] = left_for((a, 1))


def features(alignment, ln_gain, ln_bias, w_left, b_left, w_right, b_right, row_count, col_count):
    seqs, width, channels = alignment.shape
    c = w_left.shape[1]
    rows = seqs * width * c // LANES
    chips = row_count // col_count
    part = rows // chips
    shapes = [(part, LANES)] + [(rows + 2 * part, LANES)] * chips
    operands = (alignment, ln_gain.reshape(1, -1), ln_bias.reshape(1, -1), w_left.T, b_left.reshape(1, -1),
                w_right.T, b_right.reshape(1, -1))
    return pl.pallas_call(
        functools.partial(features_kernel, 1.0 / (seqs * row_count)),
        grid=(1,),
        out_shape=[jax.ShapeDtypeStruct(shape, jnp.bfloat16) for shape in shapes],
        in_specs=[whole(a.shape) for a in operands],
        out_specs=[whole(shape) for shape in shapes],
        scratch_shapes=[pltpu.VMEM((channels // LANES, seqs * width, LANES), jnp.float32),
                        pltpu.VMEM((rows, LANES), jnp.float32),
                        pltpu.VMEM((rows, LANES), jnp.float32)],
        compiler_params=pltpu.CompilerParams(vmem_limit_bytes=VMEM_LIMIT),
        name="features",
    )(*operands)


def sequence_rows(block, f32_ref, inner, seqs):
    sources = f32_ref.shape[0]
    for n in range(sources):
        f32_ref[n] = block(n)
    if seqs % 8 == 0:
        return lambda m: jnp.concatenate(
            [f32_ref[n, m * seqs:(m + 1) * seqs] for n in range(sources)], axis=0)
    flat = f32_ref.reshape(sources * inner * seqs, LANES)
    return lambda m: jnp.concatenate(
        [flat[pl.ds(m * seqs + s, sources, stride=inner * seqs), :] for s in range(seqs)], axis=0)


def prepare_kernel(seqs, mine_ref, other_ref, left_ref, left_f32):
    sources, left_rows, _ = left_f32.shape
    same_half = lax.axis_index("row") // (sources // 2) == lax.axis_index("col")

    def block(n):
        first = n * left_rows
        mine = mine_ref[first:first + left_rows].astype(jnp.float32)
        other = other_ref[first:first + left_rows].astype(jnp.float32)
        return jnp.where(same_half, mine, other)

    left_of = sequence_rows(block, left_f32, left_rows // seqs, seqs)
    for k in range(left_rows // seqs):
        left_ref[k * LANES:(k + 1) * LANES] = left_of(k).T.astype(jnp.bfloat16)


def prepare(mine, other, sources, seqs):
    left_rows = mine.shape[0] // sources
    shape = (left_rows // seqs * LANES, sources * seqs)
    return pl.pallas_call(
        functools.partial(prepare_kernel, seqs),
        grid=(1,),
        out_shape=jax.ShapeDtypeStruct(shape, jnp.bfloat16),
        in_specs=[whole(mine.shape), whole(other.shape)],
        out_specs=whole(shape),
        scratch_shapes=[pltpu.VMEM((sources, left_rows, LANES), jnp.float32)],
        compiler_params=pltpu.CompilerParams(vmem_limit_bytes=48 * 1024 * 1024),
        name="prepare",
    )(mine, other)


def constants_kernel(c, first, w_ref, bias_ref, message_ref, weights_ref, bias_out_ref, right_ref, w_f32):
    w_f32[...] = w_ref[...].astype(jnp.float32)
    for e in range(c):
        weights_ref[:, e * c:(e + 1) * c] = w_f32[pl.ds(e, c, stride=c), :].T.astype(jnp.bfloat16)
    bias_out_ref[...] = bias_ref[...]
    right_ref[...] = message_ref[first:first + right_ref.shape[0]]


def constants(w_out, b_out, message, first, rows, c):
    z = w_out.shape[1]
    operands = (w_out, b_out.reshape(1, -1), message)
    outs = [((z, w_out.shape[0]), jnp.bfloat16), ((1, z), jnp.float32), ((rows, LANES), jnp.bfloat16)]
    return pl.pallas_call(
        functools.partial(constants_kernel, c, first),
        grid=(1,),
        out_shape=[jax.ShapeDtypeStruct(*out) for out in outs],
        in_specs=[whole(a.shape) for a in operands],
        out_specs=[whole(out[0]) for out in outs],
        scratch_shapes=[pltpu.VMEM(w_out.shape, jnp.float32)],
        compiler_params=pltpu.CompilerParams(vmem_limit_bytes=48 * 1024 * 1024),
        name="constants",
    )(*operands)


def pair_kernel(seqs, c, right_at, left_ref, weights_ref, bias_ref, *refs):
    right_refs, (out_ref, right_f32, right_b, outer_ref) = refs[:-4], refs[-4:]
    rows_step = out_ref.shape[0]
    blocks = out_ref.shape[1] // LANES

    def block_of(n, at):
        array, first = right_at[n]
        return right_refs[array][first + at:first + at + c * seqs].astype(jnp.float32)

    @pl.when(pl.program_id(0) == 0)
    def _():
        for b in range(blocks):
            at = b * c * seqs
            right_of = sequence_rows(
                lambda n: block_of(n, at), right_f32, c, seqs)
            for e in range(c):
                lanes = (b * c + e) * LANES
                right_b[:, lanes:lanes + LANES] = right_of(e).astype(jnp.bfloat16)

    for b in range(blocks):
        for e in range(0, c, 2):
            at = (b * c + e) * LANES
            outer = jnp.dot(left_ref[...], right_b[:, at:at + 2 * LANES], preferred_element_type=jnp.float32)
            outer = outer.astype(jnp.bfloat16)
            for half in range(2):
                for i in range(rows_step):
                    outer_ref[i // 2, (e + half) * c:(e + half + 1) * c,
                              (i % 2) * LANES:(i % 2 + 1) * LANES] = (
                        outer[i * c:(i + 1) * c, half * LANES:(half + 1) * LANES])
        for p in range(rows_step // 2):
            update = jnp.dot(weights_ref[...], outer_ref[p], preferred_element_type=jnp.float32)
            for half in range(2):
                mine = update[:, half * LANES:(half + 1) * LANES].T + bias_ref[...]
                out_ref[2 * p + half, b * LANES:(b + 1) * LANES, :] = mine.astype(out_ref.dtype)


def pairs(left, weights, bias, rights, right_at, seqs, c, width):
    sources = len(right_at)
    z = weights.shape[0]
    rows = left.shape[0] // c
    rows_step = 16
    total = sources * seqs
    operands = (left, weights, bias, *rights)
    return pl.pallas_call(
        functools.partial(pair_kernel, seqs, c, right_at),
        grid=(rows // rows_step,),
        out_shape=jax.ShapeDtypeStruct((rows, width, z), jnp.bfloat16),
        in_specs=[pl.BlockSpec((rows_step * c, total), lambda i: (i, 0))] + [whole(a.shape) for a in operands[1:]],
        out_specs=pl.BlockSpec((rows_step, width, z), lambda i: (i, 0, 0)),
        scratch_shapes=[pltpu.VMEM((sources, c * seqs, LANES), jnp.float32),
                        pltpu.VMEM((total, width * c), jnp.bfloat16),
                        pltpu.VMEM((rows_step // 2, c * c, 2 * LANES), jnp.bfloat16)],
        compiler_params=pltpu.CompilerParams(vmem_limit_bytes=32 * 1024 * 1024),
        cost_estimate=pl.CostEstimate(flops=2 * rows * c * width * c * (total + z),
                                      bytes_accessed=2 * rows * width * z, transcendentals=0),
        name="pairs",
    )(*operands)


def source_at(here, step):
    return here ^ (2 * step[0] + step[1])


def direct_steps(chips):
    return [(chips - 1, 0), (0, 1)] + [(a, 0) for a in reversed(range(1, chips - 1))]


def sent_by(n):
    return n, n ^ 1


def by_core(core, of_0, of_1):
    return jax.tree.map(lambda x, y: jnp.where(core == 0, x, y), of_0, of_1)


def fetch(array, step, count):
    return lax.ppermute(array, "row", [(source_at(r, step), r) for r in range(count)])


def fetch_direct(array, n, count):
    steps = direct_steps(count // 2)
    moves = [(2 * source_at(r, steps[m]) + core, 2 * r + core) for r in range(count) for core, m in enumerate(sent_by(n))]
    return lax.ppermute(array, ("row", "col"), moves)


def on_device(alignment, ln_gain, ln_bias, w_left, b_left, w_right, b_right, w_out, b_out):
    seqs, width, _ = alignment.shape
    c = w_left.shape[1]
    row_count = lax.axis_size("row")
    col_count = lax.axis_size("col")
    own, *messages = features(alignment, ln_gain, ln_bias, w_left, b_left, w_right, b_right, row_count, col_count)
    along = row_count // 2
    left_rows = own.shape[0]
    rows = messages[0].shape[0] - 2 * left_rows

    core = lax.axis_index("col")
    direct = [fetch_direct(message, n, row_count) for n, message in reversed([*enumerate(messages)])][::-1]
    last, across = by_core(core, (direct[0], direct[1]), (direct[1], direct[0]))
    last_far = fetch(last[left_rows:], (0, 1), row_count)
    *rest, last_far = lax.optimization_barrier((*direct[2:], last_far))
    near = [by_core(core, *(rest[m] for m in sent_by(n))) for n in range(along - 2)][::-1]
    far = fetch(jnp.concatenate([block[left_rows:] for block in near]), (0, 1), row_count)

    message, _ = lax.optimization_barrier((messages[-1], across))
    weights, bias, right = constants(w_out, b_out, message, left_rows, rows, c)
    far_at = [n * (rows + left_rows) for n in range(along - 2)]
    mine = jnp.concatenate([own] + [block[:left_rows] for block in (*near, last, across)]
                           + [far[at + rows:at + rows + left_rows] for at in far_at] + [last_far[rows:]])
    other = lax.ppermute(mine, "col", [(0, 1), (1, 0)])
    left = prepare(mine, other, row_count, seqs)
    right_at = [(0, 0)] + [(n, left_rows) for n in range(1, along + 1)]
    right_at += [(along + 1, at) for at in far_at] + [(along + 2, 0)]
    return pairs(left, weights, bias, [right, *near, last, across, far, last_far], right_at, seqs, c, width)


def solution(mesh):
    in_specs = (P(("group", "row"), "col", None), P(), P(), P(), P(), P(), P(), P(), P())
    out_specs = P(("group", "row"), "col", None)
    return jax.shard_map(
        on_device, mesh=mesh, in_specs=in_specs, out_specs=out_specs, check_vma=False
    )
```

```python
import functools

import jax
import jax.numpy as jnp
from jax import lax
from jax.experimental import pallas as pl
from jax.experimental.pallas import tpu as pltpu
from jax.sharding import PartitionSpec as P

LANES = 128
VMEM_LIMIT = 60 * 1024 * 1024


def whole(shape):
    return pl.BlockSpec(shape, lambda i: (0,) * len(shape))


def features_kernel(scale, x_ref, gain_ref, bias_ref, wl_ref, bl_ref, wr_ref, br_ref,
                    *refs):
    outs, (normed_ref, left_f32, right_f32) = refs[:-3], refs[-3:]
    seqs, width, channels = x_ref.shape
    c = wl_ref.shape[0]
    blocks = width // LANES
    fold = LANES // c
    quarter = width // fold
    right_bias = jnp.broadcast_to(br_ref[...], (LANES, c)).T[:, :1]
    for s in range(seqs):
        values = x_ref[s].astype(jnp.float32)
        average = jnp.mean(values, axis=-1, keepdims=True)
        centred = values - average
        variance = jnp.mean(centred * centred, axis=-1, keepdims=True)
        normed = centred * lax.rsqrt(variance + 1e-05) * gain_ref[...] + bias_ref[...]
        for h in range(channels // LANES):
            normed_ref[h, s * width:(s + 1) * width] = normed[:, h * LANES:(h + 1) * LANES]
        right = lax.dot_general(wr_ref[...], normed.astype(jnp.bfloat16), (((1,), (1,)), ((), ())),
                                preferred_element_type=jnp.float32) + right_bias
        for b in range(blocks):
            right_f32[pl.ds(b * c * seqs + s, c, stride=seqs), :] = right[:, b * LANES:(b + 1) * LANES]
    total = None
    for q in range(fold):
        rows = jnp.concatenate(
            [normed_ref[h, pl.ds(q, seqs * quarter, stride=fold), :] for h in range(channels // LANES)], axis=1
        ).astype(jnp.bfloat16)
        zeros = [jnp.zeros((c, channels), jnp.bfloat16)]
        w = jnp.concatenate(zeros * q + [wl_ref[...]] + zeros * (fold - 1 - q), axis=0)
        term = lax.dot_general(rows, w, (((1,), (1,)), ((), ())), preferred_element_type=jnp.float32)
        total = term if total is None else total + term
    total = (total + jnp.concatenate([bl_ref[...]] * fold, axis=1)) * scale
    for s in range(seqs):
        left_f32[pl.ds(s, quarter, stride=seqs), :] = total[s * quarter:(s + 1) * quarter]
    own_ref, *message_refs = outs
    here = lax.axis_index("row")
    rows = own_ref.shape[0]
    chips = left_f32.shape[0] // rows

    def left_for(step):
        block = source_at(here, step) % chips
        return left_f32[pl.ds(pl.multiple_of(block * rows, rows), rows), :].astype(jnp.bfloat16)

    own_ref[...] = left_for((0, 0))
    right = right_f32[...].astype(jnp.bfloat16)
    core = lax.axis_index("col")
    for n, message_ref in enumerate(message_refs[:chips]):
        a, b = by_core(core, *(direct_steps(chips)[m] for m in sent_by(n)))
        first = message_ref.shape[0] - right.shape[0] - rows
        if first:
            message_ref[:rows] = left_for((a, b))
        message_ref[first:first + right.shape[0]] = right
        message_ref[first + right.shape[0]:] = left_for((a, 1) if first else (a, b))
    same_half = here // chips == lax.axis_index("col")
    for (a, b), message_ref in zip(far_steps(chips), message_refs[chips:]):
        message_ref[...] = jnp.where(same_half, left_for((a + 1, b)), left_for((a, b)))


def features(alignment, ln_gain, ln_bias, w_left, b_left, w_right, b_right, row_count, col_count):
    seqs, width, channels = alignment.shape
    c = w_left.shape[1]
    rows = seqs * width * c // LANES
    chips = row_count // col_count
    part = rows // chips
    shapes = [(part, LANES)]
    shapes += [(rows + part * (2 if n < 2 else 1), LANES) for n in range(chips)]
    shapes += [(part, LANES)] * len(far_steps(chips))
    operands = (alignment, ln_gain.reshape(1, -1), ln_bias.reshape(1, -1), w_left.T, b_left.reshape(1, -1),
                w_right.T, b_right.reshape(1, -1))
    return pl.pallas_call(
        functools.partial(features_kernel, 1.0 / (seqs * row_count)),
        grid=(1,),
        out_shape=[jax.ShapeDtypeStruct(shape, jnp.bfloat16) for shape in shapes],
        in_specs=[whole(a.shape) for a in operands],
        out_specs=[whole(shape) for shape in shapes],
        scratch_shapes=[pltpu.VMEM((channels // LANES, seqs * width, LANES), jnp.float32),
                        pltpu.VMEM((rows, LANES), jnp.float32),
                        pltpu.VMEM((rows, LANES), jnp.float32)],
        compiler_params=pltpu.CompilerParams(vmem_limit_bytes=VMEM_LIMIT),
        name="features",
    )(*operands)


def sequence_rows(block, f32_ref, inner, seqs):
    sources = f32_ref.shape[0]
    for n in range(sources):
        f32_ref[n] = block(n)
    if seqs % 8 == 0:
        return lambda m: jnp.concatenate(
            [f32_ref[n, m * seqs:(m + 1) * seqs] for n in range(sources)], axis=0)
    flat = f32_ref.reshape(sources * inner * seqs, LANES)
    return lambda m: jnp.concatenate(
        [flat[pl.ds(m * seqs + s, sources, stride=inner * seqs), :] for s in range(seqs)], axis=0)


def prepare_kernel(seqs, left_at, mine_ref, other_ref, left_ref, left_f32):
    sources, left_rows, _ = left_f32.shape
    same_half = lax.axis_index("row") // (sources // 2) == lax.axis_index("col")

    def block(n):
        first, of_same_half = left_at[n][0] * left_rows, left_at[n][1]
        mine = mine_ref[first:first + left_rows].astype(jnp.float32)
        other = other_ref[first:first + left_rows].astype(jnp.float32)
        return jnp.where(same_half == of_same_half, mine, other)

    left_of = sequence_rows(block, left_f32, left_rows // seqs, seqs)
    for k in range(left_rows // seqs):
        left_ref[k * LANES:(k + 1) * LANES] = left_of(k).T.astype(jnp.bfloat16)


def prepare(mine, other, left_at, left_rows, seqs):
    sources = len(left_at)
    shape = (left_rows // seqs * LANES, sources * seqs)
    return pl.pallas_call(
        functools.partial(prepare_kernel, seqs, left_at),
        grid=(1,),
        out_shape=jax.ShapeDtypeStruct(shape, jnp.bfloat16),
        in_specs=[whole(mine.shape), whole(other.shape)],
        out_specs=whole(shape),
        scratch_shapes=[pltpu.VMEM((sources, left_rows, LANES), jnp.float32)],
        compiler_params=pltpu.CompilerParams(vmem_limit_bytes=48 * 1024 * 1024),
        name="prepare",
    )(mine, other)


def constants_kernel(c, rows, w_ref, bias_ref, message_ref, weights_ref, bias_out_ref, right_ref, w_f32):
    w_f32[...] = w_ref[...].astype(jnp.float32)
    for e in range(c):
        weights_ref[:, e * c:(e + 1) * c] = w_f32[pl.ds(e, c, stride=c), :].T.astype(jnp.bfloat16)
    bias_out_ref[...] = bias_ref[...]
    right_ref[...] = message_ref[:rows]


def constants(w_out, b_out, message, rows, c):
    z = w_out.shape[1]
    operands = (w_out, b_out.reshape(1, -1), message)
    outs = [((z, w_out.shape[0]), jnp.bfloat16), ((1, z), jnp.float32), ((rows, LANES), jnp.bfloat16)]
    return pl.pallas_call(
        functools.partial(constants_kernel, c, rows),
        grid=(1,),
        out_shape=[jax.ShapeDtypeStruct(*out) for out in outs],
        in_specs=[whole(a.shape) for a in operands],
        out_specs=[whole(out[0]) for out in outs],
        scratch_shapes=[pltpu.VMEM(w_out.shape, jnp.float32)],
        compiler_params=pltpu.CompilerParams(vmem_limit_bytes=48 * 1024 * 1024),
        name="constants",
    )(*operands)


def pair_kernel(seqs, c, right_at, left_ref, weights_ref, bias_ref, *refs):
    right_refs, (out_ref, right_f32, right_b, outer_ref) = refs[:-4], refs[-4:]
    rows_step = out_ref.shape[0]
    blocks = out_ref.shape[1] // LANES

    def block_of(n, at):
        array, first = right_at[n]
        return right_refs[array][first + at:first + at + c * seqs].astype(jnp.float32)

    @pl.when(pl.program_id(0) == 0)
    def _():
        for b in range(blocks):
            at = b * c * seqs
            right_of = sequence_rows(
                lambda n: block_of(n, at), right_f32, c, seqs)
            for e in range(c):
                lanes = (b * c + e) * LANES
                right_b[:, lanes:lanes + LANES] = right_of(e).astype(jnp.bfloat16)

    for b in range(blocks):
        for e in range(0, c, 2):
            at = (b * c + e) * LANES
            outer = jnp.dot(left_ref[...], right_b[:, at:at + 2 * LANES], preferred_element_type=jnp.float32)
            outer = outer.astype(jnp.bfloat16)
            for half in range(2):
                for i in range(rows_step):
                    outer_ref[i // 2, (e + half) * c:(e + half + 1) * c,
                              (i % 2) * LANES:(i % 2 + 1) * LANES] = (
                        outer[i * c:(i + 1) * c, half * LANES:(half + 1) * LANES])
        for p in range(rows_step // 2):
            update = jnp.dot(weights_ref[...], outer_ref[p], preferred_element_type=jnp.float32)
            for half in range(2):
                mine = update[:, half * LANES:(half + 1) * LANES].T + bias_ref[...]
                out_ref[2 * p + half, b * LANES:(b + 1) * LANES, :] = mine.astype(out_ref.dtype)


def pairs(left, weights, bias, rights, right_at, seqs, c, width):
    sources = len(right_at)
    z = weights.shape[0]
    rows = left.shape[0] // c
    rows_step = 16
    total = sources * seqs
    operands = (left, weights, bias, *rights)
    return pl.pallas_call(
        functools.partial(pair_kernel, seqs, c, right_at),
        grid=(rows // rows_step,),
        out_shape=jax.ShapeDtypeStruct((rows, width, z), jnp.bfloat16),
        in_specs=[pl.BlockSpec((rows_step * c, total), lambda i: (i, 0))] + [whole(a.shape) for a in operands[1:]],
        out_specs=pl.BlockSpec((rows_step, width, z), lambda i: (i, 0, 0)),
        scratch_shapes=[pltpu.VMEM((sources, c * seqs, LANES), jnp.float32),
                        pltpu.VMEM((total, width * c), jnp.bfloat16),
                        pltpu.VMEM((rows_step // 2, c * c, 2 * LANES), jnp.bfloat16)],
        compiler_params=pltpu.CompilerParams(vmem_limit_bytes=32 * 1024 * 1024),
        cost_estimate=pl.CostEstimate(flops=2 * rows * c * width * c * (total + z),
                                      bytes_accessed=2 * rows * width * z, transcendentals=0),
        name="pairs",
    )(*operands)


def source_at(here, step):
    return here ^ (2 * step[0] + step[1])


def direct_steps(chips):
    return [(chips - 1, 0), (0, 1)] + [(a, 0) for a in reversed(range(1, chips - 1))]


def sent_by(n):
    return n, n ^ 1


def by_core(core, of_0, of_1):
    return jax.tree.map(lambda x, y: jnp.where(core == 0, x, y), of_0, of_1)


def far_steps(chips):
    return [(a, 1) for a in range(chips // 2 - 1)]


def fetch(array, step, count):
    return lax.ppermute(array, "row", [(source_at(r, step), r) for r in range(count)])


def fetch_direct(array, n, count):
    steps = direct_steps(count // 2)
    moves = [(2 * source_at(r, steps[m]) + core, 2 * r + core) for r in range(count) for core, m in enumerate(sent_by(n))]
    return lax.ppermute(array, ("row", "col"), moves)


def fetch_far(array, step, count):
    chips = count // 2
    a, b = step
    moves = []
    for r in range(count):
        half = r // chips
        moves.append((2 * source_at(r, (a + 1, b)) + half, 2 * r + half))
        moves.append((2 * source_at(r, (a + chips // 2, b)) + half, 2 * r + 1 - half))
    return lax.ppermute(array, ("row", "col"), moves)


def on_device(alignment, ln_gain, ln_bias, w_left, b_left, w_right, b_right, w_out, b_out):
    seqs, width, _ = alignment.shape
    c = w_left.shape[1]
    row_count = lax.axis_size("row")
    col_count = lax.axis_size("col")
    own, *messages = features(alignment, ln_gain, ln_bias, w_left, b_left, w_right, b_right, row_count, col_count)
    along = row_count // 2
    left_rows = own.shape[0]
    rows = messages[0].shape[0] - 2 * left_rows

    core = lax.axis_index("col")
    direct = [fetch_direct(message, n, row_count) for n, message in reversed([*enumerate(messages[:along])])][::-1]
    beyond = [fetch_far(message, step, row_count) for step, message in zip(far_steps(along), messages[along:])]
    last, across = by_core(core, (direct[0], direct[1]), (direct[1], direct[0]))
    last_far = fetch(last[left_rows:], (0, 1), row_count)
    *rest, last_far = lax.optimization_barrier((*direct[2:], last_far))
    rest = [by_core(core, *(rest[m] for m in sent_by(n))) for n in range(along - 2)]
    far = fetch(jnp.concatenate([block[:rows] for block in rest]), (0, 1), row_count)

    message, _ = lax.optimization_barrier((messages[along - 1], across))
    weights, bias, right = constants(w_out, b_out, message, rows, c)
    near = rest[::-1]
    mine = jnp.concatenate([own] + [block[rows:] for block in near] + [last[:left_rows], across[:left_rows]]
                           + beyond + [last_far[rows:]])
    other = lax.ppermute(mine, "col", [(0, 1), (1, 0)])
    half = along // 2
    left_at = [(a, True) for a in range(along + 1)]
    left_at += [(along + a, True) if a < half else (along + 1 + a - half, False) for a in range(1, along - 1)]
    left_at += [(along + half, True)]
    left = prepare(mine, other, left_at, left_rows, seqs)
    right_at = [(a, 0) for a in range(along - 1)] + [(along - 1, left_rows), (along, left_rows)]
    right_at += [(along + 1, (along - 2 - a) * rows) for a in range(1, along - 1)] + [(along + 2, 0)]
    return pairs(left, weights, bias, [right, *near, last, across, far, last_far], right_at, seqs, c, width)


def solution(mesh):
    in_specs = (P(("group", "row"), "col", None), P(), P(), P(), P(), P(), P(), P(), P())
    out_specs = P(("group", "row"), "col", None)
    return jax.shard_map(
        on_device, mesh=mesh, in_specs=in_specs, out_specs=out_specs, check_vma=False
    )
```

```python
import functools

import jax
import jax.numpy as jnp
from jax import lax
from jax.experimental import pallas as pl
from jax.experimental.pallas import tpu as pltpu
from jax.sharding import PartitionSpec as P

LANES = 128
VMEM_LIMIT = 60 * 1024 * 1024


def whole(shape):
    return pl.BlockSpec(shape, lambda i: (0,) * len(shape))


def features_kernel(scale, x_ref, gain_ref, bias_ref, wl_ref, bl_ref, wr_ref, br_ref,
                    *refs):
    outs, (normed_ref, left_f32, right_f32) = refs[:-3], refs[-3:]
    seqs, width, channels = x_ref.shape
    c = wl_ref.shape[0]
    blocks = width // LANES
    fold = LANES // c
    quarter = width // fold
    right_bias = jnp.broadcast_to(br_ref[...], (LANES, c)).T[:, :1]
    for s in range(seqs):
        values = x_ref[s].astype(jnp.float32)
        average = jnp.mean(values, axis=-1, keepdims=True)
        centred = values - average
        variance = jnp.mean(centred * centred, axis=-1, keepdims=True)
        normed = centred * lax.rsqrt(variance + 1e-05) * gain_ref[...] + bias_ref[...]
        for h in range(channels // LANES):
            normed_ref[h, s * width:(s + 1) * width] = normed[:, h * LANES:(h + 1) * LANES]
        right = lax.dot_general(wr_ref[...], normed.astype(jnp.bfloat16), (((1,), (1,)), ((), ())),
                                preferred_element_type=jnp.float32) + right_bias
        for b in range(blocks):
            right_f32[pl.ds(b * c * seqs + s, c, stride=seqs), :] = right[:, b * LANES:(b + 1) * LANES]
    total = None
    for q in range(fold):
        rows = jnp.concatenate(
            [normed_ref[h, pl.ds(q, seqs * quarter, stride=fold), :] for h in range(channels // LANES)], axis=1
        ).astype(jnp.bfloat16)
        zeros = [jnp.zeros((c, channels), jnp.bfloat16)]
        w = jnp.concatenate(zeros * q + [wl_ref[...]] + zeros * (fold - 1 - q), axis=0)
        term = lax.dot_general(rows, w, (((1,), (1,)), ((), ())), preferred_element_type=jnp.float32)
        total = term if total is None else total + term
    total = (total + jnp.concatenate([bl_ref[...]] * fold, axis=1)) * scale
    for s in range(seqs):
        left_f32[pl.ds(s, quarter, stride=seqs), :] = total[s * quarter:(s + 1) * quarter]
    own_ref, *message_refs = outs
    here = lax.axis_index("row")
    rows = own_ref.shape[0]
    chips = left_f32.shape[0] // rows

    def left_for(step):
        block = source_at(here, step) % chips
        return left_f32[pl.ds(pl.multiple_of(block * rows, rows), rows), :].astype(jnp.bfloat16)

    own_ref[...] = left_for((0, 0))
    right = right_f32[...].astype(jnp.bfloat16)
    core = lax.axis_index("col")
    for n, message_ref in enumerate(message_refs[:chips]):
        a, b = by_core(core, *(direct_steps(chips)[m] for m in sent_by(n)))
        first = message_ref.shape[0] - right.shape[0] - rows
        if first:
            message_ref[:rows] = left_for((a, b))
        message_ref[first:first + right.shape[0]] = right
        message_ref[first + right.shape[0]:] = left_for((a, 1) if first else (a, b))
    same_half = here // chips == lax.axis_index("col")
    for (a, b), message_ref in zip(far_steps(chips), message_refs[chips:]):
        message_ref[...] = jnp.where(same_half, left_for((a + 1, b)), left_for((a, b)))


def features(alignment, ln_gain, ln_bias, w_left, b_left, w_right, b_right, row_count, col_count):
    seqs, width, channels = alignment.shape
    c = w_left.shape[1]
    rows = seqs * width * c // LANES
    chips = row_count // col_count
    part = rows // chips
    shapes = [(part, LANES)]
    shapes += [(rows + part * (2 if n < 2 else 1), LANES) for n in range(chips)]
    shapes += [(part, LANES)] * len(far_steps(chips))
    operands = (alignment, ln_gain.reshape(1, -1), ln_bias.reshape(1, -1), w_left.T, b_left.reshape(1, -1),
                w_right.T, b_right.reshape(1, -1))
    return pl.pallas_call(
        functools.partial(features_kernel, 1.0 / (seqs * row_count)),
        grid=(1,),
        out_shape=[jax.ShapeDtypeStruct(shape, jnp.bfloat16) for shape in shapes],
        in_specs=[whole(a.shape) for a in operands],
        out_specs=[whole(shape) for shape in shapes],
        scratch_shapes=[pltpu.VMEM((channels // LANES, seqs * width, LANES), jnp.float32),
                        pltpu.VMEM((rows, LANES), jnp.float32),
                        pltpu.VMEM((rows, LANES), jnp.float32)],
        compiler_params=pltpu.CompilerParams(vmem_limit_bytes=VMEM_LIMIT),
        name="features",
    )(*operands)


def sequence_rows(block, f32_ref, inner, seqs):
    sources = f32_ref.shape[0]
    for n in range(sources):
        f32_ref[n] = block(n)
    if seqs % 8 == 0:
        return lambda m: jnp.concatenate(
            [f32_ref[n, m * seqs:(m + 1) * seqs] for n in range(sources)], axis=0)
    flat = f32_ref.reshape(sources * inner * seqs, LANES)
    return lambda m: jnp.concatenate(
        [flat[pl.ds(m * seqs + s, sources, stride=inner * seqs), :] for s in range(seqs)], axis=0)


def prepare_kernel(seqs, left_at, mine_ref, other_ref, left_ref, left_f32):
    sources, left_rows, _ = left_f32.shape
    same_half = lax.axis_index("row") // (sources // 2) == lax.axis_index("col")

    def block(n):
        first, of_same_half = left_at[n][0] * left_rows, left_at[n][1]
        mine = mine_ref[first:first + left_rows].astype(jnp.float32)
        other = other_ref[first:first + left_rows].astype(jnp.float32)
        return jnp.where(same_half == of_same_half, mine, other)

    left_of = sequence_rows(block, left_f32, left_rows // seqs, seqs)
    for k in range(left_rows // seqs):
        left_ref[k * LANES:(k + 1) * LANES] = left_of(k).T.astype(jnp.bfloat16)


def prepare(mine, other, left_at, left_rows, seqs):
    sources = len(left_at)
    shape = (left_rows // seqs * LANES, sources * seqs)
    return pl.pallas_call(
        functools.partial(prepare_kernel, seqs, left_at),
        grid=(1,),
        out_shape=jax.ShapeDtypeStruct(shape, jnp.bfloat16),
        in_specs=[whole(mine.shape), whole(other.shape)],
        out_specs=whole(shape),
        scratch_shapes=[pltpu.VMEM((sources, left_rows, LANES), jnp.float32)],
        compiler_params=pltpu.CompilerParams(vmem_limit_bytes=48 * 1024 * 1024),
        name="prepare",
    )(mine, other)


def constants_kernel(c, rows, w_ref, bias_ref, message_ref, weights_ref, bias_out_ref, right_ref, w_f32):
    w_f32[...] = w_ref[...].astype(jnp.float32)
    for e in range(c):
        weights_ref[:, e * c:(e + 1) * c] = w_f32[pl.ds(e, c, stride=c), :].T.astype(jnp.bfloat16)
    bias_out_ref[...] = bias_ref[...]
    right_ref[...] = message_ref[:rows]


def constants(w_out, b_out, message, rows, c):
    z = w_out.shape[1]
    operands = (w_out, b_out.reshape(1, -1), message)
    outs = [((z, w_out.shape[0]), jnp.bfloat16), ((1, z), jnp.float32), ((rows, LANES), jnp.bfloat16)]
    return pl.pallas_call(
        functools.partial(constants_kernel, c, rows),
        grid=(1,),
        out_shape=[jax.ShapeDtypeStruct(*out) for out in outs],
        in_specs=[whole(a.shape) for a in operands],
        out_specs=[whole(out[0]) for out in outs],
        scratch_shapes=[pltpu.VMEM(w_out.shape, jnp.float32)],
        compiler_params=pltpu.CompilerParams(vmem_limit_bytes=48 * 1024 * 1024),
        name="constants",
    )(*operands)


def pair_kernel(seqs, c, right_at, left_ref, weights_ref, bias_ref, *refs):
    right_refs, (out_ref, right_f32, right_b, outer_ref) = refs[:-4], refs[-4:]
    rows_step = out_ref.shape[0]
    blocks = out_ref.shape[1] // LANES

    def block_of(n, at):
        array, first = right_at[n]
        return right_refs[array][first + at:first + at + c * seqs].astype(jnp.float32)

    @pl.when(pl.program_id(0) == 0)
    def _():
        for b in range(blocks):
            at = b * c * seqs
            right_of = sequence_rows(
                lambda n: block_of(n, at), right_f32, c, seqs)
            for e in range(c):
                lanes = (b * c + e) * LANES
                right_b[:, lanes:lanes + LANES] = right_of(e).astype(jnp.bfloat16)

    for b in range(blocks):
        for e in range(0, c, 2):
            at = (b * c + e) * LANES
            outer = jnp.dot(left_ref[...], right_b[:, at:at + 2 * LANES], preferred_element_type=jnp.float32)
            outer = outer.astype(jnp.bfloat16)
            for half in range(2):
                for i in range(rows_step):
                    outer_ref[i // 2, (e + half) * c:(e + half + 1) * c,
                              (i % 2) * LANES:(i % 2 + 1) * LANES] = (
                        outer[i * c:(i + 1) * c, half * LANES:(half + 1) * LANES])
        for p in range(rows_step // 2):
            update = jnp.dot(weights_ref[...], outer_ref[p], preferred_element_type=jnp.float32)
            for half in range(2):
                mine = update[:, half * LANES:(half + 1) * LANES].T + bias_ref[...]
                out_ref[2 * p + half, b * LANES:(b + 1) * LANES, :] = mine.astype(out_ref.dtype)


def pairs(left, weights, bias, rights, right_at, seqs, c, width):
    sources = len(right_at)
    z = weights.shape[0]
    rows = left.shape[0] // c
    rows_step = 32
    total = sources * seqs
    operands = (left, weights, bias, *rights)
    return pl.pallas_call(
        functools.partial(pair_kernel, seqs, c, right_at),
        grid=(rows // rows_step,),
        out_shape=jax.ShapeDtypeStruct((rows, width, z), jnp.bfloat16),
        in_specs=[pl.BlockSpec((rows_step * c, total), lambda i: (i, 0))] + [whole(a.shape) for a in operands[1:]],
        out_specs=pl.BlockSpec((rows_step, width, z), lambda i: (i, 0, 0)),
        scratch_shapes=[pltpu.VMEM((sources, c * seqs, LANES), jnp.float32),
                        pltpu.VMEM((total, width * c), jnp.bfloat16),
                        pltpu.VMEM((rows_step // 2, c * c, 2 * LANES), jnp.bfloat16)],
        compiler_params=pltpu.CompilerParams(vmem_limit_bytes=32 * 1024 * 1024),
        cost_estimate=pl.CostEstimate(flops=2 * rows * c * width * c * (total + z),
                                      bytes_accessed=2 * rows * width * z, transcendentals=0),
        name="pairs",
    )(*operands)


def source_at(here, step):
    return here ^ (2 * step[0] + step[1])


def direct_steps(chips):
    return [(chips - 1, 0), (0, 1)] + [(a, 0) for a in reversed(range(1, chips - 1))]


def sent_by(n):
    return n, n ^ 1


def by_core(core, of_0, of_1):
    return jax.tree.map(lambda x, y: jnp.where(core == 0, x, y), of_0, of_1)


def far_steps(chips):
    return [(a, 1) for a in range(chips // 2 - 1)]


def fetch(array, step, count):
    return lax.ppermute(array, "row", [(source_at(r, step), r) for r in range(count)])


def fetch_direct(array, n, count):
    steps = direct_steps(count // 2)
    moves = [(2 * source_at(r, steps[m]) + core, 2 * r + core) for r in range(count) for core, m in enumerate(sent_by(n))]
    return lax.ppermute(array, ("row", "col"), moves)


def fetch_far(array, step, count):
    chips = count // 2
    a, b = step
    moves = []
    for r in range(count):
        half = r // chips
        moves.append((2 * source_at(r, (a + 1, b)) + half, 2 * r + half))
        moves.append((2 * source_at(r, (a + chips // 2, b)) + half, 2 * r + 1 - half))
    return lax.ppermute(array, ("row", "col"), moves)


def on_device(alignment, ln_gain, ln_bias, w_left, b_left, w_right, b_right, w_out, b_out):
    seqs, width, _ = alignment.shape
    c = w_left.shape[1]
    row_count = lax.axis_size("row")
    col_count = lax.axis_size("col")
    own, *messages = features(alignment, ln_gain, ln_bias, w_left, b_left, w_right, b_right, row_count, col_count)
    along = row_count // 2
    left_rows = own.shape[0]
    rows = messages[0].shape[0] - 2 * left_rows

    core = lax.axis_index("col")
    direct = [fetch_direct(message, n, row_count) for n, message in reversed([*enumerate(messages[:along])])][::-1]
    beyond = [fetch_far(message, step, row_count) for step, message in zip(far_steps(along), messages[along:])]
    last, across = by_core(core, (direct[0], direct[1]), (direct[1], direct[0]))
    last_far = fetch(last[left_rows:], (0, 1), row_count)
    *rest, last_far = lax.optimization_barrier((*direct[2:], last_far))
    rest = [by_core(core, *(rest[m] for m in sent_by(n))) for n in range(along - 2)]
    far = fetch(jnp.concatenate([block[:rows] for block in rest]), (0, 1), row_count)

    message, _ = lax.optimization_barrier((messages[along - 1], across))
    weights, bias, right = constants(w_out, b_out, message, rows, c)
    near = rest[::-1]
    mine = jnp.concatenate([own] + [block[rows:] for block in near] + [last[:left_rows], across[:left_rows]]
                           + beyond + [last_far[rows:]])
    other = lax.ppermute(mine, "col", [(0, 1), (1, 0)])
    half = along // 2
    left_at = [(a, True) for a in range(along + 1)]
    left_at += [(along + a, True) if a < half else (along + 1 + a - half, False) for a in range(1, along - 1)]
    left_at += [(along + half, True)]
    left = prepare(mine, other, left_at, left_rows, seqs)
    right_at = [(a, 0) for a in range(along - 1)] + [(along - 1, left_rows), (along, left_rows)]
    right_at += [(along + 1, (along - 2 - a) * rows) for a in range(1, along - 1)] + [(along + 2, 0)]
    return pairs(left, weights, bias, [right, *near, last, across, far, last_far], right_at, seqs, c, width)


def solution(mesh):
    in_specs = (P(("group", "row"), "col", None), P(), P(), P(), P(), P(), P(), P(), P())
    out_specs = P(("group", "row"), "col", None)
    return jax.shard_map(
        on_device, mesh=mesh, in_specs=in_specs, out_specs=out_specs, check_vma=False
    )
```
